128 devices in a mesh: replica: 8 (over x, core), shard: 16 (over z, y).
Axes of the slice: x: 4, y: 4, z: 4, core: 2. Of those that a mesh axis runs over, the one named last changes fastest.
Arguments:
- tokens: bfloat16 [16384, 768], P(('replica', 'shard')), may hold values from -6 to 6
- cotangent: bfloat16 [16384, 768], P(('replica', 'shard')), may hold values from -6 to 6
- lengths: int32 [8, 3], P('replica'), may hold values from 1 to 1536, 2048 in all within a row
- positions: int32 [8, 2048], P('replica'), may hold values from 0 to 2047, each once within a row
- w_rows: float32 [768, 6144], P('shard'), may hold values from -0.8660254 to 0.8660254
- w_down: float32 [3072, 768], P('shard'), may hold values from -0.109375 to 0.109375
- vectors: float32 [12, 768], P(None, 'shard'), may hold values from -1.8 to 1.8
- moment_rows: float32 [768, 6144], P('shard'), may hold values from -40 to 40
- second_rows: float32 [768, 6144], P('shard'), may hold values from 212.992 to 868.352
- moment_down: float32 [3072, 768], P('shard'), may hold values from -40 to 40
- second_down: float32 [3072, 768], P('shard'), may hold values from 212.992 to 868.352
- moment_vectors: float32 [12, 768], P(None, 'shard'), may hold values from -40 to 40
- second_vectors: float32 [12, 768], P(None, 'shard'), may hold values from 212.992 to 868.352
Outputs:
- outputs: bfloat16 [16384, 768], P(('replica', 'shard'))
- grad_input: bfloat16 [16384, 768], P(('replica', 'shard'))
- new_rows: float32 [768, 6144], P('shard')
- new_moment_rows: float32 [768, 6144], P('shard')
- new_second_rows: float32 [768, 6144], P('shard')
- new_down: float32 [3072, 768], P('shard')
- new_moment_down: float32 [3072, 768], P('shard')
- new_second_down: float32 [3072, 768], P('shard')
- new_vectors: float32 [12, 768], P(None, 'shard')
- new_moment_vectors: float32 [12, 768], P(None, 'shard')
- new_second_vectors: float32 [12, 768], P(None, 'shard')
The draws below stay inside these ranges and needn't reach their ends.
Inputs may be any that keep to these rules, and one draw needn't show every extreme that they name: Each row of lengths sums to 2048; its largest entry is three quarters of 2048. Each row of positions is a permutation of 0 to 2047.
All inputs are finite; a program needn't handle non-finite values.
Results may differ from the reference program's by a relative error of at most 0.012.
The reference program's roundings to bfloat16 on the way count: a program that leaves them out, or rounds other values in their place, can miss the bound.
Values may be sent and summed in bfloat16 or wider, within the bound.
A program may use at most 192 MiB of HBM per device.

```python
import math
import jax
import jax.numpy as jnp
import numpy as np
from jax import lax

D = 768
H = 12
HD = 64
FF = 3072
SEQS = 3
STEP = 10
GROUP = 2048
TOKENS = 16384
VEC = 12
N_REPLICA = 8


def draw_w_rows(key, part):
    key = jax.random.fold_in(key, 11)
    column = jnp.arange(4 * D + FF)
    scale = jnp.where(column < 2 * D, 1.5, jnp.where(column < 3 * D, 1.0, jnp.where(column < 4 * D, 4.0, 1.0)))
    scale = scale.astype(jnp.float32) / jnp.sqrt(jnp.float32(D))
    base = jnp.clip(jax.random.normal(key, (D, 4 * D + FF), jnp.float32), -6.0, 6.0)
    return base * scale[None, :]


def draw_vectors(key, part):
    key = jax.random.fold_in(key, 23)
    key_gain, key_bias = jax.random.split(key)
    row = jnp.arange(VEC)[:, None]
    gains = jnp.exp(jax.random.uniform(key_gain, (VEC, D), jnp.float32, -0.5, 0.5))
    biases = 0.3 * jnp.clip(jax.random.normal(key_bias, (VEC, D), jnp.float32), -6.0, 6.0)
    return jnp.where((row == 0) | (row == 5), gains, biases)


def shard_levels(rng, dims, pieces, low, top_value):
    level = 1.0
    for dim, shards_of in pieces:
        steps = jax.random.uniform(jax.random.fold_in(jax.random.fold_in(rng, 6), dim), (shards_of,), jnp.float32, low / len(pieces), top_value / len(pieces))
        level = level * jnp.repeat(jnp.exp(steps), dims[dim] // shards_of).reshape((-1,) + (1,) * (len(dims) - 1 - dim))
    return level


def split_up(amount, total, reach, slope):
    loads = [(1 << 20) // math.isqrt(rank ** slope) + 1 for rank in range(2, amount + 1)]
    spare, holding = total - reach - (amount - 1), [1] * (amount - 1)
    while spare > 0:
        movable = [i for i in range(amount - 1) if holding[i] < reach]
        mass, remaining = sum([loads[i] for i in movable]), spare
        for i in movable:
            extra = min(reach - holding[i], max(1, remaining * loads[i] // mass), spare)
            holding[i] = holding[i] + extra
            spare = spare - extra
    return np.array([reach] + holding)


def ragged(key, count, total, reach, skew):
    if count == 2:
        one = jax.random.randint(key, (), max(1, total - reach), min(reach, total - 1) + 1)
        return jnp.stack([one, total - one])
    tallies = jnp.asarray(split_up(count, total, reach, skew), jnp.int32)
    pairs = (count - 1) // 2
    giver, sink = tallies[1:1 + 2 * pairs:2], tallies[2:2 + 2 * pairs:2]
    room = jnp.minimum(giver - 1, reach - sink)
    passed = jax.random.randint(jax.random.fold_in(key, 1), (pairs,), 0, 1 << 20) % (room + 1)
    tallies = tallies.at[1:1 + 2 * pairs:2].set(giver - passed).at[2:2 + 2 * pairs:2].set(sink + passed)
    return tallies[jax.random.permutation(jax.random.fold_in(key, 2), count)]


def gaussian(key, dims, scale, bound, cuts=(), held_as=jnp.bfloat16):
    result = jax.random.normal(key, dims, jnp.float32) * scale
    if len(cuts) > 0:
        result = shard_levels(key, dims, cuts, -0.22, 0.18) * result
    return jnp.clip(result, min=-bound, max=bound).astype(held_as)


def setup_inputs(seed: int = 0) -> dict:
    key_list = jax.random.split(jax.random.key(seed), 14)
    return {
        "tokens": gaussian(key_list[0], (TOKENS, D), 1.0, 6.0, ((0, 128),)),
        "cotangent": gaussian(key_list[1], (TOKENS, D), 1.0, 6.0, ((0, 128),)),
        "lengths": jax.vmap(lambda own: ragged(own, SEQS, GROUP, 3 * GROUP // 4, 2))(jax.random.split(key_list[2], N_REPLICA)).reshape((N_REPLICA, SEQS)).astype(jnp.int32),
        "positions": jax.vmap(lambda own: jax.random.permutation(own, GROUP))(jax.random.split(key_list[3], N_REPLICA)).reshape((N_REPLICA, GROUP)).astype(jnp.int32),
        "w_rows": draw_w_rows(jax.random.fold_in(key_list[13], 71), 0),
        "w_down": gaussian(key_list[5], (FF, D), FF ** -0.5, 0.109375, ((0, 16),), jnp.float32),
        "vectors": draw_vectors(jax.random.fold_in(key_list[13], 71), 0),
        "moment_rows": gaussian(key_list[7], (D, 4 * D + FF), (0.056 * TOKENS ** 0.5), 40.0, ((0, 16),), jnp.float32),
        "second_rows": jnp.clip(jnp.exp(math.log(868.352) - 1.40534252 * jax.random.uniform(key_list[8], (D, 4 * D + FF), jnp.float32) ** shard_levels(key_list[8], (D, 4 * D + FF), ((0, 16),), -0.2, 0.2)), 212.992, 868.352),
        "moment_down": gaussian(key_list[9], (FF, D), (0.056 * TOKENS ** 0.5), 40.0, ((0, 16),), jnp.float32),
        "second_down": jnp.clip(jnp.exp(math.log(868.352) - 1.40534252 * jax.random.uniform(key_list[10], (FF, D), jnp.float32) ** shard_levels(key_list[10], (FF, D), ((0, 16),), -0.2, 0.2)), 212.992, 868.352),
        "moment_vectors": gaussian(key_list[11], (VEC, D), (0.056 * TOKENS ** 0.5), 40.0, ((1, 16),), jnp.float32),
        "second_vectors": jnp.clip(jnp.exp(math.log(868.352) - 1.40534252 * jax.random.uniform(key_list[12], (VEC, D), jnp.float32) ** shard_levels(key_list[12], (VEC, D), ((1, 16),), -0.2, 0.2)), 212.992, 868.352),
    }


@jax.custom_vjp
def low(v):
    return lax.optimization_barrier(v.astype(jnp.bfloat16)).astype(jnp.float32)

@jax.custom_vjp
def low_back(v):
    return v

def low_keep(v):
    return (low(v), None)

def low_pass(kept, grad):
    return (grad,)

def back_keep(v):
    return (v, None)

def back_low(kept, grad):
    return (low(grad),)
low.defvjp(low_keep, low_pass)
low_back.defvjp(back_keep, back_low)
EPS_NORM = 1e-05
BETA_ONE = 0.9
BETA_TWO = 0.95
EPS_ADAM = 1e-08
LR_MATRIX = 0.02
LR_VECTOR = 0.3
DECAY = 0.1
HUGE_NEG = -1e+30

def layer_norm(inputs, gain, shift):
    average = lax.optimization_barrier(jnp.mean(inputs, -1, keepdims=True))
    centred = inputs - average
    spread = lax.optimization_barrier(jnp.mean(centred * centred, -1, keepdims=True))
    return centred * lax.rsqrt(spread + EPS_NORM) * gain + shift

def matmul(left, right):
    return jnp.dot(left, right, precision=lax.Precision.HIGHEST, preferred_element_type=jnp.float32)

def segment_of(place_row, length_row):
    seq_ends = jnp.cumsum(length_row)
    return lax.optimization_barrier(jnp.sum((place_row[:, None] >= seq_ends[None, :]).astype(jnp.int32), axis=1))

def block(inputs, place_row, length_row, rows_low, down_low, vec_low):
    model_dim = inputs.shape[1]
    group_rows = inputs.shape[0]
    gain_one, shift_one, bias_query, bias_value = (vec_low[0], vec_low[1], vec_low[2], vec_low[3])
    bias_out, gain_two, shift_two, bias_down = (vec_low[4], vec_low[5], vec_low[6], vec_low[7])
    bias_first = vec_low[8:].reshape(-1)
    normed = low(layer_norm(inputs, gain_one, shift_one))
    projected = matmul(normed, rows_low[:, :3 * model_dim])
    queries = low_back(low(projected[:, :model_dim] + bias_query))
    key_rows = low_back(low(projected[:, model_dim:2 * model_dim]))
    value_rows = low_back(low(projected[:, 2 * model_dim:3 * model_dim] + bias_value))
    query_heads = queries.reshape(group_rows, H, HD)
    key_heads = key_rows.reshape(group_rows, H, HD)
    value_heads = value_rows.reshape(group_rows, H, HD)
    scores = jnp.einsum('qhd,khd->hqk', query_heads, key_heads, precision=lax.Precision.HIGHEST)
    scores = low_back(scores * HD ** (-0.5))
    segments = segment_of(place_row, length_row)
    allowed = (segments[:, None] == segments[None, :]) & (place_row[None, :] <= place_row[:, None])
    scores = jnp.where(allowed[None], scores, HUGE_NEG)
    top = lax.optimization_barrier(jnp.max(scores, -1, keepdims=True))
    raised = jnp.exp(scores - top)
    probs = raised / lax.optimization_barrier(jnp.sum(raised, -1, keepdims=True))
    attended = jnp.einsum('hqk,khd->qhd', low(probs), value_heads, precision=lax.Precision.HIGHEST)
    attended = low_back(low(attended.reshape(group_rows, model_dim)))
    middle = inputs + low_back(matmul(attended, rows_low[:, 3 * model_dim:4 * model_dim]) + bias_out)
    normed_two = low(layer_norm(middle, gain_two, shift_two))
    pre_act = low_back(matmul(normed_two, rows_low[:, 4 * model_dim:]) + bias_first)
    hidden = low(jax.nn.gelu(pre_act, approximate=True))
    return middle + low_back(matmul(hidden, down_low) + bias_down)

def adamw(weight, moment, second, grad, rate, decay):
    moment_new = BETA_ONE * moment + (1.0 - BETA_ONE) * grad
    second_new = BETA_TWO * second + (1.0 - BETA_TWO) * grad * grad
    moment_hat = moment_new / (1.0 - BETA_ONE ** STEP)
    second_hat = second_new / (1.0 - BETA_TWO ** STEP)
    weight_new = weight - rate * (moment_hat / (jnp.sqrt(second_hat) + EPS_ADAM) + decay * weight)
    return (weight_new, moment_new, second_new)

def reference(tokens, cotangent, lengths, positions, w_rows, w_down, vectors, moment_rows, second_rows, moment_down, second_down, moment_vectors, second_vectors):

    def forward(inputs, rows_full, down_full, vec_full):
        rows_low = low(rows_full)
        down_low = low(down_full)
        vec_low = low(vec_full)

        def one_group(packed):
            group_in, place_row, length_row = packed
            return block(group_in, place_row, length_row, rows_low, down_low, vec_low)
        results = lax.map(jax.checkpoint(one_group), (inputs.reshape(N_REPLICA, GROUP, D), positions, lengths))
        return results.reshape(TOKENS, D)
    outputs, backward = jax.vjp(forward, tokens.astype(jnp.float32), w_rows, w_down, vectors)
    grad_in, grad_rows, grad_down, grad_vec = backward(cotangent.astype(jnp.float32))
    rows_new = adamw(w_rows, moment_rows, second_rows, grad_rows, LR_MATRIX, DECAY)
    down_new = adamw(w_down, moment_down, second_down, grad_down, LR_MATRIX, DECAY)
    vec_new = adamw(vectors, moment_vectors, second_vectors, grad_vec, LR_VECTOR, 0.0)
    return (outputs.astype(jnp.bfloat16), grad_in.astype(jnp.bfloat16), rows_new[0], rows_new[1], rows_new[2], down_new[0], down_new[1], down_new[2], vec_new[0], vec_new[1], vec_new[2])
```

```python
import functools

import jax
import jax.numpy as jnp
from jax import lax
from jax.experimental import pallas as pl
from jax.experimental.pallas import tpu as pltpu
from jax.sharding import PartitionSpec as P

H = 12
HD = 64
STEP = 10
D = 768
FF = 3072
OWN = 128
GROUP = 2048
NEIGHBOURS = 4
TILE = 256
CHUNK = 256
MIB = 1 << 20

EPS_NORM = 1e-05
BETA_ONE = 0.9
BETA_TWO = 0.95
EPS_ADAM = 1e-08
LR_MATRIX = 0.02
LR_VECTOR = 0.3
DECAY = 0.1
HUGE_NEG = -1e30

BF = jnp.bfloat16
F32 = jnp.float32
MESH = pl.DeviceIdType.MESH
VMEM = pl.BlockSpec(memory_space=pltpu.VMEM)
ANY = pl.BlockSpec(memory_space=pl.ANY)


def step4(i, d):
    return lax.rem(i + d, 4)


class Place:
    def __init__(self):
        self.r = lax.axis_index("replica")
        self.s = lax.axis_index("shard")
        self.x = lax.div(self.r, 2)
        self.c = lax.rem(self.r, 2)
        self.z = lax.div(self.s, 4)
        self.y = lax.rem(self.s, 4)

    def ydev(self, d):
        return (self.r, self.z * 4 + step4(self.y, d))

    def zdev(self, d):
        return (self.r, step4(self.z, d) * 4 + self.y)

    def xdev(self, d):
        return (step4(self.x, d) * 2 + self.c, self.s)

    def sibling(self):
        return (self.x * 2 + 1 - self.c, self.s)


def greet(devices):
    barrier = pltpu.get_barrier_semaphore()
    for device in devices:
        pl.semaphore_signal(barrier, inc=1, device_id=device, device_id_type=MESH)
    pl.semaphore_wait(barrier, len(devices))


class Wire:
    def __init__(self, send_sems, recv_sems, local_sems):
        self.send_sems, self.recv_sems, self.local_sems = send_sems, recv_sems, local_sems
        self.sent, self.moved = 0, 0

    def push(self, src, dst, device):
        k = self.sent
        self.sent += 1
        copy = pltpu.make_async_remote_copy(
            src_ref=src,
            dst_ref=dst,
            send_sem=self.send_sems.at[k],
            recv_sem=self.recv_sems.at[k],
            device_id=device,
            device_id_type=MESH,
        )
        copy.start()
        return copy

    def local(self, src, dst):
        k = self.moved
        self.moved += 1
        copy = pltpu.make_async_copy(src, dst, self.local_sems.at[k])
        copy.start()
        return copy


def sems(remote, local):
    return [
        pltpu.SemaphoreType.DMA((remote,)),
        pltpu.SemaphoreType.DMA((remote,)),
        pltpu.SemaphoreType.DMA((max(local, 1),)),
    ]


def cut(axis, base, size):
    if axis == 0:
        return (pl.ds(pl.multiple_of(base, 16), size), slice(None))
    return (slice(None), pl.ds(pl.multiple_of(base, 128), size))


class Gather:
    def __init__(self, wire, place, shard, full, axis, base, size, y_first):
        self.wire, self.place, self.shard, self.full = wire, place, shard, full
        self.region = cut(axis, base, size)
        self.y_first = y_first

    def slab(self, d):
        p = self.place
        if self.y_first:
            return self.full.at[(step4(p.z, 4 - d), slice(None)) + self.region]
        return self.full.at[(slice(None), step4(p.y, 4 - d)) + self.region]

    def first(self):
        p, w = self.place, self.wire
        src = self.shard.at[self.region]
        dst = self.full.at[(p.z, p.y) + self.region]
        self.own = w.local(src, dst)
        self.one = [w.push(src, dst, p.ydev(d) if self.y_first else p.zdev(d)) for d in (1, 3, 2)]

    def second(self):
        p, w = self.place, self.wire
        self.own.wait()
        for copy in self.one:
            copy.wait_recv()
        slab = self.slab(0)
        self.two = [(d, w.push(slab, slab, p.zdev(d) if self.y_first else p.ydev(d))) for d in (1, 3, 2)]
        self.across = [w.push(slab, slab, p.sibling())]

    def third(self):
        p, w = self.place, self.wire
        for d, copy in self.two:
            copy.wait_recv()
            slab = self.slab(d)
            self.across.append(w.push(slab, slab, p.sibling()))

    def end(self):
        for copy in self.across:
            copy.wait_recv()
        for copy in self.one + [copy for _, copy in self.two] + self.across:
            copy.wait_send()


GATHER_SENDS = 10


def scatter_shapes(rows, cols, shared, dtype):
    shapes = [
        pltpu.VMEM((4, 4, rows, cols), dtype),
        pltpu.VMEM((4, 4, rows, cols), dtype),
        pltpu.VMEM((3, 4, rows, cols), dtype),
        pltpu.VMEM((4, rows, cols), dtype),
        pltpu.VMEM((3, rows, cols), dtype),
        pltpu.VMEM((4, rows, cols), dtype),
    ]
    return shapes


class Scatter:
    def __init__(self, wire, place, grad, out, axis, half, offset, size, z_first, shared, scratch):
        self.wire, self.place, self.grad, self.out = wire, place, grad, out
        self.shared, self.z_first = shared, z_first
        if shared:
            self.mine = cut(axis, place.c * half + offset, size)
            self.other = cut(axis, (1 - place.c) * half + offset, size)
        else:
            self.mine = self.other = (slice(None), slice(None))
        self.held, self.in0, self.in1, self.part, self.in2, self.in3 = scratch
        self.sends = []

    def push(self, src, dst, device):
        copy = self.wire.push(src, dst, device)
        self.sends.append(copy)
        return copy

    def p0(self):
        every = (slice(None), slice(None))
        self.load = self.wire.local(self.grad.at[every + self.mine], self.held)
        self.wait = [self.push(self.grad.at[every + self.other], self.in0, self.place.sibling())]

    def p1(self):
        p = self.place
        self.load.wait()
        self.wait[0].wait_recv()

        def add(i, carry):
            a, b = lax.div(i, 4), lax.rem(i, 4)
            both = self.held[a, b].astype(F32) + self.in0[a, b].astype(F32)
            self.held[a, b] = both.astype(self.held.dtype)
            return carry

        lax.fori_loop(0, 16, add, 0)
        self.wait = []
        for d in (1, 3, 2):
            if self.z_first:
                src, device = self.held.at[step4(p.z, d)], p.zdev(d)
            else:
                src, device = self.held.at[:, step4(p.y, d)], p.ydev(d)
            self.wait.append(self.push(src, self.in1.at[d - 1], device))

    def p2(self):
        p = self.place
        for copy in self.wait:
            copy.wait_recv()

        def add(i, carry):
            own = self.held[p.z, i] if self.z_first else self.held[i, p.y]
            total = own.astype(F32)
            for k in range(3):
                total = total + self.in1[k, i].astype(F32)
            self.part[i] = total.astype(self.part.dtype)
            return carry

        lax.fori_loop(0, 4, add, 0)
        self.wait = []
        for d in (1, 3, 2):
            if self.z_first:
                src, device = self.part.at[step4(p.y, d)], p.ydev(d)
            else:
                src, device = self.part.at[step4(p.z, d)], p.zdev(d)
            self.wait.append(self.push(src, self.in2.at[d - 1], device))

    def p3(self):
        p = self.place
        for copy in self.wait:
            copy.wait_recv()
        total = self.part[p.y if self.z_first else p.z].astype(F32)
        for k in range(3):
            total = total + self.in2[k].astype(F32)
        self.in3[p.x] = total.astype(self.in3.dtype)
        self.wait = [self.push(self.in3.at[p.x], self.in3.at[p.x], p.xdev(d)) for d in (1, 3, 2)]

    def p4(self):
        for copy in self.wait:
            copy.wait_recv()
        total = self.in3[0].astype(F32)
        for k in range(1, 4):
            total = total + self.in3[k].astype(F32)
        self.out[self.mine] = total
        self.wait = []
        if self.shared:
            here = self.out.at[self.mine]
            self.wait = [self.push(here, here, self.place.sibling())]

    def end(self):
        for copy in self.wait:
            copy.wait_recv()
        for copy in self.sends:
            copy.wait_send()


SCATTER_SENDS = 11


def all_peers(p):
    rings = [p.ydev(d) for d in (1, 2, 3)] + [p.zdev(d) for d in (1, 2, 3)]
    return rings + [p.sibling()]


def x_peers(p):
    return [p.xdev(d) for d in (1, 2, 3)]


def gather_first_kernel(shard, full, send_sems, recv_sems, local_sems):
    p = Place()
    w = Wire(send_sems, recv_sems, local_sems)
    greet(all_peers(p))
    half = shard.shape[1] // 2
    size = half // 2
    parts = [
        Gather(w, p, shard, full, 1, p.c * half, size, True),
        Gather(w, p, shard, full, 1, p.c * half + size, size, False),
    ]
    for part in parts:
        part.first()
    for part in parts:
        part.second()
    for part in parts:
        part.third()
    for part in parts:
        part.end()


def gather_first(shard):
    rows, cols = shard.shape
    full = pl.pallas_call(
        gather_first_kernel,
        out_shape=jax.ShapeDtypeStruct((4, 4, rows, cols), BF),
        in_specs=[VMEM],
        out_specs=VMEM,
        scratch_shapes=sems(2 * GATHER_SENDS, 2),
        compiler_params=pltpu.CompilerParams(
            collective_id=0, has_side_effects=True, vmem_limit_bytes=20 * MIB
        ),
        name="gather_first",
    )(shard)
    return full.reshape(16 * rows, cols)


def half_lanes(value, right):
    lane = lax.broadcasted_iota(jnp.int32, value.shape, 1)
    keep = lane >= HD if right else lane < HD
    return jnp.where(keep, value, jnp.zeros_like(value))


def rows_max(value):
    return jnp.max(value.reshape(-1, 8, value.shape[1]), axis=0)


def rows_sum(value):
    return jnp.sum(value.reshape(-1, 8, value.shape[1]), axis=0)


def dot_lanes(left, right):
    return lax.dot_general(left, right, (((1,), (1,)), ((), ())), preferred_element_type=F32)


def dot_plain(left, right):
    return jnp.dot(left, right, preferred_element_type=F32)


def fill_bias(key_place, query_place, bias):
    def body(i, carry):
        rows = pl.ds(pl.multiple_of(i * CHUNK, CHUNK), CHUNK)
        keys = key_place[rows, :]
        ok = (keys <= query_place[0:1, :]) & (keys >= query_place[1:2, :])
        bias[rows, :] = jnp.where(ok, 0.0, HUGE_NEG).astype(F32)
        return carry

    lax.fori_loop(0, GROUP // CHUNK, body, 0)


def key_chunk(packed, i, head):
    a, b = lax.div(i, 2), lax.rem(i, 2) * 2
    return packed[a, pl.ds(b, 2), :, head * 128 : head * 128 + 128].reshape(CHUNK, 128)


def chunk_rows(i):
    return pl.ds(pl.multiple_of(i * CHUNK, CHUNK), CHUNK)


def turn_keys(packed, head, turned):
    def body(i, carry):
        turned[:, chunk_rows(i)] = key_chunk(packed, i, head).T
        return carry

    lax.fori_loop(0, GROUP // CHUNK, body, 0)


def forward_kernel(
    packed, rest, down, key_place, query_place,
    full_rest, full_down, kv, attended, lse,
    bias, scores, turned, head_out, out_send, send_sems, recv_sems, local_sems,
):
    p = Place()
    w = Wire(send_sems, recv_sems, local_sems)
    greet(all_peers(p))
    kv[p.z, p.y] = packed[p.y]
    to_y = [
        w.push(packed.at[step4(p.y, d)], kv.at[p.z, p.y], p.ydev(d)) for d in (1, 3, 2)
    ]
    rest_half, down_half = rest.shape[1] // 2, down.shape[0] // 2
    rest_one = 1024
    parts = [
        Gather(w, p, rest, full_rest, 1, p.c * rest_half, rest_one, True),
        Gather(w, p, rest, full_rest, 1, p.c * rest_half + rest_one, rest_half - rest_one, False),
        Gather(w, p, down, full_down, 0, p.c * down_half, down_half // 2, True),
        Gather(w, p, down, full_down, 0, p.c * down_half + down_half // 2, down_half // 2, False),
    ]
    for part in parts:
        part.first()
    for copy in to_y:
        copy.wait_recv()
    mine = kv.at[p.z, :, :, pl.ds(0, 384)]
    to_z = [w.push(mine, mine, p.zdev(d)) for d in (1, 3, 2)]
    for part in parts:
        part.second()
    fill_bias(key_place, query_place, bias)
    for copy in to_z:
        copy.wait_recv()
    head_out[128:192, :] = jnp.zeros((64, 512), F32)
    lse[...] = jnp.zeros_like(lse)
    for head in range(3):
        turn_keys(kv, head, turned)
        for tile in range(2):
            cols = slice(tile * TILE, tile * TILE + TILE)
            query = kv[p.z, 2 * tile : 2 * tile + 2, :, 384 + head // 2 * 128 : 512 + head // 2 * 128]
            query = half_lanes(query.reshape(TILE, 128), head == 1)

            def score(i, top):
                part = dot_lanes(key_chunk(kv, i, head), query) + bias[chunk_rows(i), cols]
                scores[chunk_rows(i), :] = part
                return jnp.maximum(top, rows_max(part))

            top = lax.fori_loop(0, GROUP // CHUNK, score, jnp.full((8, TILE), -jnp.inf, F32))
            top = jnp.max(top, axis=0, keepdims=True)

            def mix(i, carry):
                total, acc = carry
                raised = jnp.exp(scores[chunk_rows(i), :] - top)
                acc = acc + dot_plain(turned[:, chunk_rows(i)], raised.astype(BF))
                return total + rows_sum(raised), acc

            total, acc = lax.fori_loop(
                0, GROUP // CHUNK, mix, (jnp.zeros((8, TILE), F32), jnp.zeros((128, TILE), F32))
            )
            total = jnp.sum(total, axis=0, keepdims=True)
            acc = acc / total
            if head == 0:
                head_out[64:128, cols] = acc[64:128, :]
            elif head == 1:
                head_out[0:64, cols] = acc[0:64, :]
            else:
                head_out[192:256, cols] = acc[64:128, :]
            lse[head : head + 1, cols] = top + jnp.log(total)
        if head == 1:
            for part in parts:
                part.third()
    for k in range(4):
        turned_out = head_out[:, k * OWN : k * OWN + OWN].T
        out_send[k] = turned_out.astype(BF)
    attended[p.y] = out_send[p.y]
    back = [
        w.push(out_send.at[step4(p.y, d)], attended.at[p.y], p.ydev(d)) for d in (1, 3, 2)
    ]
    for copy in back:
        copy.wait_recv()
    for part in parts:
        part.end()
    for copy in to_y + to_z + back:
        copy.wait_send()


def forward_attention(packed, rest, down, key_place, query_place):
    rows, cols = rest.shape
    drows, dcols = down.shape
    out = pl.pallas_call(
        forward_kernel,
        out_shape=(
            jax.ShapeDtypeStruct((4, 4, rows, cols), BF),
            jax.ShapeDtypeStruct((4, 4, drows, dcols), BF),
            jax.ShapeDtypeStruct((4, 4, OWN, 640), BF),
            jax.ShapeDtypeStruct((4, OWN, 256), BF),
            jax.ShapeDtypeStruct((8, 512), F32),
        ),
        in_specs=[VMEM] * 5,
        out_specs=(VMEM, VMEM, VMEM, VMEM, VMEM),
        scratch_shapes=[
            pltpu.VMEM((GROUP, 512), F32),
            pltpu.VMEM((GROUP, TILE), F32),
            pltpu.VMEM((128, GROUP), BF),
            pltpu.VMEM((256, 512), F32),
            pltpu.VMEM((4, OWN, 256), BF),
        ]
        + sems(4 * GATHER_SENDS + 9, 4),
        compiler_params=pltpu.CompilerParams(
            collective_id=1, has_side_effects=True, vmem_limit_bytes=40 * MIB
        ),
        name="forward_attention",
    )(packed, rest, down, key_place, query_place)
    full_rest, full_down, kv, attended, lse = out
    return full_rest.reshape(16 * rows, cols), full_down.reshape(16 * drows, dcols), kv, attended, lse


def backward_kernel(
    grad_att, kv, lse, key_place, query_place, g_down, g_first, g_out,
    grad_packed, o_down, o_first, o_out, *scratch,
):
    (bias, probs, grad_probs, turned, dob, acc, part_send, part_in, dq, packed_send) = scratch[:10]
    send_sems, recv_sems, local_sems = scratch[-3:]
    blocks = scratch[10:-3]
    p = Place()
    w = Wire(send_sems, recv_sems, local_sems)
    greet(all_peers(p) + x_peers(p))
    dob[p.y] = grad_att[p.y]
    to_y = [
        w.push(grad_att.at[step4(p.y, d)], dob.at[p.y], p.ydev(d)) for d in (1, 3, 2)
    ]
    parts = [
        Scatter(w, p, g_down, o_down, 0, 96, 0, 48, True, True, blocks[0:6]),
        Scatter(w, p, g_down, o_down, 0, 96, 48, 48, False, True, blocks[6:12]),
        Scatter(w, p, g_first, o_first, 1, 1536, 0, 768, True, True, blocks[12:18]),
        Scatter(w, p, g_first, o_first, 1, 1536, 768, 768, False, True, blocks[18:24]),
        Scatter(w, p, g_out, o_out, 1, 384, 0, 384, True, True, blocks[24:30]),
    ]
    for part in parts:
        part.p0()
    fill_bias(key_place, query_place, bias)
    for copy in to_y:
        copy.wait_recv()
    stages = [
        lambda: [part.p1() for part in parts[:2]],
        lambda: [part.p1() for part in parts[2:]],
        lambda: [part.p2() for part in parts[:2]],
        lambda: [part.p2() for part in parts[2:]],
        lambda: [part.p3() for part in parts],
        lambda: [part.p4() for part in parts],
    ]
    to_z = []
    for head in range(3):
        turn_keys(kv, head, turned)
        for tile in range(2):
            cols = slice(tile * TILE, tile * TILE + TILE)
            block = head // 2 * 128
            query = kv[p.z, 2 * tile : 2 * tile + 2, :, 384 + block : 512 + block]
            query = half_lanes(query.reshape(TILE, 128), head == 1)
            dout = dob[2 * tile : 2 * tile + 2, :, block : block + 128]
            dout = half_lanes(dout.reshape(TILE, 128), head != 1)
            total = lse[head : head + 1, cols]

            def weigh(i, inner):
                keys = key_chunk(kv, i, head)
                prob = jnp.exp(dot_lanes(keys, query) + bias[chunk_rows(i), cols] - total)
                gprob = dot_lanes(keys, dout)
                probs[chunk_rows(i), :] = prob
                grad_probs[chunk_rows(i), :] = gprob
                return inner + rows_sum(prob * gprob)

            inner = lax.fori_loop(0, GROUP // CHUNK, weigh, jnp.zeros((8, TILE), F32))
            inner = jnp.sum(inner, axis=0, keepdims=True)

            def back(i, total_dq):
                prob = probs[chunk_rows(i), :]
                gscore = (prob * (grad_probs[chunk_rows(i), :] - inner)).astype(BF)
                both = dot_plain(gscore, query) + dot_plain(prob.astype(BF), dout)
                if tile == 0:
                    acc[chunk_rows(i), :] = both
                else:
                    part_send[head, lax.div(i, 2), pl.ds(pl.multiple_of(lax.rem(i, 2) * CHUNK, CHUNK), CHUNK), :] = (
                        acc[chunk_rows(i), :] + both
                    ).astype(BF)
                return total_dq + dot_plain(turned[:, chunk_rows(i)], gscore)

            total_dq = lax.fori_loop(0, GROUP // CHUNK, back, jnp.zeros((128, TILE), F32))
            total_dq = total_dq * (HD ** (-0.5))
            if head == 0:
                dq[0:64, cols] = total_dq[0:64, :]
            elif head == 1:
                dq[64:128, cols] = total_dq[64:128, :]
            else:
                dq[128:192, cols] = total_dq[0:64, :]
            stages[head * 2 + tile]()
        to_z.append(
            [
                w.push(part_send.at[head, step4(p.z, d)], part_in.at[head, d - 1], p.zdev(d))
                for d in (1, 3, 2)
            ]
        )
    dq[192:256, :] = jnp.zeros((64, 512), F32)
    for k in range(4):
        packed_send[k, :, 384:640] = dq[:, k * OWN : k * OWN + OWN].T.astype(BF)
    for head in range(3):
        for copy in to_z[head]:
            copy.wait_recv()
        for k in range(4):
            rows = slice(k * OWN, k * OWN + OWN)
            total = part_send[head, p.z, rows, :].astype(F32)
            for d in range(3):
                total = total + part_in[head, d, rows, :].astype(F32)
            packed_send[k, :, head * 128 : head * 128 + 128] = total.astype(BF)
    grad_packed[p.y] = packed_send[p.y]
    back_y = [
        w.push(packed_send.at[step4(p.y, d)], grad_packed.at[p.y], p.ydev(d)) for d in (1, 3, 2)
    ]
    for copy in back_y:
        copy.wait_recv()
    for part in parts:
        part.end()
    for copy in to_y + back_y + sum(to_z, []):
        copy.wait_send()


def backward_attention(grad_att, kv, lse, key_place, query_place, g_down, g_first, g_out):
    shapes = []
    for rows, cols in ((48, 768), (48, 768), (48, 768), (48, 768), (48, 384)):
        shapes += scatter_shapes(rows, cols, True, BF)
    return pl.pallas_call(
        backward_kernel,
        out_shape=(
            jax.ShapeDtypeStruct((4, OWN, 640), BF),
            jax.ShapeDtypeStruct((192, 768), F32),
            jax.ShapeDtypeStruct((48, 3072), F32),
            jax.ShapeDtypeStruct((48, 768), F32),
        ),
        in_specs=[VMEM] * 5 + [ANY] * 3,
        out_specs=(VMEM,) * 4,
        scratch_shapes=[
            pltpu.VMEM((GROUP, 512), F32),
            pltpu.VMEM((GROUP, TILE), F32),
            pltpu.VMEM((GROUP, TILE), F32),
            pltpu.VMEM((128, GROUP), BF),
            pltpu.VMEM((4, OWN, 256), BF),
            pltpu.VMEM((GROUP, 128), F32),
            pltpu.VMEM((3, 4, 512, 128), BF),
            pltpu.VMEM((3, 3, 512, 128), BF),
            pltpu.VMEM((256, 512), F32),
            pltpu.VMEM((4, OWN, 640), BF),
        ]
        + shapes
        + sems(5 * SCATTER_SENDS + 15, 5),
        compiler_params=pltpu.CompilerParams(
            collective_id=2, has_side_effects=True, vmem_limit_bytes=52 * MIB
        ),
        name="backward_attention",
    )(
        grad_att, kv, lse, key_place, query_place,
        g_down.reshape(4, 4, 192, 768), g_first.reshape(4, 4, 48, 3072), g_out.reshape(4, 4, 48, 768),
    )


def scatter_last_kernel(g_qkv, g_vec, o_qkv, o_vec, *scratch):
    send_sems, recv_sems, local_sems = scratch[-3:]
    p = Place()
    w = Wire(send_sems, recv_sems, local_sems)
    greet(all_peers(p) + x_peers(p))
    parts = [
        Scatter(w, p, g_qkv, o_qkv, 1, 1152, 0, 640, True, True, scratch[0:6]),
        Scatter(w, p, g_qkv, o_qkv, 1, 1152, 640, 512, False, True, scratch[6:12]),
        Scatter(w, p, g_vec, o_vec, 1, 0, 0, 128, False, False, scratch[12:18]),
    ]
    for stage in (Scatter.p0, Scatter.p1, Scatter.p2, Scatter.p3, Scatter.p4, Scatter.end):
        for part in parts:
            stage(part)


def scatter_last(g_qkv, g_vec):
    shapes = scatter_shapes(48, 640, True, BF) + scatter_shapes(48, 512, True, BF)
    shapes += scatter_shapes(48, 128, False, F32)
    return pl.pallas_call(
        scatter_last_kernel,
        out_shape=(jax.ShapeDtypeStruct((48, 2304), F32), jax.ShapeDtypeStruct((48, 128), F32)),
        in_specs=[ANY] * 2,
        out_specs=(VMEM,) * 2,
        scratch_shapes=shapes + sems(3 * SCATTER_SENDS, 3),
        compiler_params=pltpu.CompilerParams(
            collective_id=3, has_side_effects=True, vmem_limit_bytes=24 * MIB
        ),
        name="scatter_last",
    )(g_qkv.reshape(4, 4, 48, 2304), g_vec.reshape(4, 4, 48, 128))


def layer_norm(inputs, gain, shift):
    average = jnp.mean(inputs, -1, keepdims=True)
    centred = inputs - average
    spread = jnp.mean(centred * centred, -1, keepdims=True)
    return centred * lax.rsqrt(spread + EPS_NORM) * gain + shift


def gelu_tanh(inputs):
    return jax.nn.gelu(inputs, approximate=True)


def adamw(weight, moment, second, grad, rate, decay):
    moment_new = BETA_ONE * moment + (1.0 - BETA_ONE) * grad
    second_new = BETA_TWO * second + (1.0 - BETA_TWO) * grad * grad
    moment_hat = moment_new / (1.0 - BETA_ONE**STEP)
    second_hat = second_new / (1.0 - BETA_TWO**STEP)
    weight_new = weight - rate * (moment_hat / (jnp.sqrt(second_hat) + EPS_ADAM) + decay * weight)
    return (weight_new, moment_new, second_new)


def pack_groups(queries, keys, values):
    blank = jnp.zeros((queries.shape[0], HD), queries.dtype)
    groups = []
    for g in range(4):
        q, k, v = ([a[:, (3 * g + j) * HD : (3 * g + j + 1) * HD] for j in range(3)] for a in (queries, keys, values))
        groups.append(jnp.concatenate([k[0], v[0], v[1], k[1], k[2], v[2], q[0], q[1], q[2], blank], 1))
    return jnp.stack(groups)


def unpack_groups(packed):
    dq, dk, dv = [], [], []
    for g in range(4):
        col = [packed[g][:, j * HD : (j + 1) * HD] for j in range(9)]
        dk += [col[0], col[3], col[4]]
        dv += [col[1], col[2], col[5]]
        dq += [col[6], col[7], col[8]]
    return jnp.concatenate(dq + dk + dv, 1)


def pack_outs(matrix):
    blank = jnp.zeros((matrix.shape[0], HD), matrix.dtype)
    groups = []
    for g in range(4):
        o = [matrix[:, (3 * g + j) * HD : (3 * g + j + 1) * HD] for j in range(3)]
        groups.append(jnp.concatenate([o[1], o[0], blank, o[2]], 1))
    return jnp.stack(groups)


def unpack_outs(packed):
    parts = []
    for g in range(4):
        parts += [packed[g][:, HD : 2 * HD], packed[g][:, :HD], packed[g][:, 3 * HD :]]
    return jnp.concatenate(parts, 1)


def per_device(
    tokens,
    cotangent,
    lengths,
    positions,
    w_rows,
    w_down,
    vectors,
    moment_rows,
    second_rows,
    moment_down,
    second_down,
    moment_vectors,
    second_vectors,
):
    tok_rows, model_dim = tokens.shape
    scale = HD ** (-0.5)
    shard_index = lax.axis_index("shard")
    low_rows = w_rows.astype(BF)
    low_vecs = jnp.pad(vectors.astype(BF).T, ((0, 0), (0, 244)))
    full_qkv = gather_first(jnp.concatenate([low_rows[:, : 3 * model_dim], low_vecs], 1))
    vec_vals = full_qkv[:, 3 * model_dim : 3 * model_dim + 12].T.astype(F32)
    gain_one, shift_one, bias_query, bias_value = (
        vec_vals[0],
        vec_vals[1],
        vec_vals[2],
        vec_vals[3],
    )
    bias_out, gain_two, shift_two, bias_down = (vec_vals[4], vec_vals[5], vec_vals[6], vec_vals[7])
    bias_first = vec_vals[8:].reshape(-1)
    w_query_kv = full_qkv[:, : 3 * model_dim]
    place_all = positions[0]
    seq_ends = jnp.cumsum(lengths[0])
    place_quarter = lax.dynamic_slice_in_dim(place_all, lax.div(shard_index, 4) * 512, 512)
    seq_start = jnp.max(
        jnp.where(place_quarter[None, :] >= seq_ends[:, None], seq_ends[:, None], 0), axis=0
    )
    key_place = place_all[:, None]
    query_place = jnp.pad(jnp.stack([place_quarter, seq_start]), ((0, 6), (0, 0)))
    inputs = tokens.astype(F32)
    normed = layer_norm(inputs, gain_one, shift_one).astype(BF)
    projected = jnp.dot(normed, w_query_kv, preferred_element_type=F32)
    queries = (projected[:, :model_dim] + bias_query).astype(BF)
    key_rows = projected[:, model_dim : 2 * model_dim].astype(BF)
    value_rows = (projected[:, 2 * model_dim :] + bias_value).astype(BF)
    packed = pack_groups(queries * jnp.asarray(scale, BF), key_rows, value_rows)
    full_rest, full_down, kv, attended_packed, lse = forward_attention(
        packed, low_rows[:, 3 * model_dim :], w_down.astype(BF), key_place, query_place
    )
    attended = unpack_outs(attended_packed)
    w_out = full_rest[:, :model_dim]
    w_first = full_rest[:, model_dim:]
    middle = inputs + jnp.dot(attended, w_out, preferred_element_type=F32) + bias_out
    normed_two = layer_norm(middle, gain_two, shift_two).astype(BF)
    pre_act = jnp.dot(normed_two, w_first, preferred_element_type=F32) + bias_first
    hidden = gelu_tanh(pre_act).astype(BF)
    outputs = (
        middle + jnp.dot(hidden, full_down, preferred_element_type=F32) + bias_down
    ).astype(BF)
    grad_out = cotangent.astype(F32)
    grad_down = jnp.einsum("ti,to->io", hidden, cotangent, preferred_element_type=F32).astype(BF)
    grad_bias_down = jnp.sum(grad_out, 0)
    grad_hidden = jnp.einsum("to,io->ti", cotangent, full_down, preferred_element_type=F32)
    gelu_back = jax.vjp(gelu_tanh, pre_act)[1]
    grad_pre = gelu_back(grad_hidden)[0].astype(BF)
    grad_first = jnp.einsum("td,ti->di", normed_two, grad_pre, preferred_element_type=F32).astype(BF)
    grad_bias_first = jnp.sum(grad_pre.astype(F32), 0)
    grad_normed_two = jnp.einsum("ti,di->td", grad_pre, w_first, preferred_element_type=F32)
    norm_two_back = jax.vjp(layer_norm, middle, gain_two, shift_two)[1]
    grad_mid_norm, grad_gain_two, grad_shift_two = norm_two_back(grad_normed_two)
    grad_middle = grad_out + grad_mid_norm
    grad_branch = grad_middle.astype(BF)
    grad_out_proj = jnp.einsum("td,to->do", attended, grad_branch, preferred_element_type=F32).astype(BF)
    grad_bias_out = jnp.sum(grad_branch.astype(F32), 0)
    grad_attended = jnp.einsum("to,do->td", grad_branch, w_out, preferred_element_type=F32).astype(BF)
    grad_packed, sum_down, sum_first, sum_out = backward_attention(
        pack_outs(grad_attended), kv, lse, key_place, query_place, grad_down, grad_first, grad_out_proj
    )
    grad_projected = unpack_groups(grad_packed)
    grad_query_kv = jnp.einsum("td,tj->dj", normed, grad_projected, preferred_element_type=F32).astype(BF)
    grad_bias_query = jnp.sum(grad_projected[:, :model_dim].astype(F32), 0)
    grad_bias_value = jnp.sum(grad_projected[:, 2 * model_dim :].astype(F32), 0)
    grad_normed = jnp.einsum("tj,dj->td", grad_projected, w_query_kv, preferred_element_type=F32)
    norm_one_back = jax.vjp(layer_norm, inputs, gain_one, shift_one)[1]
    grad_in_norm, grad_gain_one, grad_shift_one = norm_one_back(grad_normed)
    grad_input = (grad_middle + grad_in_norm).astype(BF)
    grad_vec_local = jnp.concatenate(
        [
            jnp.stack(
                [
                    grad_gain_one,
                    grad_shift_one,
                    grad_bias_query,
                    grad_bias_value,
                    grad_bias_out,
                    grad_gain_two,
                    grad_shift_two,
                    grad_bias_down,
                ]
            ),
            grad_bias_first.reshape(-1, model_dim),
        ],
        0,
    )
    sum_qkv, sum_vec = scatter_last(grad_query_kv, jnp.pad(grad_vec_local.T, ((0, 0), (0, 116))))
    grad_rows = jnp.concatenate([sum_qkv, sum_out, sum_first], 1)
    rows_new = adamw(w_rows, moment_rows, second_rows, grad_rows, LR_MATRIX, DECAY)
    down_new = adamw(w_down, moment_down, second_down, sum_down, LR_MATRIX, DECAY)
    vec_new = adamw(vectors, moment_vectors, second_vectors, sum_vec[:, :12].T, LR_VECTOR, 0.0)
    return (
        outputs,
        grad_input,
        rows_new[0],
        rows_new[1],
        rows_new[2],
        down_new[0],
        down_new[1],
        down_new[2],
        vec_new[0],
        vec_new[1],
        vec_new[2],
    )


def solution(mesh):
    return jax.shard_map(
        per_device,
        mesh=mesh,
        in_specs=(
            P(("replica", "shard"), None),
            P(("replica", "shard"), None),
            P("replica", None),
            P("replica", None),
            P("shard", None),
            P("shard", None),
            P(None, "shard"),
            P("shard", None),
            P("shard", None),
            P("shard", None),
            P("shard", None),
            P(None, "shard"),
            P(None, "shard"),
        ),
        out_specs=(
            P(("replica", "shard"), None),
            P(("replica", "shard"), None),
            P("shard", None),
            P("shard", None),
            P("shard", None),
            P("shard", None),
            P("shard", None),
            P("shard", None),
            P(None, "shard"),
            P(None, "shard"),
            P(None, "shard"),
        ),
        check_vma=False,
    )
```

```python
import functools

import jax
import jax.numpy as jnp
from jax import lax
from jax.experimental import pallas as pl
from jax.experimental.pallas import tpu as pltpu
from jax.sharding import PartitionSpec as P

H = 12
HD = 64
STEP = 10
D = 768
FF = 3072
OWN = 128
GROUP = 2048
NEIGHBOURS = 4
TILE = 256
CHUNK = 256
STEPS = GROUP // CHUNK
MIB = 1 << 20

EPS_NORM = 1e-05
BETA_ONE = 0.9
BETA_TWO = 0.95
EPS_ADAM = 1e-08
LR_MATRIX = 0.02
LR_VECTOR = 0.3
DECAY = 0.1
HUGE_NEG = -1e30

BF = jnp.bfloat16
F32 = jnp.float32
MESH = pl.DeviceIdType.MESH
VMEM = pl.BlockSpec(memory_space=pltpu.VMEM)
ANY = pl.BlockSpec(memory_space=pl.ANY)


def step4(i, d):
    return lax.rem(i + d, 4)


class Place:
    def __init__(self):
        self.r = lax.axis_index("replica")
        self.s = lax.axis_index("shard")
        self.x = lax.div(self.r, 2)
        self.c = lax.rem(self.r, 2)
        self.z = lax.div(self.s, 4)
        self.y = lax.rem(self.s, 4)
        self.u = self.y + self.c * (self.z - self.y)
        self.v = self.z + self.c * (self.y - self.z)
        self.u_step = 1 + 3 * self.c
        self.v_step = 4 - 3 * self.c

    def ydev(self, d):
        return (self.r, self.z * 4 + step4(self.y, d))

    def zdev(self, d):
        return (self.r, step4(self.z, d) * 4 + self.y)

    def xdev(self, d):
        return (step4(self.x, d) * 2 + self.c, self.s)

    def udev(self, d):
        return (self.r, step4(self.u, d) * self.u_step + self.v * self.v_step)

    def vdev(self, d):
        return (self.r, self.u * self.u_step + step4(self.v, d) * self.v_step)

    def sibling(self):
        return (self.x * 2 + 1 - self.c, self.s)


def greet(devices):
    barrier = pltpu.get_barrier_semaphore()
    for device in devices:
        pl.semaphore_signal(barrier, inc=1, device_id=device, device_id_type=MESH)
    pl.semaphore_wait(barrier, len(devices))


class Wire:
    def __init__(self, send_sems, recv_sems, local_sems):
        self.send_sems, self.recv_sems, self.local_sems = send_sems, recv_sems, local_sems
        self.sent, self.moved = 0, 0

    def push(self, src, dst, device):
        k = self.sent
        self.sent += 1
        copy = pltpu.make_async_remote_copy(
            src_ref=src,
            dst_ref=dst,
            send_sem=self.send_sems.at[k],
            recv_sem=self.recv_sems.at[k],
            device_id=device,
            device_id_type=MESH,
        )
        copy.start()
        return copy

    def local(self, src, dst):
        k = self.moved
        self.moved += 1
        copy = pltpu.make_async_copy(src, dst, self.local_sems.at[k])
        copy.start()
        return copy


def sems(remote, local):
    return [
        pltpu.SemaphoreType.DMA((remote,)),
        pltpu.SemaphoreType.DMA((remote,)),
        pltpu.SemaphoreType.DMA((max(local, 1),)),
    ]


def cut(axis, base, size):
    if axis == 0:
        return (pl.ds(pl.multiple_of(base, 16), size), slice(None))
    return (slice(None), pl.ds(pl.multiple_of(base, 128), size))


class Gather:
    def __init__(self, wire, place, shard, full, axis, base, size, y_first):
        self.wire, self.place, self.shard, self.full = wire, place, shard, full
        self.region = cut(axis, base, size)
        self.y_first = y_first

    def slab(self, d):
        p = self.place
        if self.y_first:
            return self.full.at[(step4(p.z, 4 - d), slice(None)) + self.region]
        return self.full.at[(slice(None), step4(p.y, 4 - d)) + self.region]

    def first(self):
        p, w = self.place, self.wire
        src = self.shard.at[self.region]
        dst = self.full.at[(p.z, p.y) + self.region]
        self.own = w.local(src, dst)
        self.one = [w.push(src, dst, p.ydev(d) if self.y_first else p.zdev(d)) for d in (1, 3, 2)]

    def second(self):
        p, w = self.place, self.wire
        self.own.wait()
        for copy in self.one:
            copy.wait_recv()
        slab = self.slab(0)
        self.two = [(d, w.push(slab, slab, p.zdev(d) if self.y_first else p.ydev(d))) for d in (1, 3, 2)]
        self.across = [w.push(slab, slab, p.sibling())]

    def third(self):
        p, w = self.place, self.wire
        for d, copy in self.two:
            copy.wait_recv()
            slab = self.slab(d)
            self.across.append(w.push(slab, slab, p.sibling()))

    def end(self):
        for copy in self.across:
            copy.wait_recv()
        for copy in self.one + [copy for _, copy in self.two] + self.across:
            copy.wait_send()


GATHER_SENDS = 10


def scatter_shapes(rows, cols, shared, dtype):
    shapes = [
        pltpu.VMEM((4, 4, rows, cols), dtype),
        pltpu.VMEM((4, 4, rows, cols), dtype),
        pltpu.VMEM((3, 4, rows, cols), dtype),
        pltpu.VMEM((4, rows, cols), dtype),
        pltpu.VMEM((3, rows, cols), dtype),
        pltpu.VMEM((4, rows, cols), dtype),
    ]
    return shapes


class Scatter:
    def __init__(self, wire, place, grad, out, axis, half, offset, size, z_first, shared, scratch):
        self.wire, self.place, self.grad, self.out = wire, place, grad, out
        self.shared, self.z_first = shared, z_first
        if shared:
            self.mine = cut(axis, place.c * half + offset, size)
            self.other = cut(axis, (1 - place.c) * half + offset, size)
        else:
            self.mine = self.other = (slice(None), slice(None))
        self.held, self.in0, self.in1, self.part, self.in2, self.in3 = scratch
        self.sends = []

    def push(self, src, dst, device):
        copy = self.wire.push(src, dst, device)
        self.sends.append(copy)
        return copy

    def p0(self):
        every = (slice(None), slice(None))
        self.load = self.wire.local(self.grad.at[every + self.mine], self.held)
        self.wait = [self.push(self.grad.at[every + self.other], self.in0, self.place.sibling())]

    def p1(self):
        p = self.place
        self.load.wait()
        self.wait[0].wait_recv()

        def add(i, carry):
            a, b = lax.div(i, 4), lax.rem(i, 4)
            both = self.held[a, b].astype(F32) + self.in0[a, b].astype(F32)
            self.held[a, b] = both.astype(self.held.dtype)
            return carry

        lax.fori_loop(0, 16, add, 0)
        self.wait = []
        for d in (1, 3, 2):
            if self.z_first:
                src, device = self.held.at[step4(p.z, d)], p.zdev(d)
            else:
                src, device = self.held.at[:, step4(p.y, d)], p.ydev(d)
            self.wait.append(self.push(src, self.in1.at[d - 1], device))

    def p2(self):
        p = self.place
        for copy in self.wait:
            copy.wait_recv()

        def add(i, carry):
            own = self.held[p.z, i] if self.z_first else self.held[i, p.y]
            total = own.astype(F32)
            for k in range(3):
                total = total + self.in1[k, i].astype(F32)
            self.part[i] = total.astype(self.part.dtype)
            return carry

        lax.fori_loop(0, 4, add, 0)
        self.wait = []
        for d in (1, 3, 2):
            if self.z_first:
                src, device = self.part.at[step4(p.y, d)], p.ydev(d)
            else:
                src, device = self.part.at[step4(p.z, d)], p.zdev(d)
            self.wait.append(self.push(src, self.in2.at[d - 1], device))

    def p3(self):
        p = self.place
        for copy in self.wait:
            copy.wait_recv()
        total = self.part[p.y if self.z_first else p.z].astype(F32)
        for k in range(3):
            total = total + self.in2[k].astype(F32)
        self.in3[p.x] = total.astype(self.in3.dtype)
        self.wait = [self.push(self.in3.at[p.x], self.in3.at[p.x], p.xdev(d)) for d in (1, 3, 2)]

    def p4(self):
        for copy in self.wait:
            copy.wait_recv()
        total = self.in3[0].astype(F32)
        for k in range(1, 4):
            total = total + self.in3[k].astype(F32)
        self.out[self.mine] = total
        self.wait = []
        if self.shared:
            here = self.out.at[self.mine]
            self.wait = [self.push(here, here, self.place.sibling())]

    def end(self):
        for copy in self.wait:
            copy.wait_recv()
        for copy in self.sends:
            copy.wait_send()


SCATTER_SENDS = 11


def all_peers(p):
    rings = [p.ydev(d) for d in (1, 2, 3)] + [p.zdev(d) for d in (1, 2, 3)]
    return rings + [p.sibling()]


def x_peers(p):
    return [p.xdev(d) for d in (1, 2, 3)]


def gather_first_kernel(shard, full, send_sems, recv_sems, local_sems):
    p = Place()
    w = Wire(send_sems, recv_sems, local_sems)
    greet(all_peers(p))
    half = shard.shape[1] // 2
    size = half // 2
    parts = [
        Gather(w, p, shard, full, 1, p.c * half, size, True),
        Gather(w, p, shard, full, 1, p.c * half + size, size, False),
    ]
    for part in parts:
        part.first()
    for part in parts:
        part.second()
    for part in parts:
        part.third()
    for part in parts:
        part.end()


def gather_first(shard):
    rows, cols = shard.shape
    full = pl.pallas_call(
        gather_first_kernel,
        out_shape=jax.ShapeDtypeStruct((4, 4, rows, cols), BF),
        in_specs=[VMEM],
        out_specs=VMEM,
        scratch_shapes=sems(2 * GATHER_SENDS, 2),
        compiler_params=pltpu.CompilerParams(
            collective_id=0, has_side_effects=True, vmem_limit_bytes=20 * MIB
        ),
        name="gather_first",
    )(shard)
    return full.reshape(16 * rows, cols)


def half_lanes(value, right):
    lane = lax.broadcasted_iota(jnp.int32, value.shape, 1)
    keep = lane >= HD if right else lane < HD
    return jnp.where(keep, value, jnp.zeros_like(value))


def rows_max(value):
    return jnp.max(value.reshape(-1, 8, value.shape[1]), axis=0)


def rows_sum(value):
    return jnp.sum(value.reshape(-1, 8, value.shape[1]), axis=0)


def dot_lanes(left, right):
    return lax.dot_general(left, right, (((1,), (1,)), ((), ())), preferred_element_type=F32)


def dot_plain(left, right):
    return jnp.dot(left, right, preferred_element_type=F32)


def fill_bias(key_place, query_place, bias):
    def body(i, carry):
        rows = pl.ds(pl.multiple_of(i * CHUNK, CHUNK), CHUNK)
        keys = key_place[rows, :]
        ok = (keys <= query_place[0:1, :]) & (keys >= query_place[1:2, :])
        bias[rows, :] = jnp.where(ok, 0.0, HUGE_NEG).astype(BF)
        return carry

    lax.fori_loop(0, STEPS, body, 0, unroll=True)


def key_chunk(packed, i, head):
    a, b = lax.div(i, 2), lax.rem(i, 2) * 2
    return packed[a, pl.ds(b, 2), :, head * 128 : head * 128 + 128].reshape(CHUNK, 128)


def chunk_rows(i):
    return pl.ds(pl.multiple_of(i * CHUNK, CHUNK), CHUNK)


def turn_keys(packed, head, turned):
    def body(i, carry):
        turned[:, chunk_rows(i)] = key_chunk(packed, i, head).T
        return carry

    lax.fori_loop(0, STEPS, body, 0, unroll=True)


def forward_kernel(
    packed, rest, down, key_place, query_place,
    full_rest, full_down, kv, attended, lse,
    bias, scores, turned, head_out, out_send, send_sems, recv_sems, local_sems,
):
    p = Place()
    w = Wire(send_sems, recv_sems, local_sems)
    greet(all_peers(p))
    kv[p.v, p.u] = packed[p.u]
    to_y = [
        w.push(packed.at[step4(p.u, d)], kv.at[p.v, p.u], p.udev(d)) for d in (1, 3, 2)
    ]
    rest_half, down_half = rest.shape[1] // 2, down.shape[0] // 2
    rest_one = 1024
    parts = [
        Gather(w, p, rest, full_rest, 1, p.c * rest_half, rest_one, True),
        Gather(w, p, rest, full_rest, 1, p.c * rest_half + rest_one, rest_half - rest_one, False),
        Gather(w, p, down, full_down, 0, p.c * down_half, down_half // 2, True),
        Gather(w, p, down, full_down, 0, p.c * down_half + down_half // 2, down_half // 2, False),
    ]
    for part in parts:
        part.first()
    for copy in to_y:
        copy.wait_recv()
    mine = kv.at[p.v, :, :, pl.ds(0, 384)]
    to_z = [w.push(mine, mine, p.vdev(d)) for d in (1, 3, 2)]
    for part in parts:
        part.second()
    fill_bias(key_place, query_place, bias)
    for copy in to_z:
        copy.wait_recv()
    head_out[128:192, :] = jnp.zeros((64, 512), F32)
    lse[...] = jnp.zeros_like(lse)
    for head in range(3):
        turn_keys(kv, head, turned)
        for tile in range(2):
            cols = slice(tile * TILE, tile * TILE + TILE)
            query = kv[p.v, 2 * tile : 2 * tile + 2, :, 384 + head // 2 * 128 : 512 + head // 2 * 128]
            query = half_lanes(query.reshape(TILE, 128), head == 1)

            def score(i, top):
                part = dot_lanes(key_chunk(kv, i, head), query) + bias[chunk_rows(i), cols].astype(F32)
                scores[chunk_rows(i), :] = part
                return jnp.maximum(top, rows_max(part))

            top = lax.fori_loop(
                0, STEPS, score, jnp.full((8, TILE), -jnp.inf, F32), unroll=True
            )
            top = jnp.max(top, axis=0, keepdims=True)

            def mix(i, carry):
                total, acc = carry
                raised = jnp.exp(scores[chunk_rows(i), :] - top)
                acc = acc + dot_plain(turned[:, chunk_rows(i)], raised.astype(BF))
                return total + rows_sum(raised), acc

            total, acc = lax.fori_loop(
                0, STEPS, mix, (jnp.zeros((8, TILE), F32), jnp.zeros((128, TILE), F32)), unroll=True
            )
            total = jnp.sum(total, axis=0, keepdims=True)
            acc = acc / total
            if head == 0:
                head_out[64:128, cols] = acc[64:128, :]
            elif head == 1:
                head_out[0:64, cols] = acc[0:64, :]
            else:
                head_out[192:256, cols] = acc[64:128, :]
            lse[head : head + 1, cols] = top + jnp.log(total)
        if head == 1:
            for part in parts:
                part.third()
    for k in range(4):
        turned_out = head_out[:, k * OWN : k * OWN + OWN].T
        out_send[k] = turned_out.astype(BF)
    attended[p.u] = out_send[p.u]
    back = [
        w.push(out_send.at[step4(p.u, d)], attended.at[p.u], p.udev(d)) for d in (1, 3, 2)
    ]
    for copy in back:
        copy.wait_recv()
    for part in parts:
        part.end()
    for copy in to_y + to_z + back:
        copy.wait_send()


def forward_attention(packed, rest, down, key_place, query_place):
    rows, cols = rest.shape
    drows, dcols = down.shape
    out = pl.pallas_call(
        forward_kernel,
        out_shape=(
            jax.ShapeDtypeStruct((4, 4, rows, cols), BF),
            jax.ShapeDtypeStruct((4, 4, drows, dcols), BF),
            jax.ShapeDtypeStruct((4, 4, OWN, 640), BF),
            jax.ShapeDtypeStruct((4, OWN, 256), BF),
            jax.ShapeDtypeStruct((8, 512), F32),
        ),
        in_specs=[VMEM] * 5,
        out_specs=(VMEM, VMEM, VMEM, VMEM, VMEM),
        scratch_shapes=[
            pltpu.VMEM((GROUP, 512), BF),
            pltpu.VMEM((GROUP, TILE), F32),
            pltpu.VMEM((128, GROUP), BF),
            pltpu.VMEM((256, 512), F32),
            pltpu.VMEM((4, OWN, 256), BF),
        ]
        + sems(4 * GATHER_SENDS + 9, 4),
        compiler_params=pltpu.CompilerParams(
            collective_id=1, has_side_effects=True, vmem_limit_bytes=40 * MIB
        ),
        name="forward_attention",
    )(packed, rest, down, key_place, query_place)
    full_rest, full_down, kv, attended, lse = out
    return full_rest.reshape(16 * rows, cols), full_down.reshape(16 * drows, dcols), kv, attended, lse


def backward_kernel(
    grad_att, kv, lse, key_place, query_place, g_down, g_first, g_out,
    grad_packed, o_down, o_first, o_out, *scratch,
):
    (bias, probs, grad_probs, turned, dob, acc, part_send, part_in, dq, packed_send) = scratch[:10]
    send_sems, recv_sems, local_sems = scratch[-3:]
    blocks = scratch[10:-3]
    p = Place()
    w = Wire(send_sems, recv_sems, local_sems)
    greet(all_peers(p) + x_peers(p))
    dob[p.u] = grad_att[p.u]
    to_y = [
        w.push(grad_att.at[step4(p.u, d)], dob.at[p.u], p.udev(d)) for d in (1, 3, 2)
    ]
    parts = [
        Scatter(w, p, g_down, o_down, 0, 96, 0, 48, True, True, blocks[0:6]),
        Scatter(w, p, g_down, o_down, 0, 96, 48, 48, False, True, blocks[6:12]),
        Scatter(w, p, g_first, o_first, 1, 1536, 0, 768, True, True, blocks[12:18]),
        Scatter(w, p, g_first, o_first, 1, 1536, 768, 768, False, True, blocks[18:24]),
        Scatter(w, p, g_out, o_out, 1, 384, 0, 384, True, True, blocks[24:30]),
    ]
    for part in parts:
        part.p0()
    fill_bias(key_place, query_place, bias)
    for copy in to_y:
        copy.wait_recv()
    stages = [
        lambda: [part.p1() for part in parts[:2]],
        lambda: [part.p1() for part in parts[2:]],
        lambda: [part.p2() for part in parts[:2]],
        lambda: [part.p2() for part in parts[2:]],
        lambda: [part.p3() for part in parts],
        lambda: [part.p4() for part in parts],
    ]
    to_z = []
    for head in range(3):
        turn_keys(kv, head, turned)
        for tile in range(2):
            cols = slice(tile * TILE, tile * TILE + TILE)
            block = head // 2 * 128
            query = kv[p.v, 2 * tile : 2 * tile + 2, :, 384 + block : 512 + block]
            query = half_lanes(query.reshape(TILE, 128), head == 1)
            dout = dob[2 * tile : 2 * tile + 2, :, block : block + 128]
            dout = half_lanes(dout.reshape(TILE, 128), head != 1)
            total = lse[head : head + 1, cols]

            def weigh(i, inner):
                keys = key_chunk(kv, i, head)
                prob = jnp.exp(dot_lanes(keys, query) + bias[chunk_rows(i), cols].astype(F32) - total)
                gprob = dot_lanes(keys, dout)
                probs[chunk_rows(i), :] = prob
                grad_probs[chunk_rows(i), :] = gprob
                return inner + rows_sum(prob * gprob)

            inner = lax.fori_loop(0, STEPS, weigh, jnp.zeros((8, TILE), F32), unroll=True)
            inner = jnp.sum(inner, axis=0, keepdims=True)

            def back(i, total_dq):
                prob = probs[chunk_rows(i), :]
                gscore = (prob * (grad_probs[chunk_rows(i), :] - inner)).astype(BF)
                both = dot_plain(gscore, query) + dot_plain(prob.astype(BF), dout)
                if tile == 0:
                    acc[chunk_rows(i), :] = both
                else:
                    part_send[head, lax.div(i, 2), pl.ds(pl.multiple_of(lax.rem(i, 2) * CHUNK, CHUNK), CHUNK), :] = (
                        acc[chunk_rows(i), :] + both
                    ).astype(BF)
                return total_dq + dot_plain(turned[:, chunk_rows(i)], gscore)

            total_dq = lax.fori_loop(0, STEPS, back, jnp.zeros((128, TILE), F32), unroll=True)
            total_dq = total_dq * (HD ** (-0.5))
            if head == 0:
                dq[0:64, cols] = total_dq[0:64, :]
            elif head == 1:
                dq[64:128, cols] = total_dq[64:128, :]
            else:
                dq[128:192, cols] = total_dq[0:64, :]
            stages[head * 2 + tile]()
        to_z.append(
            [
                w.push(part_send.at[head, step4(p.v, d)], part_in.at[head, d - 1], p.vdev(d))
                for d in (1, 3, 2)
            ]
        )
    dq[192:256, :] = jnp.zeros((64, 512), F32)
    for k in range(4):
        packed_send[k, :, 384:640] = dq[:, k * OWN : k * OWN + OWN].T.astype(BF)
    for head in range(3):
        for copy in to_z[head]:
            copy.wait_recv()
        for k in range(4):
            rows = slice(k * OWN, k * OWN + OWN)
            total = part_send[head, p.v, rows, :].astype(F32)
            for d in range(3):
                total = total + part_in[head, d, rows, :].astype(F32)
            packed_send[k, :, head * 128 : head * 128 + 128] = total.astype(BF)
    grad_packed[p.u] = packed_send[p.u]
    back_y = [
        w.push(packed_send.at[step4(p.u, d)], grad_packed.at[p.u], p.udev(d)) for d in (1, 3, 2)
    ]
    for copy in back_y:
        copy.wait_recv()
    for part in parts:
        part.end()
    for copy in to_y + back_y + sum(to_z, []):
        copy.wait_send()


def backward_attention(grad_att, kv, lse, key_place, query_place, g_down, g_first, g_out):
    shapes = []
    for rows, cols in ((48, 768), (48, 768), (48, 768), (48, 768), (48, 384)):
        shapes += scatter_shapes(rows, cols, True, BF)
    return pl.pallas_call(
        backward_kernel,
        out_shape=(
            jax.ShapeDtypeStruct((4, OWN, 640), BF),
            jax.ShapeDtypeStruct((192, 768), F32),
            jax.ShapeDtypeStruct((48, 3072), F32),
            jax.ShapeDtypeStruct((48, 768), F32),
        ),
        in_specs=[VMEM] * 5 + [ANY] * 3,
        out_specs=(VMEM,) * 4,
        scratch_shapes=[
            pltpu.VMEM((GROUP, 512), BF),
            pltpu.VMEM((GROUP, TILE), F32),
            pltpu.VMEM((GROUP, TILE), F32),
            pltpu.VMEM((128, GROUP), BF),
            pltpu.VMEM((4, OWN, 256), BF),
            pltpu.VMEM((GROUP, 128), F32),
            pltpu.VMEM((3, 4, 512, 128), BF),
            pltpu.VMEM((3, 3, 512, 128), BF),
            pltpu.VMEM((256, 512), F32),
            pltpu.VMEM((4, OWN, 640), BF),
        ]
        + shapes
        + sems(5 * SCATTER_SENDS + 15, 5),
        compiler_params=pltpu.CompilerParams(
            collective_id=2, has_side_effects=True, vmem_limit_bytes=52 * MIB
        ),
        name="backward_attention",
    )(
        grad_att, kv, lse, key_place, query_place,
        g_down.reshape(4, 4, 192, 768), g_first.reshape(4, 4, 48, 3072), g_out.reshape(4, 4, 48, 768),
    )


def scatter_last_kernel(g_qkv, g_vec, o_qkv, o_vec, *scratch):
    send_sems, recv_sems, local_sems = scratch[-3:]
    p = Place()
    w = Wire(send_sems, recv_sems, local_sems)
    greet(all_peers(p) + x_peers(p))
    parts = [
        Scatter(w, p, g_qkv, o_qkv, 1, 1152, 0, 640, True, True, scratch[0:6]),
        Scatter(w, p, g_qkv, o_qkv, 1, 1152, 640, 512, False, True, scratch[6:12]),
        Scatter(w, p, g_vec, o_vec, 1, 0, 0, 128, False, False, scratch[12:18]),
    ]
    for stage in (Scatter.p0, Scatter.p1, Scatter.p2, Scatter.p3, Scatter.p4, Scatter.end):
        for part in parts:
            stage(part)


def scatter_last(g_qkv, g_vec):
    shapes = scatter_shapes(48, 640, True, BF) + scatter_shapes(48, 512, True, BF)
    shapes += scatter_shapes(48, 128, False, F32)
    return pl.pallas_call(
        scatter_last_kernel,
        out_shape=(jax.ShapeDtypeStruct((48, 2304), F32), jax.ShapeDtypeStruct((48, 128), F32)),
        in_specs=[ANY] * 2,
        out_specs=(VMEM,) * 2,
        scratch_shapes=shapes + sems(3 * SCATTER_SENDS, 3),
        compiler_params=pltpu.CompilerParams(
            collective_id=3, has_side_effects=True, vmem_limit_bytes=24 * MIB
        ),
        name="scatter_last",
    )(g_qkv.reshape(4, 4, 48, 2304), g_vec.reshape(4, 4, 48, 128))


def layer_norm(inputs, gain, shift):
    average = jnp.mean(inputs, -1, keepdims=True)
    centred = inputs - average
    spread = jnp.mean(centred * centred, -1, keepdims=True)
    return centred * lax.rsqrt(spread + EPS_NORM) * gain + shift


def gelu_tanh(inputs):
    return jax.nn.gelu(inputs, approximate=True)


def adamw(weight, moment, second, grad, rate, decay):
    moment_new = BETA_ONE * moment + (1.0 - BETA_ONE) * grad
    second_new = BETA_TWO * second + (1.0 - BETA_TWO) * grad * grad
    moment_hat = moment_new / (1.0 - BETA_ONE**STEP)
    second_hat = second_new / (1.0 - BETA_TWO**STEP)
    weight_new = weight - rate * (moment_hat / (jnp.sqrt(second_hat) + EPS_ADAM) + decay * weight)
    return (weight_new, moment_new, second_new)


def pack_groups(queries, keys, values):
    blank = jnp.zeros((queries.shape[0], HD), queries.dtype)
    groups = []
    for g in range(4):
        q, k, v = ([a[:, (3 * g + j) * HD : (3 * g + j + 1) * HD] for j in range(3)] for a in (queries, keys, values))
        groups.append(jnp.concatenate([k[0], v[0], v[1], k[1], k[2], v[2], q[0], q[1], q[2], blank], 1))
    return jnp.stack(groups)


def unpack_groups(packed):
    dq, dk, dv = [], [], []
    for g in range(4):
        col = [packed[g][:, j * HD : (j + 1) * HD] for j in range(9)]
        dk += [col[0], col[3], col[4]]
        dv += [col[1], col[2], col[5]]
        dq += [col[6], col[7], col[8]]
    return jnp.concatenate(dq + dk + dv, 1)


def pack_outs(matrix):
    blank = jnp.zeros((matrix.shape[0], HD), matrix.dtype)
    groups = []
    for g in range(4):
        o = [matrix[:, (3 * g + j) * HD : (3 * g + j + 1) * HD] for j in range(3)]
        groups.append(jnp.concatenate([o[1], o[0], blank, o[2]], 1))
    return jnp.stack(groups)


def unpack_outs(packed):
    parts = []
    for g in range(4):
        parts += [packed[g][:, HD : 2 * HD], packed[g][:, :HD], packed[g][:, 3 * HD :]]
    return jnp.concatenate(parts, 1)


def per_device(
    tokens,
    cotangent,
    lengths,
    positions,
    w_rows,
    w_down,
    vectors,
    moment_rows,
    second_rows,
    moment_down,
    second_down,
    moment_vectors,
    second_vectors,
):
    tok_rows, model_dim = tokens.shape
    scale = HD ** (-0.5)
    shard_index = lax.axis_index("shard")
    low_rows = w_rows.astype(BF)
    low_vecs = jnp.pad(vectors.astype(BF).T, ((0, 0), (0, 244)))
    full_qkv = gather_first(jnp.concatenate([low_rows[:, : 3 * model_dim], low_vecs], 1))
    vec_vals = full_qkv[:, 3 * model_dim : 3 * model_dim + 12].T.astype(F32)
    gain_one, shift_one, bias_query, bias_value = (
        vec_vals[0],
        vec_vals[1],
        vec_vals[2],
        vec_vals[3],
    )
    bias_out, gain_two, shift_two, bias_down = (vec_vals[4], vec_vals[5], vec_vals[6], vec_vals[7])
    bias_first = vec_vals[8:].reshape(-1)
    w_query_kv = full_qkv[:, : 3 * model_dim]
    core = lax.rem(lax.axis_index("replica"), 2)
    place_blocks = positions.reshape(4, 4, OWN)
    place_all = jnp.where(core == 0, place_blocks, place_blocks.transpose(1, 0, 2)).reshape(GROUP)
    own_quarter = jnp.where(core == 0, lax.div(shard_index, 4), lax.rem(shard_index, 4))
    seq_ends = jnp.cumsum(lengths[0])
    place_quarter = lax.dynamic_slice_in_dim(place_all, own_quarter * 512, 512)
    seq_start = jnp.max(
        jnp.where(place_quarter[None, :] >= seq_ends[:, None], seq_ends[:, None], 0), axis=0
    )
    key_place = place_all[:, None]
    query_place = jnp.pad(jnp.stack([place_quarter, seq_start]), ((0, 6), (0, 0)))
    inputs = tokens.astype(F32)
    normed = layer_norm(inputs, gain_one, shift_one).astype(BF)
    projected = jnp.dot(normed, w_query_kv, preferred_element_type=F32)
    queries = (projected[:, :model_dim] + bias_query).astype(BF)
    key_rows = projected[:, model_dim : 2 * model_dim].astype(BF)
    value_rows = (projected[:, 2 * model_dim :] + bias_value).astype(BF)
    packed = pack_groups(queries * jnp.asarray(scale, BF), key_rows, value_rows)
    full_rest, full_down, kv, attended_packed, lse = forward_attention(
        packed, low_rows[:, 3 * model_dim :], w_down.astype(BF), key_place, query_place
    )
    attended = unpack_outs(attended_packed)
    w_out = full_rest[:, :model_dim]
    w_first = full_rest[:, model_dim:]
    middle = inputs + jnp.dot(attended, w_out, preferred_element_type=F32) + bias_out
    normed_two = layer_norm(middle, gain_two, shift_two).astype(BF)
    pre_act = jnp.dot(normed_two, w_first, preferred_element_type=F32) + bias_first
    hidden = gelu_tanh(pre_act).astype(BF)
    outputs = (
        middle + jnp.dot(hidden, full_down, preferred_element_type=F32) + bias_down
    ).astype(BF)
    grad_out = cotangent.astype(F32)
    grad_down = jnp.einsum("ti,to->io", hidden, cotangent, preferred_element_type=F32).astype(BF)
    grad_bias_down = jnp.sum(grad_out, 0)
    grad_hidden = jnp.einsum("to,io->ti", cotangent, full_down, preferred_element_type=F32)
    gelu_back = jax.vjp(gelu_tanh, pre_act)[1]
    grad_pre = gelu_back(grad_hidden)[0].astype(BF)
    grad_first = jnp.einsum("td,ti->di", normed_two, grad_pre, preferred_element_type=F32).astype(BF)
    grad_bias_first = jnp.sum(grad_pre.astype(F32), 0)
    grad_normed_two = jnp.einsum("ti,di->td", grad_pre, w_first, preferred_element_type=F32)
    norm_two_back = jax.vjp(layer_norm, middle, gain_two, shift_two)[1]
    grad_mid_norm, grad_gain_two, grad_shift_two = norm_two_back(grad_normed_two)
    grad_middle = grad_out + grad_mid_norm
    grad_branch = grad_middle.astype(BF)
    grad_out_proj = jnp.einsum("td,to->do", attended, grad_branch, preferred_element_type=F32).astype(BF)
    grad_bias_out = jnp.sum(grad_branch.astype(F32), 0)
    grad_attended = jnp.einsum("to,do->td", grad_branch, w_out, preferred_element_type=F32).astype(BF)
    grad_packed, sum_down, sum_first, sum_out = backward_attention(
        pack_outs(grad_attended), kv, lse, key_place, query_place, grad_down, grad_first, grad_out_proj
    )
    grad_projected = unpack_groups(grad_packed)
    grad_query_kv = jnp.einsum("td,tj->dj", normed, grad_projected, preferred_element_type=F32).astype(BF)
    grad_bias_query = jnp.sum(grad_projected[:, :model_dim].astype(F32), 0)
    grad_bias_value = jnp.sum(grad_projected[:, 2 * model_dim :].astype(F32), 0)
    grad_normed = jnp.einsum("tj,dj->td", grad_projected, w_query_kv, preferred_element_type=F32)
    norm_one_back = jax.vjp(layer_norm, inputs, gain_one, shift_one)[1]
    grad_in_norm, grad_gain_one, grad_shift_one = norm_one_back(grad_normed)
    grad_input = (grad_middle + grad_in_norm).astype(BF)
    grad_vec_local = jnp.concatenate(
        [
            jnp.stack(
                [
                    grad_gain_one,
                    grad_shift_one,
                    grad_bias_query,
                    grad_bias_value,
                    grad_bias_out,
                    grad_gain_two,
                    grad_shift_two,
                    grad_bias_down,
                ]
            ),
            grad_bias_first.reshape(-1, model_dim),
        ],
        0,
    )
    sum_qkv, sum_vec = scatter_last(grad_query_kv, jnp.pad(grad_vec_local.T, ((0, 0), (0, 116))))
    grad_rows = jnp.concatenate([sum_qkv, sum_out, sum_first], 1)
    rows_new = adamw(w_rows, moment_rows, second_rows, grad_rows, LR_MATRIX, DECAY)
    down_new = adamw(w_down, moment_down, second_down, sum_down, LR_MATRIX, DECAY)
    vec_new = adamw(vectors, moment_vectors, second_vectors, sum_vec[:, :12].T, LR_VECTOR, 0.0)
    return (
        outputs,
        grad_input,
        rows_new[0],
        rows_new[1],
        rows_new[2],
        down_new[0],
        down_new[1],
        down_new[2],
        vec_new[0],
        vec_new[1],
        vec_new[2],
    )


def solution(mesh):
    return jax.shard_map(
        per_device,
        mesh=mesh,
        in_specs=(
            P(("replica", "shard"), None),
            P(("replica", "shard"), None),
            P("replica", None),
            P("replica", None),
            P("shard", None),
            P("shard", None),
            P(None, "shard"),
            P("shard", None),
            P("shard", None),
            P("shard", None),
            P("shard", None),
            P(None, "shard"),
            P(None, "shard"),
        ),
        out_specs=(
            P(("replica", "shard"), None),
            P(("replica", "shard"), None),
            P("shard", None),
            P("shard", None),
            P("shard", None),
            P("shard", None),
            P("shard", None),
            P("shard", None),
            P(None, "shard"),
            P(None, "shard"),
            P(None, "shard"),
        ),
        check_vma=False,
    )
```

```python
import functools

import jax
import jax.numpy as jnp
from jax import lax
from jax.experimental import pallas as pl
from jax.experimental.pallas import tpu as pltpu
from jax.sharding import PartitionSpec as P

H = 12
HD = 64
STEP = 10
D = 768
FF = 3072
OWN = 128
GROUP = 2048
NEIGHBOURS = 4
TILE = 256
CHUNK = 256
STEPS = GROUP // CHUNK
MIB = 1 << 20

EPS_NORM = 1e-05
BETA_ONE = 0.9
BETA_TWO = 0.95
EPS_ADAM = 1e-08
LR_MATRIX = 0.02
LR_VECTOR = 0.3
DECAY = 0.1
HUGE_NEG = -1e30

BF = jnp.bfloat16
F32 = jnp.float32
MESH = pl.DeviceIdType.MESH
VMEM = pl.BlockSpec(memory_space=pltpu.VMEM)
ANY = pl.BlockSpec(memory_space=pl.ANY)


def step4(i, d):
    return lax.rem(i + d, 4)


class Place:
    def __init__(self):
        self.r = lax.axis_index("replica")
        self.s = lax.axis_index("shard")
        self.x = lax.div(self.r, 2)
        self.c = lax.rem(self.r, 2)
        self.z = lax.div(self.s, 4)
        self.y = lax.rem(self.s, 4)
        self.u = self.y + self.c * (self.z - self.y)
        self.v = self.z + self.c * (self.y - self.z)
        self.u_step = 1 + 3 * self.c
        self.v_step = 4 - 3 * self.c

    def ydev(self, d):
        return (self.r, self.z * 4 + step4(self.y, d))

    def zdev(self, d):
        return (self.r, step4(self.z, d) * 4 + self.y)

    def xdev(self, d):
        return (step4(self.x, d) * 2 + self.c, self.s)

    def udev(self, d):
        return (self.r, step4(self.u, d) * self.u_step + self.v * self.v_step)

    def vdev(self, d):
        return (self.r, self.u * self.u_step + step4(self.v, d) * self.v_step)

    def sibling(self):
        return (self.x * 2 + 1 - self.c, self.s)


def greet(devices):
    barrier = pltpu.get_barrier_semaphore()
    for device in devices:
        pl.semaphore_signal(barrier, inc=1, device_id=device, device_id_type=MESH)
    pl.semaphore_wait(barrier, len(devices))


class Wire:
    def __init__(self, send_sems, recv_sems, local_sems):
        self.send_sems, self.recv_sems, self.local_sems = send_sems, recv_sems, local_sems
        self.sent, self.moved = 0, 0

    def push(self, src, dst, device):
        k = self.sent
        self.sent += 1
        copy = pltpu.make_async_remote_copy(
            src_ref=src,
            dst_ref=dst,
            send_sem=self.send_sems.at[k],
            recv_sem=self.recv_sems.at[k],
            device_id=device,
            device_id_type=MESH,
        )
        copy.start()
        return copy

    def local(self, src, dst):
        k = self.moved
        self.moved += 1
        copy = pltpu.make_async_copy(src, dst, self.local_sems.at[k])
        copy.start()
        return copy


def sems(remote, local):
    return [
        pltpu.SemaphoreType.DMA((remote,)),
        pltpu.SemaphoreType.DMA((remote,)),
        pltpu.SemaphoreType.DMA((max(local, 1),)),
    ]


def region(row, rows, col, cols):
    row_cut = slice(None) if rows is None else pl.ds(row, rows)
    col_cut = slice(None) if cols is None else pl.ds(pl.multiple_of(col, 128), cols)
    return (row_cut, col_cut)


class Gather:
    def __init__(self, wire, place, shard, full, cut, y_first):
        self.wire, self.place, self.shard, self.full, self.cut = wire, place, shard, full, cut
        self.y_first = y_first
        self.near = place.ydev if y_first else place.zdev
        self.far = place.zdev if y_first else place.ydev
        self.sends = []

    def push(self, src, dst, device):
        copy = self.wire.push(src, dst, device)
        self.sends.append(copy)
        return copy

    def slab(self, d, blocks=slice(None)):
        p = self.place
        if self.y_first:
            return self.full.at[(step4(p.z, 4 - d), blocks) + self.cut]
        return self.full.at[(blocks, step4(p.y, 4 - d)) + self.cut]

    def first(self):
        p = self.place
        src = self.shard.at[self.cut]
        dst = self.full.at[(p.z, p.y) + self.cut]
        self.own = self.wire.local(src, dst)
        self.one = [self.push(src, dst, self.near(d)) for d in (1, 3, 2)]

    def second(self):
        self.own.wait()
        for copy in self.one:
            copy.wait_recv()
        slab = self.slab(0)
        self.two = [self.push(slab, slab, self.far(d)) for d in (1, 3)]
        self.across = [self.push(slab, slab, self.place.sibling())]

    def third(self):
        self.two[0].wait_recv()
        half = self.slab(1, pl.ds(0, 2))
        self.three = [self.push(half, half, self.far(1))]
        self.two[1].wait_recv()
        half = self.slab(3, pl.ds(2, 2))
        self.three.append(self.push(half, half, self.far(3)))
        for d in (1, 3):
            slab = self.slab(d)
            self.across.append(self.push(slab, slab, self.place.sibling()))

    def fourth(self):
        for copy in self.three:
            copy.wait_recv()
        slab = self.slab(2)
        self.across.append(self.push(slab, slab, self.place.sibling()))

    def end(self):
        for copy in self.across:
            copy.wait_recv()
        for copy in self.sends:
            copy.wait_send()


GATHER_SENDS = 11


def scatter_shapes(rows, cols, dtype):
    return [
        pltpu.VMEM((4, 4, rows, cols), dtype),
        pltpu.VMEM((3, 4, rows, cols), dtype),
        pltpu.VMEM((4, rows, cols), dtype),
        pltpu.VMEM((3, rows, cols), dtype),
        pltpu.VMEM((4, rows, cols), dtype),
    ]


class Scatter:
    def __init__(self, wire, place, grad, out, mine, other, z_first, shared, scratch):
        self.wire, self.place, self.grad, self.out = wire, place, grad, out
        self.shared, self.z_first = shared, z_first
        self.mine, self.other = mine, other
        self.in0, self.in1, self.part, self.in2, self.in3 = scratch
        self.sends, self.wait = [], []

    def push(self, src, dst, device):
        copy = self.wire.push(src, dst, device)
        self.sends.append(copy)
        return copy

    def p0(self):
        every = (slice(None), slice(None))
        self.wait.append(self.push(self.grad.at[every + self.other], self.in0, self.place.sibling()))

    def p0_slab(self, i):
        here = self.grad.at[(i, slice(None)) + self.other]
        self.wait.append(self.push(here, self.in0.at[i], self.place.sibling()))

    def p1(self):
        p = self.place
        for copy in self.wait:
            copy.wait_recv()
        if not self.shared:
            for copy in self.sends:
                copy.wait_send()
            self.sends = []

        def add(i, carry):
            at = (lax.div(i, 4), lax.rem(i, 4))
            both = self.grad[at + self.mine].astype(F32) + self.in0[at].astype(F32)
            self.grad[at + self.mine] = both.astype(self.grad.dtype)
            return carry

        lax.fori_loop(0, 16, add, 0)
        self.wait = []
        for d in (1, 3, 2):
            if self.z_first:
                src, device = self.grad.at[(step4(p.z, d), slice(None)) + self.mine], p.zdev(d)
            else:
                src, device = self.grad.at[(slice(None), step4(p.y, d)) + self.mine], p.ydev(d)
            self.wait.append(self.push(src, self.in1.at[d - 1], device))

    def p2(self):
        p = self.place
        for copy in self.wait:
            copy.wait_recv()

        def add(i, carry):
            at = (p.z, i) if self.z_first else (i, p.y)
            total = self.grad[at + self.mine].astype(F32)
            for k in range(3):
                total = total + self.in1[k, i].astype(F32)
            self.part[i] = total.astype(self.part.dtype)
            return carry

        lax.fori_loop(0, 4, add, 0)
        self.wait = []
        for d in (1, 3, 2):
            if self.z_first:
                src, device = self.part.at[step4(p.y, d)], p.ydev(d)
            else:
                src, device = self.part.at[step4(p.z, d)], p.zdev(d)
            self.wait.append(self.push(src, self.in2.at[d - 1], device))

    def p3(self):
        p = self.place
        for copy in self.wait:
            copy.wait_recv()
        total = self.part[p.y if self.z_first else p.z].astype(F32)
        for k in range(3):
            total = total + self.in2[k].astype(F32)
        self.in3[p.x] = total.astype(self.in3.dtype)
        self.wait = [self.push(self.in3.at[p.x], self.in3.at[p.x], p.xdev(d)) for d in (1, 3, 2)]

    def p4(self):
        for copy in self.wait:
            copy.wait_recv()
        total = self.in3[0].astype(F32)
        for k in range(1, 4):
            total = total + self.in3[k].astype(F32)
        self.out[self.mine] = total
        self.wait = []
        if self.shared:
            here = self.out.at[self.mine]
            self.wait = [self.push(here, here, self.place.sibling())]

    def end(self):
        for copy in self.wait:
            copy.wait_recv()
        for copy in self.sends:
            copy.wait_send()


SCATTER_SENDS = 14


def all_peers(p):
    rings = [p.ydev(d) for d in (1, 2, 3)] + [p.zdev(d) for d in (1, 2, 3)]
    return rings + [p.sibling()]


def x_peers(p):
    return [p.xdev(d) for d in (1, 2, 3)]


def owner(p, u, v):
    return v * p.v_step + u * p.u_step


def first_kernel(x, w_qkv, vec, x_all, w_all, vec_all, send_sems, recv_sems, local_sems):
    p = Place()
    w = Wire(send_sems, recv_sems, local_sems)
    greet(all_peers(p))
    one = [(d, w.push(w_qkv.at[step4(p.u, d)], w_all.at[p.s], p.udev(d))) for d in (1, 3, 2)]
    vec_one = [w.push(vec, vec_all.at[p.s], p.ydev(d)) for d in (1, 3, 2)]
    w_all[p.s] = w_qkv[p.u]
    vec_all[p.s] = vec[...]
    two = [w.push(w_all.at[p.s], w_all.at[p.s], p.vdev(e)) for e in (1, 3, 2)]
    rows = [w.push(x, x_all.at[p.u], p.udev(d)) for d in (1, 3, 2)]
    x_all[p.u] = x[...]
    for d, copy in one:
        copy.wait_recv()
        block = w_all.at[owner(p, step4(p.u, 4 - d), p.v)]
        two += [w.push(block, block, p.vdev(e)) for e in (1, 3, 2)]
    for copy in vec_one:
        copy.wait_recv()
    slab = vec_all.at[pl.ds(p.z * 4, 4)]
    vec_two = [w.push(slab, slab, p.zdev(d)) for d in (1, 3, 2)]
    for copy in two + rows + vec_two:
        copy.wait_recv()
    for copy in [c for _, c in one] + vec_one + two + rows + vec_two:
        copy.wait_send()


def gather_first(x, w_qkv, vec):
    return pl.pallas_call(
        first_kernel,
        out_shape=(
            jax.ShapeDtypeStruct((4, OWN, D), BF),
            jax.ShapeDtypeStruct((16, 48, 640), BF),
            jax.ShapeDtypeStruct((16, 16, 128), BF),
        ),
        in_specs=[VMEM] * 3,
        out_specs=(VMEM,) * 3,
        scratch_shapes=sems(24, 1),
        compiler_params=pltpu.CompilerParams(
            collective_id=0, has_side_effects=True, vmem_limit_bytes=20 * MIB
        ),
        name="gather_first",
    )(x, w_qkv, vec)

def half_lanes(value, right):
    lane = lax.broadcasted_iota(jnp.int32, value.shape, 1)
    keep = lane >= HD if right else lane < HD
    return jnp.where(keep, value, jnp.zeros_like(value))


def rows_max(value):
    return jnp.max(value.reshape(-1, 8, value.shape[1]), axis=0)


def rows_sum(value):
    return jnp.sum(value.reshape(-1, 8, value.shape[1]), axis=0)


def dot_lanes(left, right):
    return lax.dot_general(left, right, (((1,), (1,)), ((), ())), preferred_element_type=F32)


def dot_plain(left, right):
    return jnp.dot(left, right, preferred_element_type=F32)


def fill_bias(key_place, query_place, bias):
    def body(i, carry):
        rows = pl.ds(pl.multiple_of(i * CHUNK, CHUNK), CHUNK)
        keys = key_place[rows, :]
        ok = (keys <= query_place[0:1, :]) & (keys >= query_place[1:2, :])
        bias[rows, :] = jnp.where(ok, 0.0, HUGE_NEG).astype(BF)
        return carry

    lax.fori_loop(0, STEPS, body, 0, unroll=True)


def key_chunk(kv, i, head):
    a, b = lax.div(i, 2), lax.rem(i, 2) * CHUNK
    return kv[a, pl.ds(pl.multiple_of(b, CHUNK), CHUNK), head * 128 : head * 128 + 128]


def chunk_rows(i):
    return pl.ds(pl.multiple_of(i * CHUNK, CHUNK), CHUNK)


def turn_keys(kv, head, turned):
    def body(i, carry):
        turned[head, :, chunk_rows(i)] = key_chunk(kv, i, head).T
        return carry

    lax.fori_loop(0, STEPS, body, 0, unroll=True)


def query_tile(kv, p, head, tile):
    block = 384 + head // 2 * 128
    return half_lanes(kv[p.v, tile * TILE : tile * TILE + TILE, block : block + 128], head != 1)


def attend(kv, p, head, tile, bias, scores, turned, head_out, lse):
    cols = slice(tile * TILE, tile * TILE + TILE)
    query = query_tile(kv, p, head, tile)

    def score(i, top):
        part = dot_lanes(key_chunk(kv, i, head), query) + bias[chunk_rows(i), cols].astype(F32)
        scores[chunk_rows(i), :] = part
        return jnp.maximum(top, rows_max(part))

    top = lax.fori_loop(0, STEPS, score, jnp.full((8, TILE), -jnp.inf, F32), unroll=True)
    top = jnp.max(top, axis=0, keepdims=True)

    def mix(i, carry):
        total, acc = carry
        raised = jnp.exp(scores[chunk_rows(i), :] - top)
        acc = acc + dot_plain(turned[head, :, chunk_rows(i)], raised.astype(BF))
        return total + rows_sum(raised), acc

    total, acc = lax.fori_loop(
        0, STEPS, mix, (jnp.zeros((8, TILE), F32), jnp.zeros((128, TILE), F32)), unroll=True
    )
    total = jnp.sum(total, axis=0, keepdims=True)
    acc = acc / total
    at = 64 if head == 1 else 0
    head_out[head * 64 : head * 64 + 64, cols] = acc[at : at + 64, :]
    lse[head : head + 1, cols] = top + jnp.log(total)


def attend_back(kv, p, head, tile, bias, probs, grad_probs, turned, dob, lse, acc, part_send, dq):
    cols = slice(tile * TILE, tile * TILE + TILE)
    query = query_tile(kv, p, head, tile)
    block = head // 2 * 128
    dout = dob[2 * tile : 2 * tile + 2, :, block : block + 128]
    dout = half_lanes(dout.reshape(TILE, 128), head == 1)
    total = lse[head : head + 1, cols]

    def weigh(i, inner):
        keys = key_chunk(kv, i, head)
        prob = jnp.exp(dot_lanes(keys, query) + bias[chunk_rows(i), cols].astype(F32) - total)
        gprob = dot_lanes(keys, dout)
        probs[chunk_rows(i), :] = prob
        grad_probs[chunk_rows(i), :] = gprob
        return inner + rows_sum(prob * gprob)

    inner = lax.fori_loop(0, STEPS, weigh, jnp.zeros((8, TILE), F32), unroll=True)
    inner = jnp.sum(inner, axis=0, keepdims=True)

    def back(i, total_dq):
        prob = probs[chunk_rows(i), :]
        gscore = (prob * (grad_probs[chunk_rows(i), :] - inner)).astype(BF)
        both = dot_plain(gscore, query) + dot_plain(prob.astype(BF), dout)
        if tile == 0:
            acc[chunk_rows(i), :] = both
        else:
            rows = pl.ds(pl.multiple_of(lax.rem(i, 2) * CHUNK, CHUNK), CHUNK)
            part_send[head, lax.div(i, 2), rows, :] = (acc[chunk_rows(i), :] + both).astype(BF)
        return total_dq + dot_plain(turned[head, :, chunk_rows(i)], gscore)

    total_dq = lax.fori_loop(0, STEPS, back, jnp.zeros((128, TILE), F32), unroll=True)
    total_dq = total_dq * (HD ** (-0.5))
    at = 0 if head == 1 else 64
    row = (64, 0, 192)[head]
    dq[row : row + 64, cols] = total_dq[at : at + 64, :]


def col_sum(value):
    return jnp.sum(value, axis=0, keepdims=True)


def normalise(value):
    average = jnp.mean(value, -1, keepdims=True)
    centred = value - average
    spread = jnp.mean(centred * centred, -1, keepdims=True)
    inverse = lax.rsqrt(spread + EPS_NORM)
    return centred * inverse, inverse


def normalise_back(grad, unit, inverse, gain):
    g = grad * gain
    return inverse * (
        g - jnp.mean(g, -1, keepdims=True) - unit * jnp.mean(g * unit, -1, keepdims=True)
    )


GELU_A = 0.7978845608028654
GELU_B = 0.044715


def out_rows(full_rest, g):
    own = full_rest[g, :, :, 0:D].reshape(192, D)
    return jnp.concatenate([own, jnp.zeros((64, D), BF)], 0)


def layer_kernel(
    packed, x, cot, rest, down, key_place, query_place, vecs, bias_first,
    grad_packed, outputs, grad_middle, grad_vecs, o_down, o_first, o_out, *scratch,
):
    (
        full_rest, full_down, kv, bias, probs, grad_probs, turned, head_out, out_send, attended, lse,
        g_down, g_first, g_out, grad_send, dob, acc, part_send, part_in, dq, total_out, total_dc, low,
    ) = scratch[:23]
    blocks = scratch[23:-3]
    p = Place()
    w = Wire(*scratch[-3:])
    greet(all_peers(p) + x_peers(p))

    kv[p.v] = packed[...]
    mine = kv.at[p.v, :, pl.ds(0, 384)]
    to_v = [w.push(mine, mine, p.vdev(d)) for d in (1, 3, 2)]
    half = p.c * 1920
    parts = [
        Gather(w, p, rest, full_rest, region(0, None, half, 1024), True),
        Gather(w, p, rest, full_rest, region(0, None, half + 1024, 896), False),
        Gather(w, p, down, full_down, region(pl.multiple_of(p.c * 96, 16), 48, 0, None), True),
        Gather(w, p, down, full_down, region(pl.multiple_of(p.c * 96 + 48, 16), 48, 0, None), False),
    ]
    for part in parts:
        part.first()
    fill_bias(key_place, query_place, bias)
    for part in parts:
        part.second()
    for copy in to_v:
        copy.wait_recv()
    head_out[192:256, :] = jnp.zeros((64, 512), F32)
    for head in range(3):
        turn_keys(kv, head, turned)
        for tile in range(2):
            attend(kv, p, head, tile, bias, probs, turned, head_out, lse)
        if head == 1:
            for part in parts[:2]:
                part.third()
    for k in range(4):
        out_send[k] = head_out[:, k * OWN : k * OWN + OWN].T.astype(BF)
    attended[p.u] = out_send[p.u]
    out_back = [w.push(out_send.at[step4(p.u, d)], attended.at[p.u], p.udev(d)) for d in (1, 3, 2)]
    for part in parts[2:]:
        part.third()
    for part in parts:
        part.fourth()
    for copy in out_back:
        copy.wait_recv()
    for part in parts:
        part.end()
    for copy in to_v + out_back:
        copy.wait_send()

    grad_y = cot[...].astype(F32)
    middle = x[...].astype(F32) + vecs[4:5, :]
    for g in range(4):
        middle = middle + dot_plain(attended[g], out_rows(full_rest, g))
    unit, inverse = normalise(middle)
    low[0] = (unit * vecs[5:6, :] + vecs[6:7, :]).astype(BF)
    total_out[...] = middle + vecs[7:8, :]
    total_dc[...] = jnp.zeros((OWN, D), F32)
    low_turned = low[0].T

    def first_part(i):
        at = i * D + p.c * 384
        to = i * D + (1 - p.c) * 384
        return Scatter(
            w, p, g_first, o_first, region(0, None, at, 384), region(0, None, to, 384),
            i % 2 == 0, True, blocks[5 * i : 5 * i + 5],
        )

    firsts = [first_part(i) for i in range(4)]
    at, to = p.c * 384, (1 - p.c) * 384
    downs = [
        Scatter(w, p, g_down, o_down, region(0, 96, at, 384), region(0, 96, to, 384), True, True, blocks[20:25]),
        Scatter(w, p, g_down, o_down, region(96, 96, at, 384), region(96, 96, to, 384), False, True, blocks[25:30]),
    ]
    outs = [
        Scatter(w, p, g_out, o_out, region(0, None, at, 384), region(0, None, to, 384), False, True, blocks[30:35])
    ]
    for i in range(4):
        w_first = full_rest[:, :, :, D + i * D : 2 * D + i * D].reshape(D, D)
        w_down = full_down[i].reshape(D, D)
        act = dot_plain(low[0], w_first) + bias_first[i : i + 1, :]
        square = act * act
        bent = jnp.tanh(GELU_A * (act + GELU_B * act * square))
        hidden = (0.5 * act * (1.0 + bent)).astype(BF)
        slope = 0.5 * (1.0 + bent) + 0.5 * act * (1.0 - bent * bent) * (
            GELU_A * (1.0 + 3.0 * GELU_B * square)
        )
        g_down[i] = dot_plain(hidden.T, cot[...]).astype(BF).reshape(4, 192, D)
        for part in downs:
            part.p0_slab(i)
        grad_act = (dot_lanes(cot[...], w_down) * slope).astype(BF)
        grad_vecs[8 + i : 9 + i, :] = col_sum(grad_act.astype(F32))
        g_first[:, :, :, i * D : i * D + D] = (
            dot_plain(low_turned, grad_act).astype(BF).reshape(4, 4, 48, D)
        )
        firsts[i].p0()
        total_dc[...] += dot_lanes(grad_act, w_first)
        total_out[...] += dot_plain(hidden, w_down)
        if i > 0:
            firsts[i - 1].p1()
    outputs[...] = total_out[...].astype(BF)

    grad_c = total_dc[...]
    grad_m = grad_y + normalise_back(grad_c, unit, inverse, vecs[5:6, :])
    grad_middle[...] = grad_m
    low[1] = grad_m.astype(BF)
    for g in range(4):
        grad_send[g] = dot_lanes(low[1], out_rows(full_rest, g)).astype(BF)
    dob[p.u] = grad_send[p.u]
    to_u = [w.push(grad_send.at[step4(p.u, d)], dob.at[p.u], p.udev(d)) for d in (1, 3, 2)]
    for g in range(4):
        g_out[g] = dot_plain(attended[g].T, low[1])[0:192, :].astype(BF).reshape(4, 48, D)
    outs[0].p0()
    grad_vecs[0:4, :] = jnp.zeros((4, D), F32)
    grad_vecs[4:5, :] = col_sum(low[1].astype(F32))
    grad_vecs[5:6, :] = col_sum(grad_c * unit)
    grad_vecs[6:7, :] = col_sum(grad_c)
    grad_vecs[7:8, :] = col_sum(grad_y)
    grad_vecs[12:16, :] = jnp.zeros((4, D), F32)
    for copy in to_u:
        copy.wait_recv()

    stages = [
        lambda: [part.p1() for part in firsts[3:] + downs],
        lambda: [part.p2() for part in firsts[:2]] + [outs[0].p1()],
        lambda: [part.p2() for part in firsts[2:]] + [part.p3() for part in firsts[:2]],
        lambda: [part.p2() for part in downs],
        lambda: [part.p3() for part in firsts[2:]] + [outs[0].p2()] + [part.p4() for part in firsts[:2]],
        lambda: [part.p3() for part in downs + outs],
    ]
    to_v_back = []
    for head in range(3):
        for tile in range(2):
            attend_back(
                kv, p, head, tile, bias, probs, grad_probs, turned, dob, lse, acc, part_send, dq
            )
            if tile == 1:
                to_v_back.append(
                    [
                        w.push(part_send.at[head, step4(p.v, d)], part_in.at[head, d - 1], p.vdev(d))
                        for d in (1, 3, 2)
                    ]
                )
            stages[head * 2 + tile]()
    dq[128:192, :] = jnp.zeros((64, 512), F32)
    for k in range(4):
        rows = slice(k * OWN, k * OWN + OWN)
        grad_packed[rows, 384:640] = dq[:, rows].T.astype(BF)
    for head in range(3):
        for copy in to_v_back[head]:
            copy.wait_recv()
        for k in range(4):
            rows = slice(k * OWN, k * OWN + OWN)
            total = part_send[head, p.v, rows, :].astype(F32)
            for d in range(3):
                total = total + part_in[head, d, rows, :].astype(F32)
            grad_packed[rows, head * 128 : head * 128 + 128] = total.astype(BF)
    for part in firsts[2:] + downs + outs:
        part.p4()
    for part in firsts + downs + outs:
        part.end()
    for copy in to_u + sum(to_v_back, []):
        copy.wait_send()


def layer(packed, x, cot, rest, down, key_place, query_place, vecs, bias_first):
    shapes = [
        pltpu.VMEM((4, 4, 48, 5 * D), BF),
        pltpu.VMEM((4, 4, 192, D), BF),
        pltpu.VMEM((4, 512, 640), BF),
        pltpu.VMEM((GROUP, 512), BF),
        pltpu.VMEM((GROUP, TILE), F32),
        pltpu.VMEM((GROUP, TILE), F32),
        pltpu.VMEM((3, 128, GROUP), BF),
        pltpu.VMEM((256, 512), F32),
        pltpu.VMEM((4, OWN, 256), BF),
        pltpu.VMEM((4, OWN, 256), BF),
        pltpu.VMEM((8, 512), F32),
        pltpu.VMEM((4, 4, 192, D), BF),
        pltpu.VMEM((4, 4, 48, FF), BF),
        pltpu.VMEM((4, 4, 48, D), BF),
        pltpu.VMEM((4, OWN, 256), BF),
        pltpu.VMEM((4, OWN, 256), BF),
        pltpu.VMEM((GROUP, 128), F32),
        pltpu.VMEM((3, 4, 512, 128), BF),
        pltpu.VMEM((3, 3, 512, 128), BF),
        pltpu.VMEM((256, 512), F32),
        pltpu.VMEM((OWN, D), F32),
        pltpu.VMEM((OWN, D), F32),
        pltpu.VMEM((2, OWN, D), BF),
    ]
    for rows in (48, 48, 48, 48, 96, 96, 48):
        shapes += scatter_shapes(rows, 384, BF)
    return pl.pallas_call(
        layer_kernel,
        out_shape=(
            jax.ShapeDtypeStruct((512, 640), BF),
            jax.ShapeDtypeStruct((OWN, D), BF),
            jax.ShapeDtypeStruct((OWN, D), F32),
            jax.ShapeDtypeStruct((16, D), F32),
            jax.ShapeDtypeStruct((192, D), F32),
            jax.ShapeDtypeStruct((48, FF), F32),
            jax.ShapeDtypeStruct((48, D), F32),
        ),
        in_specs=[VMEM] * 9,
        out_specs=(VMEM,) * 7,
        scratch_shapes=shapes + sems(4 * GATHER_SENDS + 7 * SCATTER_SENDS + 18, 4),
        compiler_params=pltpu.CompilerParams(
            collective_id=1, has_side_effects=True, vmem_limit_bytes=60 * MIB
        ),
        name="layer",
    )(packed, x, cot, rest, down, key_place, query_place, vecs, bias_first)


def last_kernel(grad_a, g_qkv, g_vec, o_a, o_qkv, o_vec, *scratch):
    in_a, in1, part, in2, in0, held, in3 = scratch[:7]
    vec_blocks = scratch[7:12]
    p = Place()
    w = Wire(*scratch[-3:])
    greet(all_peers(p) + x_peers(p))
    vec = Scatter(
        w, p, g_vec, o_vec, (slice(None), slice(None)), (slice(None), slice(None)), False, False, vec_blocks
    )
    one = []
    for d in (1, 3, 2):
        for k in range(4):
            src = g_qkv.at[owner(p, k, step4(p.v, d))]
            one.append(w.push(src, in1.at[d - 1, k], p.vdev(d)))
    rows = [w.push(grad_a.at[step4(p.u, d)], in_a.at[d - 1], p.udev(d)) for d in (1, 3, 2)]
    vec.p0()
    for copy in one:
        copy.wait_recv()
    for k in range(4):
        total = g_qkv[owner(p, k, p.v)].astype(F32)
        for d in range(3):
            total = total + in1[d, k].astype(F32)
        part[k] = total.astype(BF)
    two = [w.push(part.at[step4(p.u, d)], in2.at[p.u], p.udev(d)) for d in (1, 3, 2)]
    in2[p.u] = part[p.u]
    vec.p1()
    for copy in two:
        copy.wait_recv()
    other = in2.at[pl.ds((1 - p.c) * 2, 2)]
    three = [w.push(other, in0, p.sibling())]
    vec.p2()
    three[0].wait_recv()
    for k in range(2):
        held[k] = (in2[p.c * 2 + k].astype(F32) + in0[k].astype(F32)).astype(BF)
    in3[p.x] = held[...]
    four = [w.push(held, in3.at[p.x], p.xdev(d)) for d in (1, 3, 2)]
    for copy in rows:
        copy.wait_recv()
    total = grad_a[p.u].astype(F32)
    for d in range(3):
        total = total + in_a[d].astype(F32)
    o_a[...] = total
    vec.p3()
    for copy in four:
        copy.wait_recv()
    for k in range(2):
        total = in3[0, k].astype(F32)
        for d in range(1, 4):
            total = total + in3[d, k].astype(F32)
        o_qkv[p.c * 2 + k] = total
    here = o_qkv.at[pl.ds(p.c * 2, 2)]
    five = [w.push(here, here, p.sibling())]
    vec.p4()
    five[0].wait_recv()
    vec.end()
    for copy in one + rows + two + three + four + five:
        copy.wait_send()


def scatter_last(grad_a, g_qkv, g_vec):
    shapes = [
        pltpu.VMEM((3, OWN, D), BF),
        pltpu.VMEM((3, 4, 48, 640), BF),
        pltpu.VMEM((4, 48, 640), BF),
        pltpu.VMEM((4, 48, 640), BF),
        pltpu.VMEM((2, 48, 640), BF),
        pltpu.VMEM((2, 48, 640), BF),
        pltpu.VMEM((4, 2, 48, 640), BF),
    ]
    shapes += scatter_shapes(16, 128, F32)
    return pl.pallas_call(
        last_kernel,
        out_shape=(
            jax.ShapeDtypeStruct((OWN, D), F32),
            jax.ShapeDtypeStruct((4, 48, 640), F32),
            jax.ShapeDtypeStruct((16, 128), F32),
        ),
        in_specs=[VMEM] * 3,
        out_specs=(VMEM,) * 3,
        scratch_shapes=shapes + sems(SCATTER_SENDS + 24, 1),
        compiler_params=pltpu.CompilerParams(
            collective_id=2, has_side_effects=True, vmem_limit_bytes=24 * MIB
        ),
        name="scatter_last",
    )(grad_a, g_qkv, g_vec)


def adamw(weight, moment, second, grad, rate, decay):
    moment_new = BETA_ONE * moment + (1.0 - BETA_ONE) * grad
    second_new = BETA_TWO * second + (1.0 - BETA_TWO) * grad * grad
    moment_hat = moment_new / (1.0 - BETA_ONE**STEP)
    second_hat = second_new / (1.0 - BETA_TWO**STEP)
    weight_new = weight - rate * (moment_hat / (jnp.sqrt(second_hat) + EPS_ADAM) + decay * weight)
    return (weight_new, moment_new, second_new)


def pack_groups(queries, keys, values):
    blank = jnp.zeros((queries.shape[0], HD), queries.dtype)
    groups = []
    for g in range(4):
        q, k, v = ([a[:, (3 * g + j) * HD : (3 * g + j + 1) * HD] for j in range(3)] for a in (queries, keys, values))
        groups.append(jnp.concatenate([v[0], k[0], k[1], v[1], v[2], k[2], q[1], q[0], blank, q[2]], 1))
    return jnp.stack(groups)


def unpack_group(packed):
    col = [packed[:, j * HD : (j + 1) * HD] for j in range(10)]
    return [jnp.concatenate([col[j] for j in order], 1) for order in ((7, 6, 9), (1, 2, 5), (0, 3, 4))]


def per_device(
    tokens,
    cotangent,
    lengths,
    positions,
    w_rows,
    w_down,
    vectors,
    moment_rows,
    second_rows,
    moment_down,
    second_down,
    moment_vectors,
    second_vectors,
):
    shard_index = lax.axis_index("shard")
    core = lax.rem(lax.axis_index("replica"), 2)
    z, y = lax.div(shard_index, 4), lax.rem(shard_index, 4)
    own_u, own_v = jnp.where(core == 0, y, z), jnp.where(core == 0, z, y)
    low_rows = w_rows.astype(BF)
    low_qkv = pack_groups(low_rows[:, :D], low_rows[:, D : 2 * D], low_rows[:, 2 * D : 3 * D])
    low_vecs = jnp.pad(vectors.astype(BF), ((0, 4), (0, 80)))
    x_quarter, w_qkv, vec_all = gather_first(tokens, low_qkv, low_vecs)
    w_qkv = w_qkv.reshape(D, 640)
    vecs = vec_all[:, :, :48].transpose(1, 0, 2).reshape(16, D).astype(F32)

    place_blocks = positions.reshape(4, 4, OWN)
    place_all = jnp.where(core == 0, place_blocks, place_blocks.transpose(1, 0, 2)).reshape(GROUP)
    seq_ends = jnp.cumsum(lengths[0])
    place_quarter = lax.dynamic_slice_in_dim(place_all, own_v * 512, 512)
    seq_start = jnp.max(
        jnp.where(place_quarter[None, :] >= seq_ends[:, None], seq_ends[:, None], 0), axis=0
    )
    key_place = place_all[:, None]
    query_place = jnp.pad(jnp.stack([place_quarter, seq_start]), ((0, 6), (0, 0)))

    unit_quarter, _ = normalise(x_quarter.reshape(512, D).astype(F32))
    normed = (unit_quarter * vecs[0:1] + vecs[1:2]).astype(BF)
    projected = jnp.dot(normed, w_qkv, preferred_element_type=F32)
    bias_all = pack_groups(vecs[2:3], jnp.zeros((1, D), F32), vecs[3:4])
    bias_own = lax.dynamic_index_in_dim(bias_all, own_u, 0, keepdims=False)
    scale = jnp.where(jnp.arange(640) < 384, 1.0, HD ** (-0.5)).astype(BF)
    packed = (projected + bias_own).astype(BF) * scale
    grad_packed, outputs, grad_middle, vec_grads, sum_down, sum_first, sum_out = layer(
        packed, tokens, cotangent, low_rows[:, 3 * D :], w_down.astype(BF), key_place, query_place,
        vecs, vecs[8:16],
    )

    grad_qkv = jnp.einsum("td,tj->dj", normed, grad_packed, preferred_element_type=F32).astype(BF)
    grad_a = jnp.einsum("tj,dj->td", grad_packed, w_qkv, preferred_element_type=F32)
    bias_sums = unpack_group(jnp.sum(grad_packed.astype(F32), 0, keepdims=True))
    column = own_u * 192
    blank = jnp.zeros((1, D), F32)
    vec_grads = vec_grads + jnp.concatenate(
        [
            jnp.sum(grad_a * unit_quarter, 0, keepdims=True),
            jnp.sum(grad_a, 0, keepdims=True),
            lax.dynamic_update_slice(blank, bias_sums[0], (0, column)),
            lax.dynamic_update_slice(blank, bias_sums[2], (0, column)),
            jnp.zeros((12, D), F32),
        ],
        0,
    )
    vec_send = jnp.pad(vec_grads.reshape(16, 16, 48).transpose(1, 0, 2), ((0, 0), (0, 0), (0, 80)))
    grad_normed, sum_qkv, sum_vec = scatter_last(
        grad_a.astype(BF).reshape(4, OWN, D), grad_qkv.reshape(16, 48, 640), vec_send.reshape(4, 4, 16, 128)
    )
    unit, inverse = normalise(tokens.astype(F32))
    grad_input = (grad_middle + normalise_back(grad_normed, unit, inverse, vecs[0:1])).astype(BF)
    groups = [unpack_group(sum_qkv[g]) for g in range(4)]
    grad_rows = jnp.concatenate(
        [groups[g][k] for k in range(3) for g in range(4)] + [sum_out, sum_first], 1
    )
    rows_new = adamw(w_rows, moment_rows, second_rows, grad_rows, LR_MATRIX, DECAY)
    down_new = adamw(w_down, moment_down, second_down, sum_down, LR_MATRIX, DECAY)
    vec_new = adamw(vectors, moment_vectors, second_vectors, sum_vec[:12, :48], LR_VECTOR, 0.0)
    return (
        outputs,
        grad_input,
        rows_new[0],
        rows_new[1],
        rows_new[2],
        down_new[0],
        down_new[1],
        down_new[2],
        vec_new[0],
        vec_new[1],
        vec_new[2],
    )


def solution(mesh):
    return jax.shard_map(
        per_device,
        mesh=mesh,
        in_specs=(
            P(("replica", "shard"), None),
            P(("replica", "shard"), None),
            P("replica", None),
            P("replica", None),
            P("shard", None),
            P("shard", None),
            P(None, "shard"),
            P("shard", None),
            P("shard", None),
            P("shard", None),
            P("shard", None),
            P(None, "shard"),
            P(None, "shard"),
        ),
        out_specs=(
            P(("replica", "shard"), None),
            P(("replica", "shard"), None),
            P("shard", None),
            P("shard", None),
            P("shard", None),
            P("shard", None),
            P("shard", None),
            P("shard", None),
            P(None, "shard"),
            P(None, "shard"),
            P(None, "shard"),
        ),
        check_vma=False,
    )
```

```python
import functools

import jax
import jax.numpy as jnp
from jax import lax
from jax.experimental import pallas as pl
from jax.experimental.pallas import tpu as pltpu
from jax.sharding import PartitionSpec as P

H = 12
HD = 64
STEP = 10
D = 768
FF = 3072
OWN = 128
GROUP = 2048
NEIGHBOURS = 4
TILE = 256
CHUNK = 256
STEPS = GROUP // CHUNK
MIB = 1 << 20

EPS_NORM = 1e-05
BETA_ONE = 0.9
BETA_TWO = 0.95
EPS_ADAM = 1e-08
LR_MATRIX = 0.02
LR_VECTOR = 0.3
DECAY = 0.1
HUGE_NEG = -1e30

BF = jnp.bfloat16
F32 = jnp.float32
MESH = pl.DeviceIdType.MESH
VMEM = pl.BlockSpec(memory_space=pltpu.VMEM)
ANY = pl.BlockSpec(memory_space=pl.ANY)


def step4(i, d):
    return lax.rem(i + d, 4)


class Place:
    def __init__(self):
        self.r = lax.axis_index("replica")
        self.s = lax.axis_index("shard")
        self.x = lax.div(self.r, 2)
        self.c = lax.rem(self.r, 2)
        self.z = lax.div(self.s, 4)
        self.y = lax.rem(self.s, 4)
        self.u = self.y + self.c * (self.z - self.y)
        self.v = self.z + self.c * (self.y - self.z)
        self.u_step = 1 + 3 * self.c
        self.v_step = 4 - 3 * self.c

    def ydev(self, d):
        return (self.r, self.z * 4 + step4(self.y, d))

    def zdev(self, d):
        return (self.r, step4(self.z, d) * 4 + self.y)

    def xdev(self, d):
        return (step4(self.x, d) * 2 + self.c, self.s)

    def udev(self, d):
        return (self.r, step4(self.u, d) * self.u_step + self.v * self.v_step)

    def vdev(self, d):
        return (self.r, self.u * self.u_step + step4(self.v, d) * self.v_step)

    def sibling(self):
        return (self.x * 2 + 1 - self.c, self.s)


def greet(devices):
    barrier = pltpu.get_barrier_semaphore()
    for device in devices:
        pl.semaphore_signal(barrier, inc=1, device_id=device, device_id_type=MESH)
    pl.semaphore_wait(barrier, len(devices))


class Wire:
    def __init__(self, send_sems, recv_sems, local_sems):
        self.send_sems, self.recv_sems, self.local_sems = send_sems, recv_sems, local_sems
        self.sent, self.moved = 0, 0

    def push(self, src, dst, device):
        k = self.sent
        self.sent += 1
        copy = pltpu.make_async_remote_copy(
            src_ref=src,
            dst_ref=dst,
            send_sem=self.send_sems.at[k],
            recv_sem=self.recv_sems.at[k],
            device_id=device,
            device_id_type=MESH,
        )
        copy.start()
        return copy

    def local(self, src, dst):
        k = self.moved
        self.moved += 1
        copy = pltpu.make_async_copy(src, dst, self.local_sems.at[k])
        copy.start()
        return copy


def sems(remote, local):
    return [
        pltpu.SemaphoreType.DMA((remote,)),
        pltpu.SemaphoreType.DMA((remote,)),
        pltpu.SemaphoreType.DMA((max(local, 1),)),
    ]


def region(row, rows, col, cols):
    row_cut = slice(None) if rows is None else pl.ds(row, rows)
    col_cut = slice(None) if cols is None else pl.ds(pl.multiple_of(col, 128), cols)
    return (row_cut, col_cut)


class Gather:
    def __init__(self, wire, place, shard, full, cut, y_first):
        self.wire, self.place, self.shard, self.full, self.cut = wire, place, shard, full, cut
        self.y_first = y_first
        self.near = place.ydev if y_first else place.zdev
        self.far = place.zdev if y_first else place.ydev
        self.sends = []

    def push(self, src, dst, device):
        copy = self.wire.push(src, dst, device)
        self.sends.append(copy)
        return copy

    def slab(self, d, blocks=slice(None)):
        p = self.place
        if self.y_first:
            return self.full.at[(step4(p.z, 4 - d), blocks) + self.cut]
        return self.full.at[(blocks, step4(p.y, 4 - d)) + self.cut]

    def first(self):
        p = self.place
        src = self.shard.at[self.cut]
        dst = self.full.at[(p.z, p.y) + self.cut]
        self.own = self.wire.local(src, dst)
        self.one = [self.push(src, dst, self.near(d)) for d in (1, 3, 2)]

    def second(self):
        self.own.wait()
        for copy in self.one:
            copy.wait_recv()
        slab = self.slab(0)
        self.two = [self.push(slab, slab, self.far(d)) for d in (1, 3)]
        self.across = [self.push(slab, slab, self.place.sibling())]

    def third(self):
        self.two[0].wait_recv()
        half = self.slab(1, pl.ds(0, 2))
        self.three = [self.push(half, half, self.far(1))]
        self.two[1].wait_recv()
        half = self.slab(3, pl.ds(2, 2))
        self.three.append(self.push(half, half, self.far(3)))
        for d in (1, 3):
            slab = self.slab(d)
            self.across.append(self.push(slab, slab, self.place.sibling()))

    def fourth(self):
        for copy in self.three:
            copy.wait_recv()
        slab = self.slab(2)
        self.across.append(self.push(slab, slab, self.place.sibling()))

    def end(self):
        for copy in self.across:
            copy.wait_recv()
        for copy in self.sends:
            copy.wait_send()


GATHER_SENDS = 11


def scatter_shapes(rows, cols, dtype):
    return [
        pltpu.VMEM((4, 4, rows, cols), dtype),
        pltpu.VMEM((3, 4, rows, cols), dtype),
        pltpu.VMEM((4, rows, cols), dtype),
        pltpu.VMEM((3, rows, cols), dtype),
        pltpu.VMEM((4, rows, cols), dtype),
    ]


class Scatter:
    def __init__(self, wire, place, grad, out, mine, other, to, z_first, scratch):
        self.wire, self.place, self.grad, self.out = wire, place, grad, out
        self.z_first = z_first
        self.mine, self.other, self.to = mine, other, to
        self.in0, self.in1, self.part, self.in2, self.in3 = scratch
        self.sends, self.wait = [], []

    def push(self, src, dst, device):
        copy = self.wire.push(src, dst, device)
        self.sends.append(copy)
        return copy

    def p0(self):
        every = (slice(None), slice(None))
        self.wait.append(self.push(self.grad.at[every + self.other], self.in0, self.place.sibling()))

    def p0_slab(self, i):
        here = self.grad.at[(i, slice(None)) + self.other]
        self.wait.append(self.push(here, self.in0.at[i], self.place.sibling()))

    def p1(self):
        p = self.place
        for copy in self.wait:
            copy.wait_recv()

        def add(i, carry):
            at = (lax.div(i, 4), lax.rem(i, 4))
            both = self.grad[at + self.mine].astype(F32) + self.in0[at].astype(F32)
            self.grad[at + self.mine] = both.astype(self.grad.dtype)
            return carry

        lax.fori_loop(0, 16, add, 0)
        self.wait = []
        for d in (1, 3, 2):
            if self.z_first:
                src, device = self.grad.at[(step4(p.z, d), slice(None)) + self.mine], p.zdev(d)
            else:
                src, device = self.grad.at[(slice(None), step4(p.y, d)) + self.mine], p.ydev(d)
            self.wait.append(self.push(src, self.in1.at[d - 1], device))

    def p2(self):
        p = self.place
        for copy in self.wait:
            copy.wait_recv()

        def add(i, carry):
            at = (p.z, i) if self.z_first else (i, p.y)
            total = self.grad[at + self.mine].astype(F32)
            for k in range(3):
                total = total + self.in1[k, i].astype(F32)
            self.part[i] = total.astype(self.part.dtype)
            return carry

        lax.fori_loop(0, 4, add, 0)
        self.wait = []
        for d in (1, 3, 2):
            if self.z_first:
                src, device = self.part.at[step4(p.y, d)], p.ydev(d)
            else:
                src, device = self.part.at[step4(p.z, d)], p.zdev(d)
            self.wait.append(self.push(src, self.in2.at[d - 1], device))

    def p3(self):
        p = self.place
        for copy in self.wait:
            copy.wait_recv()
        total = self.part[p.y if self.z_first else p.z].astype(F32)
        for k in range(3):
            total = total + self.in2[k].astype(F32)
        self.in3[p.x] = total.astype(self.in3.dtype)
        self.wait = [self.push(self.in3.at[p.x], self.in3.at[p.x], p.xdev(d)) for d in (1, 3, 2)]

    def p4(self):
        for copy in self.wait:
            copy.wait_recv()
        total = self.in3[0].astype(F32)
        for k in range(1, 4):
            total = total + self.in3[k].astype(F32)
        self.out[self.to] = total
        here = self.out.at[self.to]
        self.wait = [self.push(here, here, self.place.sibling())]

    def end(self):
        for copy in self.wait:
            copy.wait_recv()
        for copy in self.sends:
            copy.wait_send()


SCATTER_SENDS = 14


def all_peers(p):
    rings = [p.ydev(d) for d in (1, 2, 3)] + [p.zdev(d) for d in (1, 2, 3)]
    return rings + [p.sibling()]


def x_peers(p):
    return [p.xdev(d) for d in (1, 2, 3)]


def owner(p, u, v):
    return v * p.v_step + u * p.u_step


def half_lanes(value, right):
    lane = lax.broadcasted_iota(jnp.int32, value.shape, 1)
    keep = lane >= HD if right else lane < HD
    return jnp.where(keep, value, jnp.zeros_like(value))


def rows_max(value):
    return jnp.max(value.reshape(-1, 8, value.shape[1]), axis=0)


def rows_sum(value):
    return jnp.sum(value.reshape(-1, 8, value.shape[1]), axis=0)


def dot_lanes(left, right):
    return lax.dot_general(left, right, (((1,), (1,)), ((), ())), preferred_element_type=F32)


def dot_plain(left, right):
    return jnp.dot(left, right, preferred_element_type=F32)


def fill_bias(key_place, query_place, bias):
    def body(i, carry):
        rows = pl.ds(pl.multiple_of(i * CHUNK, CHUNK), CHUNK)
        keys = key_place[rows, 0:128]
        for k in range(4):
            cols = slice(k * 128, k * 128 + 128)
            ok = (keys <= query_place[0:1, cols]) & (keys >= query_place[1:2, cols])
            bias[rows, cols] = jnp.where(ok, 0.0, HUGE_NEG).astype(BF)
        return carry

    lax.fori_loop(0, STEPS, body, 0, unroll=True)


def key_chunk(kv, i, head):
    a, b = lax.div(i, 2), lax.rem(i, 2) * CHUNK
    return kv[a, pl.ds(pl.multiple_of(b, CHUNK), CHUNK), head * 128 : head * 128 + 128]


def chunk_rows(i):
    return pl.ds(pl.multiple_of(i * CHUNK, CHUNK), CHUNK)


def turn_keys(kv, head, turned):
    def body(i, carry):
        turned[head, :, chunk_rows(i)] = key_chunk(kv, i, head).T
        return carry

    lax.fori_loop(0, STEPS, body, 0, unroll=True)


def query_tile(kv, p, head, tile):
    block = 384 + head // 2 * 128
    return half_lanes(kv[p.v, tile * TILE : tile * TILE + TILE, block : block + 128], head != 1)


def attend(kv, p, head, tile, bias, scores, turned, head_out, lse):
    cols = slice(tile * TILE, tile * TILE + TILE)
    query = query_tile(kv, p, head, tile)

    def score(i, top):
        part = dot_lanes(key_chunk(kv, i, head), query) + bias[chunk_rows(i), cols].astype(F32)
        scores[chunk_rows(i), :] = part
        return jnp.maximum(top, rows_max(part))

    top = lax.fori_loop(0, STEPS, score, jnp.full((8, TILE), -jnp.inf, F32), unroll=True)
    top = jnp.max(top, axis=0, keepdims=True)

    def mix(i, carry):
        total, acc = carry
        raised = jnp.exp(scores[chunk_rows(i), :] - top)
        acc = acc + dot_plain(turned[head, :, chunk_rows(i)], raised.astype(BF))
        return total + rows_sum(raised), acc

    total, acc = lax.fori_loop(
        0, STEPS, mix, (jnp.zeros((8, TILE), F32), jnp.zeros((128, TILE), F32)), unroll=True
    )
    total = jnp.sum(total, axis=0, keepdims=True)
    acc = acc / total
    at = 64 if head == 1 else 0
    head_out[head * 64 : head * 64 + 64, cols] = acc[at : at + 64, :]
    lse[head : head + 1, cols] = top + jnp.log(total)


def attend_back(kv, p, head, tile, bias, probs, grad_probs, turned, dob, lse, acc, part_send, dq):
    cols = slice(tile * TILE, tile * TILE + TILE)
    query = query_tile(kv, p, head, tile)
    block = head // 2 * 128
    dout = dob[2 * tile : 2 * tile + 2, :, block : block + 128]
    dout = half_lanes(dout.reshape(TILE, 128), head == 1)
    total = lse[head : head + 1, cols]

    def weigh(i, inner):
        keys = key_chunk(kv, i, head)
        prob = jnp.exp(dot_lanes(keys, query) + bias[chunk_rows(i), cols].astype(F32) - total)
        gprob = dot_lanes(keys, dout)
        probs[chunk_rows(i), :] = prob
        grad_probs[chunk_rows(i), :] = gprob
        return inner + rows_sum(prob * gprob)

    inner = lax.fori_loop(0, STEPS, weigh, jnp.zeros((8, TILE), F32), unroll=True)
    inner = jnp.sum(inner, axis=0, keepdims=True)

    def back(i, total_dq):
        prob = probs[chunk_rows(i), :]
        gscore = (prob * (grad_probs[chunk_rows(i), :] - inner)).astype(BF)
        both = dot_plain(gscore, query) + dot_plain(prob.astype(BF), dout)
        if tile == 0:
            acc[chunk_rows(i), :] = both
        else:
            total_kv = (acc[chunk_rows(i), :] + both).astype(BF)
            lanes = slice(head * 128, head * 128 + 128)
            part_send[lax.div(i, 2), pl.ds(lax.rem(i, 2) * 2, 2), 0:OWN, lanes] = total_kv.reshape(2, OWN, 128)
        return total_dq + dot_plain(turned[head, :, chunk_rows(i)], gscore)

    total_dq = lax.fori_loop(0, STEPS, back, jnp.zeros((128, TILE), F32), unroll=True)
    total_dq = total_dq * (HD ** (-0.5))
    at = 0 if head == 1 else 64
    row = (64, 0, 192)[head]
    dq[row : row + 64, cols] = total_dq[at : at + 64, :]


def col_sum(value):
    return jnp.sum(value, axis=0, keepdims=True)


def normalise(value):
    average = jnp.mean(value, -1, keepdims=True)
    centred = value - average
    spread = jnp.mean(centred * centred, -1, keepdims=True)
    inverse = lax.rsqrt(spread + EPS_NORM)
    return centred * inverse, inverse


def normalise_back(grad, unit, inverse, gain):
    g = grad * gain
    return inverse * (
        g - jnp.mean(g, -1, keepdims=True) - unit * jnp.mean(g * unit, -1, keepdims=True)
    )


GELU_A = 0.7978845608028654
GELU_B = 0.044715


def out_rows(full_rest, g):
    own = full_rest[g, :, :, 0:D].reshape(192, D)
    return jnp.concatenate([own, jnp.zeros((64, D), BF)], 0)


def ordered_sum(blocks):
    total = blocks[0].astype(F32)
    for k in range(1, blocks.shape[0]):
        total = total + blocks[k].astype(F32)
    return total


def natural_group(packed):
    col = [packed[:, j * HD : (j + 1) * HD] for j in range(10)]
    return [[col[j] for j in order] for order in ((7, 6, 9), (1, 2, 5), (0, 3, 4))]


def layer_kernel(
    x, cot, w_qkv, vec, lanes, rest, down, key_place, query_place,
    outputs, grad_input, o_rows, o_down, o_vec, *scratch,
):
    (
        full_rest, full_down, kv, bias, probs, grad_probs, turned, head_out, out_send, attended, lse,
        g_down, g_first, g_out, dob, acc, part_in, total_out, total_dc, low,
        x_all, w_all, normed, vec_y, vec_z, vecs, grad_vecs, vec_in, back, in_a, in1, part, in2, in0, held, in3, packed_sum,
    ) = scratch[:37]
    part_send, grad_send, dq = full_down, out_send, head_out
    blocks = scratch[37:-3]
    p = Place()
    w = Wire(*scratch[-3:])
    greet(all_peers(p) + x_peers(p))

    places = w.local(key_place, grad_probs.at[:, pl.ds(0, 128)])
    w_one = [(d, w.push(w_qkv.at[step4(p.u, d)], w_all.at[p.s], p.udev(d))) for d in (1, 3, 2)]
    vec_one = [w.push(vec, vec_y.at[p.y], p.ydev(d)) for d in (1, 3, 2)]
    w_all[p.s] = w_qkv[p.u]
    vec_y[p.y] = vec[...]
    w_two = [w.push(w_all.at[p.s], w_all.at[p.s], p.vdev(e)) for e in (1, 3, 2)]
    x_one = [w.push(x, x_all.at[p.u], p.udev(d)) for d in (1, 3, 2)]
    x_all[p.u] = x[...]
    for d, copy in w_one:
        copy.wait_recv()
        block = w_all.at[owner(p, step4(p.u, 4 - d), p.v)]
        w_two += [w.push(block, block, p.vdev(e)) for e in (1, 3, 2)]
    for copy in vec_one:
        copy.wait_recv()
    vec_z[p.z] = ordered_sum(vec_y).astype(BF)
    vec_two = [w.push(vec_z.at[p.z], vec_z.at[p.z], p.zdev(d)) for d in (1, 3, 2)]
    half = p.c * 1920
    parts = [
        Gather(w, p, rest, full_rest, region(0, None, half, 1024), True),
        Gather(w, p, rest, full_rest, region(0, None, half + 1024, 896), False),
        Gather(w, p, down, full_down, region(pl.multiple_of(p.c * 96, 16), 48, 0, None), True),
        Gather(w, p, down, full_down, region(pl.multiple_of(p.c * 96 + 48, 16), 48, 0, None), False),
    ]
    for part_ in parts:
        part_.first()
    places.wait()
    fill_bias(grad_probs, query_place, bias)
    for copy in x_one + vec_two:
        copy.wait_recv()
    vecs[...] = ordered_sum(vec_z)
    low_vecs = vecs[...].astype(BF)

    def pick(row, dtype):
        column = lax.broadcasted_iota(jnp.int32, (D, 640), 0) - 192 * p.u
        return (column == lanes[row : row + 1, :]).astype(dtype)

    bias_own = dot_plain(low_vecs, pick(0, BF))[2:3, :] + dot_plain(low_vecs, pick(1, BF))[3:4, :]
    scale = jnp.where(lax.broadcasted_iota(jnp.int32, (1, 640), 1) < 384, 1.0, HD ** (-0.5)).astype(F32)
    for k in range(4):
        unit, _ = normalise(x_all[k].astype(F32))
        normed[k] = (unit * vecs[0:1, :] + vecs[1:2, :]).astype(BF)
    for copy in w_two:
        copy.wait_recv()
    for k in range(4):
        projected = dot_plain(normed[k], w_all[...].reshape(D, 640)) + bias_own
        kv[p.v, k * OWN : k * OWN + OWN, :] = (projected.astype(BF).astype(F32) * scale).astype(BF)
    mine = kv.at[p.v, :, pl.ds(0, 384)]
    to_v = [w.push(mine, mine, p.vdev(d)) for d in (1, 3, 2)]
    for part_ in parts:
        part_.second()
    for copy in to_v:
        copy.wait_recv()
    head_out[192:256, :] = jnp.zeros((64, 512), F32)
    for head in range(3):
        turn_keys(kv, head, turned)
        for tile in range(2):
            attend(kv, p, head, tile, bias, probs, turned, head_out, lse)
        if head == 1:
            for part_ in parts[:2]:
                part_.third()
    for k in range(4):
        out_send[k] = head_out[:, k * OWN : k * OWN + OWN].T.astype(BF)
    attended[p.u] = out_send[p.u]
    out_back = [w.push(out_send.at[step4(p.u, d)], attended.at[p.u], p.udev(d)) for d in (1, 3, 2)]
    for part_ in parts[2:]:
        part_.third()
    for part_ in parts:
        part_.fourth()
    for copy in out_back:
        copy.wait_recv()
    for part_ in parts:
        part_.end()
    for copy in to_v + out_back + x_one + w_two + vec_one + vec_two + [c for _, c in w_one]:
        copy.wait_send()

    grad_y = cot[...].astype(F32)
    middle = x[...].astype(F32) + vecs[4:5, :]
    for g in range(4):
        middle = middle + dot_plain(attended[g], out_rows(full_rest, g))
    unit, inverse = normalise(middle)
    low[0] = (unit * vecs[5:6, :] + vecs[6:7, :]).astype(BF)
    total_out[...] = middle + vecs[7:8, :]
    total_dc[...] = jnp.zeros((OWN, D), F32)
    low_turned = low[0].T

    def first_part(i):
        at = i * D + p.c * 384
        to = i * D + (1 - p.c) * 384
        return Scatter(
            w, p, g_first, o_rows, region(0, None, at, 384), region(0, None, to, 384),
            region(0, None, at + 4 * D, 384), i % 2 == 0, blocks[5 * i : 5 * i + 5],
        )

    firsts = [first_part(i) for i in range(4)]
    at, to = p.c * 384, (1 - p.c) * 384
    downs = [
        Scatter(
            w, p, g_down, o_down, region(0, 96, at, 384), region(0, 96, to, 384),
            region(0, 96, at, 384), True, blocks[20:25],
        ),
        Scatter(
            w, p, g_down, o_down, region(96, 96, at, 384), region(96, 96, to, 384),
            region(96, 96, at, 384), False, blocks[25:30],
        ),
    ]
    outs = [
        Scatter(
            w, p, g_out, o_rows, region(0, None, at, 384), region(0, None, to, 384),
            region(0, None, at + 3 * D, 384), False, blocks[30:35],
        )
    ]
    for i in range(4):
        w_first = full_rest[:, :, :, D + i * D : 2 * D + i * D].reshape(D, D)
        w_down = full_down[i].reshape(D, D)
        act = dot_plain(low[0], w_first) + vecs[8 + i : 9 + i, :]
        square = act * act
        bent = jnp.tanh(GELU_A * (act + GELU_B * act * square))
        hidden = (0.5 * act * (1.0 + bent)).astype(BF)
        slope = 0.5 * (1.0 + bent) + 0.5 * act * (1.0 - bent * bent) * (
            GELU_A * (1.0 + 3.0 * GELU_B * square)
        )
        hidden_turned = hidden.T
        for k in range(2):
            rows = slice(k * 384, k * 384 + 384)
            g_down[i, 2 * k : 2 * k + 2] = (
                dot_plain(hidden_turned[rows], cot[...]).astype(BF).reshape(2, 192, D)
            )
        for part_ in downs:
            part_.p0_slab(i)
        grad_act = (dot_lanes(cot[...], w_down) * slope).astype(BF)
        grad_vecs[8 + i : 9 + i, :] = col_sum(grad_act.astype(F32))
        for k in range(2):
            rows = slice(k * 384, k * 384 + 384)
            g_first[2 * k : 2 * k + 2, :, :, i * D : i * D + D] = (
                dot_plain(low_turned[rows], grad_act).astype(BF).reshape(2, 4, 48, D)
            )
        firsts[i].p0()
        total_dc[...] += dot_lanes(grad_act, w_first)
        total_out[...] += dot_plain(hidden, w_down)
    outputs[...] = total_out[...].astype(BF)

    grad_c = total_dc[...]
    grad_m = grad_y + normalise_back(grad_c, unit, inverse, vecs[5:6, :])
    total_out[...] = grad_m
    low[1] = grad_m.astype(BF)
    for g in range(4):
        grad_send[g] = dot_lanes(low[1], out_rows(full_rest, g)).astype(BF)
    dob[p.u] = grad_send[p.u]
    to_u = [w.push(grad_send.at[step4(p.u, d)], dob.at[p.u], p.udev(d)) for d in (1, 3, 2)]
    for g in range(4):
        g_out[g] = dot_plain(attended[g].T, low[1])[0:192, :].astype(BF).reshape(4, 48, D)
    outs[0].p0()
    grad_vecs[0:4, :] = jnp.zeros((4, D), F32)
    grad_vecs[4:5, :] = col_sum(low[1].astype(F32))
    grad_vecs[5:6, :] = col_sum(grad_c * unit)
    grad_vecs[6:7, :] = col_sum(grad_c)
    grad_vecs[7:8, :] = col_sum(grad_y)
    grad_vecs[12:16, :] = jnp.zeros((4, D), F32)
    for part_ in firsts[:2]:
        part_.p1()
    for copy in to_u:
        copy.wait_recv()

    stages = [
        lambda: [part_.p1() for part_ in firsts[2:3]],
        lambda: [part_.p1() for part_ in firsts[3:]],
        lambda: [part_.p1() for part_ in downs],
        lambda: [part_.p2() for part_ in firsts[:2]],
        lambda: [part_.p1() for part_ in outs],
        lambda: [part_.p2() for part_ in firsts[2:]] + [part_.p3() for part_ in firsts[:2]],
    ]
    to_v_back = []
    for head in range(3):
        for tile in range(2):
            attend_back(
                kv, p, head, tile, bias, probs, grad_probs, turned, dob, lse, acc, part_send, dq
            )
            if tile == 1:
                to_v_back.append(
                    [
                        w.push(
                            part_send.at[step4(p.v, d), :, pl.ds(0, OWN), pl.ds(head * 128, 128)],
                            part_in.at[head, d - 1],
                            p.vdev(d),
                        )
                        for d in (1, 3, 2)
                    ]
                )
            stages[head * 2 + tile]()
    dq[128:192, :] = jnp.zeros((64, 512), F32)
    for k in range(4):
        back[k, :, 384:640] = dq[:, k * OWN : k * OWN + OWN].T.astype(BF)
    for head in range(3):
        for copy in to_v_back[head]:
            copy.wait_recv()
        columns = slice(head * 128, head * 128 + 128)
        for k in range(4):
            total = part_send[p.v, k, 0:OWN, columns].astype(F32)
            for d in range(3):
                total = total + part_in[head, d, k].astype(F32)
            back[k, :, columns] = total.astype(BF)

    grad_qkv = back[...].reshape(512, 640)
    for k in range(2):
        turned_rows = normed[:, :, k * 384 : k * 384 + 384].reshape(512, 384).T
        g_qkv = dot_plain(turned_rows, grad_qkv).astype(BF)
        full_rest[2 * k : 2 * k + 2, :, :, 0:640] = g_qkv.reshape(2, 4, 48, 640)

    def rows_of(u, v):
        return full_rest.at[v + p.c * (u - v), u + p.c * (v - u), :, pl.ds(0, 640)]

    one = []
    for d in (1, 3, 2):
        for k in range(4):
            one.append(w.push(rows_of(k, step4(p.v, d)), in1.at[d - 1, k], p.vdev(d)))
    grad_gain = jnp.zeros((1, D), F32)
    grad_shift = jnp.zeros((1, D), F32)
    for k in range(4):
        grad_a = dot_lanes(back[k], w_all[...].reshape(D, 640))
        unit_k, _ = normalise(x_all[k].astype(F32))
        grad_gain = grad_gain + col_sum(grad_a * unit_k)
        grad_shift = grad_shift + col_sum(grad_a)
        normed[k] = grad_a.astype(BF)
    a_one = [w.push(normed.at[step4(p.u, d)], in_a.at[d - 1], p.udev(d)) for d in (1, 3, 2)]
    sums = jnp.broadcast_to(col_sum(grad_qkv.astype(F32)), (8, 640))
    spread = (((1,), (1,)), ((), ()))
    exact = lax.Precision.HIGHEST
    bias_q = lax.dot_general(sums, pick(0, F32), spread, precision=exact, preferred_element_type=F32)
    bias_v = lax.dot_general(sums, pick(1, F32), spread, precision=exact, preferred_element_type=F32)
    grad_vecs[0:1, :] = grad_gain
    grad_vecs[1:2, :] = grad_shift
    grad_vecs[2:3, :] = bias_q[0:1, :]
    grad_vecs[3:4, :] = bias_v[0:1, :]
    vec_in[0, p.z] = grad_vecs[...]
    vec_sends = [[w.push(grad_vecs, vec_in.at[0, p.z], p.zdev(d)) for d in (1, 3, 2)]]
    for part_ in firsts[2:]:
        part_.p3()
    for part_ in downs + outs:
        part_.p2()
    for copy in one:
        copy.wait_recv()
    for k in range(4):
        total = rows_of(k, p.v)[...].astype(F32)
        for d in range(3):
            total = total + in1[d, k].astype(F32)
        part[k] = total.astype(BF)
    two = [w.push(part.at[step4(p.u, d)], in2.at[p.u], p.udev(d)) for d in (1, 3, 2)]
    in2[p.u] = part[p.u]
    for copy in vec_sends[0]:
        copy.wait_recv()
    vec_in[1, p.y] = ordered_sum(vec_in.at[0])
    vec_sends.append([w.push(vec_in.at[1, p.y], vec_in.at[1, p.y], p.ydev(d)) for d in (1, 3, 2)])
    for part_ in firsts[:2]:
        part_.p4()
    for copy in two:
        copy.wait_recv()
    three = [w.push(in2.at[pl.ds((1 - p.c) * 2, 2)], in0, p.sibling())]
    for copy in vec_sends[1]:
        copy.wait_recv()
    vec_in[2, p.x] = ordered_sum(vec_in.at[1])
    vec_sends.append([w.push(vec_in.at[2, p.x], vec_in.at[2, p.x], p.xdev(d)) for d in (1, 3, 2)])
    three[0].wait_recv()
    for k in range(2):
        held[k] = (in2[p.c * 2 + k].astype(F32) + in0[k].astype(F32)).astype(BF)
    in3[p.x] = held[...]
    four = [w.push(held, in3.at[p.x], p.xdev(d)) for d in (1, 3, 2)]
    for part_ in downs + outs:
        part_.p3()
    for part_ in firsts[2:]:
        part_.p4()
    for copy in a_one:
        copy.wait_recv()
    grad_a = normed[p.u].astype(F32)
    for d in range(3):
        grad_a = grad_a + in_a[d].astype(F32)
    unit, inverse = normalise(x[...].astype(F32))
    grad_input[...] = (total_out[...] + normalise_back(grad_a, unit, inverse, vecs[0:1, :])).astype(BF)
    for copy in vec_sends[2]:
        copy.wait_recv()
    vec_in[3, 0] = ordered_sum(vec_in.at[2])
    vec_sends.append([w.push(vec_in.at[3, 0], vec_in.at[3, 1], p.sibling())])
    for copy in four:
        copy.wait_recv()
    for k in range(2):
        total = in3[0, k].astype(F32)
        for d in range(1, 4):
            total = total + in3[d, k].astype(F32)
        packed_sum[p.c * 2 + k] = total
    here = packed_sum.at[pl.ds(p.c * 2, 2)]
    five = [w.push(here, here, p.sibling())]
    for part_ in downs + outs:
        part_.p4()
    vec_sends[3][0].wait_recv()
    o_vec[...] = vec_in[3, 0] + vec_in[3, 1]
    five[0].wait_recv()
    groups = [natural_group(packed_sum[g]) for g in range(4)]
    for k in range(3):
        o_rows[:, k * D : k * D + D] = jnp.concatenate(sum([groups[g][k] for g in range(4)], []), 1)
    for part_ in firsts + downs + outs:
        part_.end()
    rest_sends = one + a_one + two + three + four + five + sum(vec_sends, [])
    for copy in to_u + sum(to_v_back, []) + rest_sends:
        copy.wait_send()


def layer(x, cot, w_qkv, vec, lanes, rest, down, key_place, query_place):
    shapes = [
        pltpu.VMEM((4, 4, 48, 5 * D), BF),
        pltpu.VMEM((4, 4, 192, D), BF),
        pltpu.VMEM((4, 512, 640), BF),
        pltpu.VMEM((GROUP, 512), BF),
        pltpu.VMEM((GROUP, TILE), F32),
        pltpu.VMEM((GROUP, TILE), F32),
        pltpu.VMEM((3, 128, GROUP), BF),
        pltpu.VMEM((256, 512), F32),
        pltpu.VMEM((4, OWN, 256), BF),
        pltpu.VMEM((4, OWN, 256), BF),
        pltpu.VMEM((8, 512), F32),
        pltpu.VMEM((4, 4, 192, D), BF),
        pltpu.VMEM((4, 4, 48, FF), BF),
        pltpu.VMEM((4, 4, 48, D), BF),
        pltpu.VMEM((4, OWN, 256), BF),
        pltpu.VMEM((GROUP, 128), F32),
        pltpu.VMEM((3, 3, 4, OWN, 128), BF),
        pltpu.VMEM((OWN, D), F32),
        pltpu.VMEM((OWN, D), F32),
        pltpu.VMEM((2, OWN, D), BF),
        pltpu.VMEM((4, OWN, D), BF),
        pltpu.VMEM((16, 48, 640), BF),
        pltpu.VMEM((4, OWN, D), BF),
        pltpu.VMEM((4, 16, D), BF),
        pltpu.VMEM((4, 16, D), BF),
        pltpu.VMEM((16, D), F32),
        pltpu.VMEM((16, D), F32),
        pltpu.VMEM((4, 4, 16, D), F32),
        pltpu.VMEM((4, OWN, 640), BF),
        pltpu.VMEM((3, OWN, D), BF),
        pltpu.VMEM((3, 4, 48, 640), BF),
        pltpu.VMEM((4, 48, 640), BF),
        pltpu.VMEM((4, 48, 640), BF),
        pltpu.VMEM((2, 48, 640), BF),
        pltpu.VMEM((2, 48, 640), BF),
        pltpu.VMEM((4, 2, 48, 640), BF),
        pltpu.VMEM((4, 48, 640), F32),
    ]
    for rows in (48, 48, 48, 48, 96, 96, 48):
        shapes += scatter_shapes(rows, 384, BF)
    return pl.pallas_call(
        layer_kernel,
        out_shape=(
            jax.ShapeDtypeStruct((OWN, D), BF),
            jax.ShapeDtypeStruct((OWN, D), BF),
            jax.ShapeDtypeStruct((48, 8 * D), F32),
            jax.ShapeDtypeStruct((192, D), F32),
            jax.ShapeDtypeStruct((16, D), F32),
        ),
        in_specs=[VMEM] * 7 + [ANY, VMEM],
        out_specs=(VMEM,) * 5,
        scratch_shapes=shapes + sems(4 * GATHER_SENDS + 7 * SCATTER_SENDS + 80, 5),
        compiler_params=pltpu.CompilerParams(
            collective_id=1, has_side_effects=True, vmem_limit_bytes=62 * MIB
        ),
        name="layer",
    )(x, cot, w_qkv, vec, lanes, rest, down, key_place, query_place)


def adamw(weight, moment, second, grad, rate, decay):
    moment_new = BETA_ONE * moment + (1.0 - BETA_ONE) * grad
    second_new = BETA_TWO * second + (1.0 - BETA_TWO) * grad * grad
    moment_hat = moment_new / (1.0 - BETA_ONE**STEP)
    second_hat = second_new / (1.0 - BETA_TWO**STEP)
    weight_new = weight - rate * (moment_hat / (jnp.sqrt(second_hat) + EPS_ADAM) + decay * weight)
    return (weight_new, moment_new, second_new)


def pack_groups(queries, keys, values):
    blank = jnp.zeros((queries.shape[0], HD), queries.dtype)
    groups = []
    for g in range(4):
        q, k, v = ([a[:, (3 * g + j) * HD : (3 * g + j + 1) * HD] for j in range(3)] for a in (queries, keys, values))
        groups.append(jnp.concatenate([v[0], k[0], k[1], v[1], v[2], k[2], q[1], q[0], blank, q[2]], 1))
    return jnp.stack(groups)


def per_device(
    tokens,
    cotangent,
    lengths,
    positions,
    w_rows,
    w_down,
    vectors,
    moment_rows,
    second_rows,
    moment_down,
    second_down,
    moment_vectors,
    second_vectors,
):
    shard_index = lax.axis_index("shard")
    core = lax.rem(lax.axis_index("replica"), 2)
    z, y = lax.div(shard_index, 4), lax.rem(shard_index, 4)
    own_v = jnp.where(core == 0, z, y)
    low_rows = w_rows.astype(BF)
    low_qkv = pack_groups(low_rows[:, :D], low_rows[:, D : 2 * D], low_rows[:, 2 * D : 3 * D])
    own_vecs = lax.dynamic_update_slice(
        jnp.zeros((16, D), BF), vectors.astype(BF), (0, shard_index * 48)
    )
    place_blocks = positions.reshape(4, 4, OWN)
    place_all = jnp.where(core == 0, place_blocks, place_blocks.transpose(1, 0, 2)).reshape(GROUP)
    seq_ends = jnp.cumsum(lengths[0])
    place_quarter = lax.dynamic_slice_in_dim(place_all, own_v * 512, 512)
    seq_start = jnp.max(
        jnp.where(place_quarter[None, :] >= seq_ends[:, None], seq_ends[:, None], 0), axis=0
    )
    key_place = jnp.broadcast_to(place_all.astype(F32)[:, None], (GROUP, 128))
    query_place = jnp.pad(jnp.stack([place_quarter, seq_start]).astype(F32), ((0, 6), (0, 0)))

    column = jnp.arange(640)
    block, within = column // HD, column % HD
    lanes = jnp.full((8, 640), -GROUP, jnp.int32)
    for row, places in ((0, ((7, 0), (6, 1), (9, 2))), (1, ((0, 0), (3, 1), (4, 2)))):
        for at, head in places:
            lanes = lanes.at[row].set(jnp.where(block == at, within + head * HD, lanes[row]))
    outputs, grad_input, grad_rows, grad_down, grad_vecs = layer(
        tokens, cotangent, low_qkv, own_vecs, lanes, low_rows[:, 3 * D :], w_down.astype(BF), key_place, query_place
    )
    own_grads = lax.dynamic_slice(grad_vecs, (0, shard_index * 48), (12, 48))
    rows_new = adamw(w_rows, moment_rows, second_rows, grad_rows, LR_MATRIX, DECAY)
    down_new = adamw(w_down, moment_down, second_down, grad_down, LR_MATRIX, DECAY)
    vec_new = adamw(vectors, moment_vectors, second_vectors, own_grads, LR_VECTOR, 0.0)
    return (
        outputs,
        grad_input,
        rows_new[0],
        rows_new[1],
        rows_new[2],
        down_new[0],
        down_new[1],
        down_new[2],
        vec_new[0],
        vec_new[1],
        vec_new[2],
    )


def solution(mesh):
    return jax.shard_map(
        per_device,
        mesh=mesh,
        in_specs=(
            P(("replica", "shard"), None),
            P(("replica", "shard"), None),
            P("replica", None),
            P("replica", None),
            P("shard", None),
            P("shard", None),
            P(None, "shard"),
            P("shard", None),
            P("shard", None),
            P("shard", None),
            P("shard", None),
            P(None, "shard"),
            P(None, "shard"),
        ),
        out_specs=(
            P(("replica", "shard"), None),
            P(("replica", "shard"), None),
            P("shard", None),
            P("shard", None),
            P("shard", None),
            P("shard", None),
            P("shard", None),
            P("shard", None),
            P(None, "shard"),
            P(None, "shard"),
            P(None, "shard"),
        ),
        check_vma=False,
    )
```

```python
import functools

import jax
import jax.numpy as jnp
from jax import lax
from jax.experimental import pallas as pl
from jax.experimental.pallas import tpu as pltpu
from jax.sharding import PartitionSpec as P

H = 12
HD = 64
STEP = 10
D = 768
FF = 3072
OWN = 128
GROUP = 2048
NEIGHBOURS = 4
TILE = 256
CHUNK = 256
STEPS = GROUP // CHUNK
MIB = 1 << 20

EPS_NORM = 1e-05
BETA_ONE = 0.9
BETA_TWO = 0.95
EPS_ADAM = 1e-08
LR_MATRIX = 0.02
LR_VECTOR = 0.3
DECAY = 0.1
HUGE_NEG = -1e30

BF = jnp.bfloat16
F32 = jnp.float32
MESH = pl.DeviceIdType.MESH
VMEM = pl.BlockSpec(memory_space=pltpu.VMEM)
ANY = pl.BlockSpec(memory_space=pl.ANY)


def step4(i, d):
    return lax.rem(i + d, 4)


class Place:
    def __init__(self):
        self.r = lax.axis_index("replica")
        self.s = lax.axis_index("shard")
        self.x = lax.div(self.r, 2)
        self.c = lax.rem(self.r, 2)
        self.z = lax.div(self.s, 4)
        self.y = lax.rem(self.s, 4)
        self.u = self.y + self.c * (self.z - self.y)
        self.v = self.z + self.c * (self.y - self.z)
        self.u_step = 1 + 3 * self.c
        self.v_step = 4 - 3 * self.c

    def ydev(self, d):
        return (self.r, self.z * 4 + step4(self.y, d))

    def zdev(self, d):
        return (self.r, step4(self.z, d) * 4 + self.y)

    def xdev(self, d):
        return (step4(self.x, d) * 2 + self.c, self.s)

    def udev(self, d):
        return (self.r, step4(self.u, d) * self.u_step + self.v * self.v_step)

    def vdev(self, d):
        return (self.r, self.u * self.u_step + step4(self.v, d) * self.v_step)

    def sibling(self):
        return (self.x * 2 + 1 - self.c, self.s)


def greet(devices):
    barrier = pltpu.get_barrier_semaphore()
    for device in devices:
        pl.semaphore_signal(barrier, inc=1, device_id=device, device_id_type=MESH)
    pl.semaphore_wait(barrier, len(devices))


class Wire:
    def __init__(self, send_sems, recv_sems, local_sems):
        self.send_sems, self.recv_sems, self.local_sems = send_sems, recv_sems, local_sems
        self.sent, self.moved = 0, 0

    def push(self, src, dst, device):
        k = self.sent
        self.sent += 1
        copy = pltpu.make_async_remote_copy(
            src_ref=src,
            dst_ref=dst,
            send_sem=self.send_sems.at[k],
            recv_sem=self.recv_sems.at[k],
            device_id=device,
            device_id_type=MESH,
        )
        copy.start()
        return copy

    def local(self, src, dst):
        k = self.moved
        self.moved += 1
        copy = pltpu.make_async_copy(src, dst, self.local_sems.at[k])
        copy.start()
        return copy


def sems(remote, local):
    return [
        pltpu.SemaphoreType.DMA((remote,)),
        pltpu.SemaphoreType.DMA((remote,)),
        pltpu.SemaphoreType.DMA((max(local, 1),)),
    ]


def region(row, rows, col, cols):
    row_cut = slice(None) if rows is None else pl.ds(row, rows)
    col_cut = slice(None) if cols is None else pl.ds(pl.multiple_of(col, 128), cols)
    return (row_cut, col_cut)


class Gather:
    def __init__(self, wire, place, shard, full, cut, y_first):
        self.wire, self.place, self.shard, self.full, self.cut = wire, place, shard, full, cut
        self.y_first = y_first
        self.near = place.ydev if y_first else place.zdev
        self.far = place.zdev if y_first else place.ydev
        self.sends = []

    def push(self, src, dst, device):
        copy = self.wire.push(src, dst, device)
        self.sends.append(copy)
        return copy

    def slab(self, d, blocks=slice(None)):
        p = self.place
        if self.y_first:
            return self.full.at[(step4(p.z, 4 - d), blocks) + self.cut]
        return self.full.at[(blocks, step4(p.y, 4 - d)) + self.cut]

    def first(self):
        p = self.place
        src = self.shard.at[self.cut]
        dst = self.full.at[(p.z, p.y) + self.cut]
        self.own = self.wire.local(src, dst)
        self.one = [self.push(src, dst, self.near(d)) for d in (1, 3, 2)]

    def second(self):
        self.own.wait()
        for copy in self.one:
            copy.wait_recv()
        slab = self.slab(0)
        self.two = [self.push(slab, slab, self.far(d)) for d in (1, 3)]
        self.across = [self.push(slab, slab, self.place.sibling())]

    def third(self):
        self.two[0].wait_recv()
        half = self.slab(1, pl.ds(0, 2))
        self.three = [self.push(half, half, self.far(1))]
        self.two[1].wait_recv()
        half = self.slab(3, pl.ds(2, 2))
        self.three.append(self.push(half, half, self.far(3)))
        for d in (1, 3):
            slab = self.slab(d)
            self.across.append(self.push(slab, slab, self.place.sibling()))

    def fourth(self):
        for copy in self.three:
            copy.wait_recv()
        slab = self.slab(2)
        self.across.append(self.push(slab, slab, self.place.sibling()))

    def end(self):
        for copy in self.across:
            copy.wait_recv()
        for copy in self.sends:
            copy.wait_send()


GATHER_SENDS = 11


def scatter_shapes(rows, cols, dtype):
    return [
        pltpu.VMEM((4, 4, rows, cols), dtype),
        pltpu.VMEM((3, 4, rows, cols), dtype),
        pltpu.VMEM((4, rows, cols), dtype),
        pltpu.VMEM((3, rows, cols), dtype),
        pltpu.VMEM((4, rows, cols), dtype),
    ]


class Scatter:
    def __init__(self, wire, place, grad, out, mine, other, to, z_first, scratch):
        self.wire, self.place, self.grad, self.out = wire, place, grad, out
        self.z_first = z_first
        self.mine, self.other, self.to = mine, other, to
        self.in0, self.in1, self.part, self.in2, self.in3 = scratch
        self.sends, self.wait = [], []

    def push(self, src, dst, device):
        copy = self.wire.push(src, dst, device)
        self.sends.append(copy)
        return copy

    def p0(self):
        every = (slice(None), slice(None))
        self.wait.append(self.push(self.grad.at[every + self.other], self.in0, self.place.sibling()))

    def p0_slab(self, i):
        here = self.grad.at[(i, slice(None)) + self.other]
        self.wait.append(self.push(here, self.in0.at[i], self.place.sibling()))

    def p1(self):
        p = self.place
        for copy in self.wait:
            copy.wait_recv()

        def add(i, carry):
            at = (lax.div(i, 4), lax.rem(i, 4))
            both = self.grad[at + self.mine].astype(F32) + self.in0[at].astype(F32)
            self.grad[at + self.mine] = both.astype(self.grad.dtype)
            return carry

        lax.fori_loop(0, 16, add, 0)
        self.wait = []
        for d in (1, 3, 2):
            if self.z_first:
                src, device = self.grad.at[(step4(p.z, d), slice(None)) + self.mine], p.zdev(d)
            else:
                src, device = self.grad.at[(slice(None), step4(p.y, d)) + self.mine], p.ydev(d)
            self.wait.append(self.push(src, self.in1.at[d - 1], device))

    def p2(self):
        p = self.place
        for copy in self.wait:
            copy.wait_recv()

        def add(i, carry):
            at = (p.z, i) if self.z_first else (i, p.y)
            total = self.grad[at + self.mine].astype(F32)
            for k in range(3):
                total = total + self.in1[k, i].astype(F32)
            self.part[i] = total.astype(self.part.dtype)
            return carry

        lax.fori_loop(0, 4, add, 0)
        self.wait = []
        for d in (1, 3, 2):
            if self.z_first:
                src, device = self.part.at[step4(p.y, d)], p.ydev(d)
            else:
                src, device = self.part.at[step4(p.z, d)], p.zdev(d)
            self.wait.append(self.push(src, self.in2.at[d - 1], device))

    def p3(self):
        p = self.place
        for copy in self.wait:
            copy.wait_recv()
        total = self.part[p.y if self.z_first else p.z].astype(F32)
        for k in range(3):
            total = total + self.in2[k].astype(F32)
        self.in3[p.x] = total.astype(self.in3.dtype)
        self.wait = [self.push(self.in3.at[p.x], self.in3.at[p.x], p.xdev(d)) for d in (1, 3, 2)]

    def p4(self):
        for copy in self.wait:
            copy.wait_recv()
        total = self.in3[0].astype(F32)
        for k in range(1, 4):
            total = total + self.in3[k].astype(F32)
        self.out[self.to] = total
        here = self.out.at[self.to]
        self.wait = [self.push(here, here, self.place.sibling())]

    def end(self):
        for copy in self.wait:
            copy.wait_recv()
        for copy in self.sends:
            copy.wait_send()


SCATTER_SENDS = 14


class GatherWide(Gather):
    def __init__(self, wire, place, shard, full, rows, cols):
        piece = (pl.ds(pl.multiple_of(place.x * rows, 16), rows), cols)
        super().__init__(wire, place, shard, full, piece, True)
        self.rows, self.cols = rows, cols
        self.along_x = {}

    def hand_on(self, d):
        slab = self.slab(d)
        self.along_x[d] = [self.push(slab, slab, self.place.xdev(e)) for e in (1, 3, 2)]

    def second(self):
        self.own.wait()
        for copy in self.one:
            copy.wait_recv()
        slab = self.slab(0)
        self.two = [self.push(slab, slab, self.far(d)) for d in (1, 3)]
        self.hand_on(0)

    def third(self):
        self.two[0].wait_recv()
        half = self.slab(1, pl.ds(0, 2))
        self.three = [self.push(half, half, self.far(1))]
        self.two[1].wait_recv()
        half = self.slab(3, pl.ds(2, 2))
        self.three.append(self.push(half, half, self.far(3)))
        self.hand_on(1)
        self.hand_on(3)

    def fourth(self):
        for copy in self.three:
            copy.wait_recv()
        self.hand_on(2)

    def fifth(self, order):
        self.across = []
        for d in order:
            for copy in self.along_x[d]:
                copy.wait_recv()
            slab = self.full.at[step4(self.place.z, 4 - d), :, :, self.cols]
            self.across.append(self.push(slab, slab, self.place.sibling()))


GATHER_WIDE_SENDS = 3 + 2 + 2 + 12 + 4


def scatter_wide_shapes(rows, cols, dtype):
    return [
        pltpu.VMEM((4, 4, 4 * rows, cols), dtype),
        pltpu.VMEM((3, 4, 4, rows, cols), dtype),
        pltpu.VMEM((3, 4, rows, cols), dtype),
        pltpu.VMEM((4, rows, cols), dtype),
        pltpu.VMEM((3, rows, cols), dtype),
    ]


class ScatterWide:
    def __init__(self, wire, place, grad, out, rows, mine, other, scratch):
        self.wire, self.place, self.grad, self.out, self.rows = wire, place, grad, out, rows
        self.mine, self.other = mine, other
        self.in0, self.in_x, self.in1, self.part, self.in2 = scratch
        self.sends, self.wait = [], []
        self.piece = self.quarter(place.x)

    def quarter(self, x):
        return (pl.ds(pl.multiple_of(x * self.rows, 16), self.rows), self.mine)

    def push(self, src, dst, device):
        copy = self.wire.push(src, dst, device)
        self.sends.append(copy)
        return copy

    def arrive(self):
        for copy in self.wait:
            copy.wait_recv()
        self.wait = []

    def p0_slab(self, i):
        here = self.grad.at[i, :, :, self.other]
        self.wait.append(self.push(here, self.in0.at[i], self.place.sibling()))

    def p1(self):
        p = self.place
        self.arrive()

        def add(i, carry):
            at = (lax.div(i, 4), lax.rem(i, 4))
            here = at + (slice(None), self.mine)
            both = self.grad[here].astype(F32) + self.in0[at].astype(F32)
            self.grad[here] = both.astype(self.grad.dtype)
            return carry

        lax.fori_loop(0, 16, add, 0)
        for d in (1, 3, 2):
            src = self.grad.at[(slice(None), slice(None)) + self.quarter(step4(p.x, d))]
            self.wait.append(self.push(src, self.in_x.at[d - 1], p.xdev(d)))

    def p2(self):
        p = self.place
        self.arrive()

        def add(i, carry):
            at = (lax.div(i, 4), lax.rem(i, 4))
            total = self.grad[at + self.piece].astype(F32)
            for k in range(3):
                total = total + self.in_x[(k,) + at].astype(F32)
            self.grad[at + self.piece] = total.astype(self.grad.dtype)
            return carry

        lax.fori_loop(0, 16, add, 0)
        for d in (1, 3, 2):
            src = self.grad.at[(step4(p.z, d), slice(None)) + self.piece]
            self.wait.append(self.push(src, self.in1.at[d - 1], p.zdev(d)))

    def p3(self):
        p = self.place
        self.arrive()
        for i in range(4):
            total = self.grad[(p.z, i) + self.piece].astype(F32)
            for k in range(3):
                total = total + self.in1[k, i].astype(F32)
            self.part[i] = total.astype(self.part.dtype)
        for d in (1, 3, 2):
            self.wait.append(self.push(self.part.at[step4(p.y, d)], self.in2.at[d - 1], p.ydev(d)))

    def p4(self):
        p = self.place
        self.arrive()
        total = self.part[p.y].astype(F32)
        for k in range(3):
            total = total + self.in2[k].astype(F32)
        self.out[self.piece] = total
        here = self.out.at[self.piece]
        self.wait = [self.push(here, here, p.xdev(d)) for d in (1, 3, 2)]

    def p5(self):
        self.arrive()
        here = self.out.at[:, self.mine]
        self.wait = [self.push(here, here, self.place.sibling())]

    def end(self):
        self.arrive()
        for copy in self.sends:
            copy.wait_send()


SCATTER_WIDE_SENDS = 4 + 3 + 3 + 3 + 3 + 1


def all_peers(p):
    rings = [p.ydev(d) for d in (1, 2, 3)] + [p.zdev(d) for d in (1, 2, 3)]
    return rings + [p.sibling()]


def x_peers(p):
    return [p.xdev(d) for d in (1, 2, 3)]


def owner(p, u, v):
    return v * p.v_step + u * p.u_step


def half_lanes(value, right):
    lane = lax.broadcasted_iota(jnp.int32, value.shape, 1)
    keep = lane >= HD if right else lane < HD
    return jnp.where(keep, value, jnp.zeros_like(value))


def rows_max(value):
    return jnp.max(value.reshape(-1, 8, value.shape[1]), axis=0)


def rows_sum(value):
    return jnp.sum(value.reshape(-1, 8, value.shape[1]), axis=0)


def dot_lanes(left, right):
    return lax.dot_general(left, right, (((1,), (1,)), ((), ())), preferred_element_type=F32)


def dot_plain(left, right):
    return jnp.dot(left, right, preferred_element_type=F32)


def fill_bias(key_place, query_place, bias):
    def body(i, carry):
        rows = pl.ds(pl.multiple_of(i * CHUNK, CHUNK), CHUNK)
        keys = key_place[rows, 0:128]
        for k in range(4):
            cols = slice(k * 128, k * 128 + 128)
            ok = (keys <= query_place[0:1, cols]) & (keys >= query_place[1:2, cols])
            bias[rows, cols] = jnp.where(ok, 0.0, HUGE_NEG).astype(BF)
        return carry

    lax.fori_loop(0, STEPS, body, 0, unroll=True)


def key_chunk(kv, i, head):
    a, b = lax.div(i, 2), lax.rem(i, 2) * CHUNK
    return kv[a, pl.ds(pl.multiple_of(b, CHUNK), CHUNK), head * 128 : head * 128 + 128]


def chunk_rows(i):
    return pl.ds(pl.multiple_of(i * CHUNK, CHUNK), CHUNK)


def turn_keys(kv, head, turned):
    def body(i, carry):
        turned[head, :, chunk_rows(i)] = key_chunk(kv, i, head).T
        return carry

    lax.fori_loop(0, STEPS, body, 0, unroll=True)


def query_tile(kv, p, head, tile):
    block = 384 + head // 2 * 128
    return half_lanes(kv[p.v, tile * TILE : tile * TILE + TILE, block : block + 128], head != 1)


def attend(kv, p, head, tile, bias, scores, turned, head_out, lse):
    cols = slice(tile * TILE, tile * TILE + TILE)
    query = query_tile(kv, p, head, tile)

    def score(i, top):
        part = dot_lanes(key_chunk(kv, i, head), query) + bias[chunk_rows(i), cols].astype(F32)
        scores[chunk_rows(i), :] = part
        return jnp.maximum(top, rows_max(part))

    top = lax.fori_loop(0, STEPS, score, jnp.full((8, TILE), -jnp.inf, F32), unroll=True)
    top = jnp.max(top, axis=0, keepdims=True)

    def mix(i, carry):
        total, acc = carry
        raised = jnp.exp(scores[chunk_rows(i), :] - top)
        acc = acc + dot_plain(turned[head, :, chunk_rows(i)], raised.astype(BF))
        return total + rows_sum(raised), acc

    total, acc = lax.fori_loop(
        0, STEPS, mix, (jnp.zeros((8, TILE), F32), jnp.zeros((128, TILE), F32)), unroll=True
    )
    total = jnp.sum(total, axis=0, keepdims=True)
    acc = acc / total
    at = 64 if head == 1 else 0
    head_out[head * 64 : head * 64 + 64, cols] = acc[at : at + 64, :]
    lse[head : head + 1, cols] = top + jnp.log(total)


def attend_back(kv, p, head, tile, bias, probs, grad_probs, turned, dob, lse, acc, part_send, dq):
    cols = slice(tile * TILE, tile * TILE + TILE)
    query = query_tile(kv, p, head, tile)
    block = head // 2 * 128
    dout = dob[2 * tile : 2 * tile + 2, :, block : block + 128]
    dout = half_lanes(dout.reshape(TILE, 128), head == 1)
    total = lse[head : head + 1, cols]

    def weigh(i, inner):
        keys = key_chunk(kv, i, head)
        prob = jnp.exp(dot_lanes(keys, query) + bias[chunk_rows(i), cols].astype(F32) - total)
        gprob = dot_lanes(keys, dout)
        probs[chunk_rows(i), :] = prob
        grad_probs[chunk_rows(i), :] = gprob
        return inner + rows_sum(prob * gprob)

    inner = lax.fori_loop(0, STEPS, weigh, jnp.zeros((8, TILE), F32), unroll=True)
    inner = jnp.sum(inner, axis=0, keepdims=True)

    def back(i, total_dq):
        prob = probs[chunk_rows(i), :]
        gscore = (prob * (grad_probs[chunk_rows(i), :] - inner)).astype(BF)
        both = dot_plain(gscore, query) + dot_plain(prob.astype(BF), dout)
        if tile == 0:
            acc[chunk_rows(i), :] = both
        else:
            total_kv = (acc[chunk_rows(i), :] + both).astype(BF)
            lanes = slice(head * 128, head * 128 + 128)
            part_send[lax.div(i, 2), pl.ds(lax.rem(i, 2) * 2, 2), 0:OWN, lanes] = total_kv.reshape(2, OWN, 128)
        return total_dq + dot_plain(turned[head, :, chunk_rows(i)], gscore)

    total_dq = lax.fori_loop(0, STEPS, back, jnp.zeros((128, TILE), F32), unroll=True)
    total_dq = total_dq * (HD ** (-0.5))
    at = 0 if head == 1 else 64
    row = (64, 0, 192)[head]
    dq[row : row + 64, cols] = total_dq[at : at + 64, :]


def col_sum(value):
    return jnp.sum(value, axis=0, keepdims=True)


def normalise(value):
    average = jnp.mean(value, -1, keepdims=True)
    centred = value - average
    spread = jnp.mean(centred * centred, -1, keepdims=True)
    inverse = lax.rsqrt(spread + EPS_NORM)
    return centred * inverse, inverse


def normalise_back(grad, unit, inverse, gain):
    g = grad * gain
    return inverse * (
        g - jnp.mean(g, -1, keepdims=True) - unit * jnp.mean(g * unit, -1, keepdims=True)
    )


GELU_A = 0.7978845608028654
GELU_B = 0.044715


def out_rows(full_rest, g):
    own = full_rest[g, :, :, 0:D].reshape(192, D)
    return jnp.concatenate([own, jnp.zeros((64, D), BF)], 0)


def ordered_sum(blocks):
    total = blocks[0].astype(F32)
    for k in range(1, blocks.shape[0]):
        total = total + blocks[k].astype(F32)
    return total


def natural_group(packed):
    col = [packed[:, j * HD : (j + 1) * HD] for j in range(10)]
    return [[col[j] for j in order] for order in ((7, 6, 9), (1, 2, 5), (0, 3, 4))]


def layer_kernel(
    x, cot, w_qkv, vec, lanes, rest, down, key_place, query_place,
    outputs, grad_input, o_rows, o_down, o_vec, *scratch,
):
    (
        full_rest, full_down, kv, bias, probs, grad_probs, turned, head_out, out_send, attended, lse,
        g_down, g_first, g_out, dob, acc, part_in, total_out, total_dc, low,
        x_all, w_all, normed, vec_y, vec_z, vecs, grad_vecs, vec_in, back, in_a, in1, part, in2, in0, held, in3, packed_sum,
    ) = scratch[:37]
    part_send, grad_send, dq = full_down, out_send, head_out
    blocks = scratch[37:-3]
    p = Place()
    w = Wire(*scratch[-3:])
    greet(all_peers(p) + x_peers(p))

    places = w.local(key_place, grad_probs.at[:, pl.ds(0, 128)])
    w_one = [(d, w.push(w_qkv.at[step4(p.u, d)], w_all.at[p.s], p.udev(d))) for d in (1, 3, 2)]
    vec_one = [w.push(vec, vec_y.at[p.y], p.ydev(d)) for d in (1, 3, 2)]
    w_all[p.s] = w_qkv[p.u]
    vec_y[p.y] = vec[...]
    w_two = [w.push(w_all.at[p.s], w_all.at[p.s], p.vdev(e)) for e in (1, 3, 2)]
    x_one = [w.push(x, x_all.at[p.u], p.udev(d)) for d in (1, 3, 2)]
    x_all[p.u] = x[...]
    for d, copy in w_one:
        copy.wait_recv()
        block = w_all.at[owner(p, step4(p.u, 4 - d), p.v)]
        w_two += [w.push(block, block, p.vdev(e)) for e in (1, 3, 2)]
    for copy in vec_one:
        copy.wait_recv()
    vec_z[p.z] = ordered_sum(vec_y).astype(BF)
    vec_two = [w.push(vec_z.at[p.z], vec_z.at[p.z], p.zdev(d)) for d in (1, 3, 2)]
    half = p.c * 1920
    parts = [
        Gather(w, p, rest, full_rest, region(0, None, half, 1024), True),
        Gather(w, p, rest, full_rest, region(0, None, half + 1024, 896), False),
        GatherWide(w, p, down, full_down, 48, pl.ds(pl.multiple_of(p.c * 384, 128), 384)),
    ]
    for part_ in parts:
        part_.first()
    places.wait()
    fill_bias(grad_probs, query_place, bias)
    for copy in x_one + vec_two:
        copy.wait_recv()
    vecs[...] = ordered_sum(vec_z)
    low_vecs = vecs[...].astype(BF)

    def pick(row, dtype):
        column = lax.broadcasted_iota(jnp.int32, (D, 640), 0) - 192 * p.u
        return (column == lanes[row : row + 1, :]).astype(dtype)

    bias_own = dot_plain(low_vecs, pick(0, BF))[2:3, :] + dot_plain(low_vecs, pick(1, BF))[3:4, :]
    scale = jnp.where(lax.broadcasted_iota(jnp.int32, (1, 640), 1) < 384, 1.0, HD ** (-0.5)).astype(F32)
    for k in range(4):
        unit, _ = normalise(x_all[k].astype(F32))
        normed[k] = (unit * vecs[0:1, :] + vecs[1:2, :]).astype(BF)
    for part_ in parts:
        part_.second()
    for copy in w_two:
        copy.wait_recv()
    for k in range(4):
        projected = dot_plain(normed[k], w_all[...].reshape(D, 640)) + bias_own
        kv[p.v, k * OWN : k * OWN + OWN, :] = (projected.astype(BF).astype(F32) * scale).astype(BF)
    mine = kv.at[p.v, :, pl.ds(0, 384)]
    to_v = [w.push(mine, mine, p.vdev(d)) for d in (1, 3, 2)]
    parts[2].third()
    for copy in to_v:
        copy.wait_recv()
    head_out[192:256, :] = jnp.zeros((64, 512), F32)
    for head in range(3):
        turn_keys(kv, head, turned)
        for tile in range(2):
            attend(kv, p, head, tile, bias, probs, turned, head_out, lse)
        if head == 0:
            for part_ in parts[:2]:
                part_.third()
            parts[2].fourth()
    for k in range(4):
        out_send[k] = head_out[:, k * OWN : k * OWN + OWN].T.astype(BF)
    attended[p.u] = out_send[p.u]
    out_back = [w.push(out_send.at[step4(p.u, d)], attended.at[p.u], p.udev(d)) for d in (1, 3, 2)]
    for part_ in parts[:2]:
        part_.fourth()
    parts[2].fifth((0, 1, 3, 2))
    for copy in out_back:
        copy.wait_recv()
    for part_ in parts:
        part_.end()
    for copy in to_v + out_back + x_one + w_two + vec_one + vec_two + [c for _, c in w_one]:
        copy.wait_send()

    grad_y = cot[...].astype(F32)
    middle = x[...].astype(F32) + vecs[4:5, :]
    for g in range(4):
        middle = middle + dot_plain(attended[g], out_rows(full_rest, g))
    unit, inverse = normalise(middle)
    low[0] = (unit * vecs[5:6, :] + vecs[6:7, :]).astype(BF)
    total_out[...] = middle + vecs[7:8, :]
    total_dc[...] = jnp.zeros((OWN, D), F32)
    low_turned = low[0].T

    def first_part(i):
        at = i * D + p.c * 384
        to = i * D + (1 - p.c) * 384
        return Scatter(
            w, p, g_first, o_rows, region(0, None, at, 384), region(0, None, to, 384),
            region(0, None, at + 4 * D, 384), i % 2 == 0, blocks[5 * i : 5 * i + 5],
        )

    firsts = [first_part(i) for i in range(4)]
    at, to = p.c * 384, (1 - p.c) * 384
    downs = [
        ScatterWide(
            w, p, g_down, o_down, 48, pl.ds(pl.multiple_of(at, 128), 384),
            pl.ds(pl.multiple_of(to, 128), 384), blocks[20:25],
        )
    ]
    outs = [
        Scatter(
            w, p, g_out, o_rows, region(0, None, at, 384), region(0, None, to, 384),
            region(0, None, at + 3 * D, 384), False, blocks[25:30],
        )
    ]
    for i in range(4):
        w_first = full_rest[:, :, :, D + i * D : 2 * D + i * D].reshape(D, D)
        w_down = full_down[i].reshape(D, D)
        act = dot_plain(low[0], w_first) + vecs[8 + i : 9 + i, :]
        square = act * act
        bent = jnp.tanh(GELU_A * (act + GELU_B * act * square))
        hidden = (0.5 * act * (1.0 + bent)).astype(BF)
        slope = 0.5 * (1.0 + bent) + 0.5 * act * (1.0 - bent * bent) * (
            GELU_A * (1.0 + 3.0 * GELU_B * square)
        )
        hidden_turned = hidden.T
        for k in range(2):
            rows = slice(k * 384, k * 384 + 384)
            g_down[i, 2 * k : 2 * k + 2] = (
                dot_plain(hidden_turned[rows], cot[...]).astype(BF).reshape(2, 192, D)
            )
        for part_ in downs:
            part_.p0_slab(i)
        grad_act = (dot_lanes(cot[...], w_down) * slope).astype(BF)
        grad_vecs[8 + i : 9 + i, :] = col_sum(grad_act.astype(F32))
        for k in range(2):
            rows = slice(k * 384, k * 384 + 384)
            g_first[2 * k : 2 * k + 2, :, :, i * D : i * D + D] = (
                dot_plain(low_turned[rows], grad_act).astype(BF).reshape(2, 4, 48, D)
            )
        firsts[i].p0()
        total_dc[...] += dot_lanes(grad_act, w_first)
        total_out[...] += dot_plain(hidden, w_down)
    outputs[...] = total_out[...].astype(BF)

    grad_c = total_dc[...]
    grad_m = grad_y + normalise_back(grad_c, unit, inverse, vecs[5:6, :])
    total_out[...] = grad_m
    low[1] = grad_m.astype(BF)
    for g in range(4):
        grad_send[g] = dot_lanes(low[1], out_rows(full_rest, g)).astype(BF)
    dob[p.u] = grad_send[p.u]
    to_u = [w.push(grad_send.at[step4(p.u, d)], dob.at[p.u], p.udev(d)) for d in (1, 3, 2)]
    for g in range(4):
        g_out[g] = dot_plain(attended[g].T, low[1])[0:192, :].astype(BF).reshape(4, 48, D)
    outs[0].p0()
    grad_vecs[0:4, :] = jnp.zeros((4, D), F32)
    grad_vecs[4:5, :] = col_sum(low[1].astype(F32))
    grad_vecs[5:6, :] = col_sum(grad_c * unit)
    grad_vecs[6:7, :] = col_sum(grad_c)
    grad_vecs[7:8, :] = col_sum(grad_y)
    grad_vecs[12:16, :] = jnp.zeros((4, D), F32)
    for part_ in firsts[:2]:
        part_.p1()
    for copy in to_u:
        copy.wait_recv()

    stages = [
        lambda: [part_.p1() for part_ in firsts[2:3]],
        lambda: [part_.p1() for part_ in firsts[3:]],
        lambda: [part_.p1() for part_ in downs],
        lambda: [part_.p1() for part_ in outs],
        lambda: [part_.p2() for part_ in firsts[:2]],
        lambda: [part_.p2() for part_ in firsts[2:]],
    ]
    to_v_back = []
    for head in range(3):
        for tile in range(2):
            attend_back(
                kv, p, head, tile, bias, probs, grad_probs, turned, dob, lse, acc, part_send, dq
            )
            if tile == 1:
                to_v_back.append(
                    [
                        w.push(
                            part_send.at[step4(p.v, d), :, pl.ds(0, OWN), pl.ds(head * 128, 128)],
                            part_in.at[head, d - 1],
                            p.vdev(d),
                        )
                        for d in (1, 3, 2)
                    ]
                )
            stages[head * 2 + tile]()
    dq[128:192, :] = jnp.zeros((64, 512), F32)
    for k in range(4):
        back[k, :, 384:640] = dq[:, k * OWN : k * OWN + OWN].T.astype(BF)
    for head in range(3):
        for copy in to_v_back[head]:
            copy.wait_recv()
        columns = slice(head * 128, head * 128 + 128)
        for k in range(4):
            total = part_send[p.v, k, 0:OWN, columns].astype(F32)
            for d in range(3):
                total = total + part_in[head, d, k].astype(F32)
            back[k, :, columns] = total.astype(BF)

    grad_qkv = back[...].reshape(512, 640)
    for k in range(2):
        turned_rows = normed[:, :, k * 384 : k * 384 + 384].reshape(512, 384).T
        g_qkv = dot_plain(turned_rows, grad_qkv).astype(BF)
        full_rest[2 * k : 2 * k + 2, :, :, 0:640] = g_qkv.reshape(2, 4, 48, 640)

    def rows_of(u, v):
        return full_rest.at[v + p.c * (u - v), u + p.c * (v - u), :, pl.ds(0, 640)]

    one = []
    for d in (1, 3, 2):
        for k in range(4):
            one.append(w.push(rows_of(k, step4(p.v, d)), in1.at[d - 1, k], p.vdev(d)))
    grad_gain = jnp.zeros((1, D), F32)
    grad_shift = jnp.zeros((1, D), F32)
    for k in range(4):
        grad_a = dot_lanes(back[k], w_all[...].reshape(D, 640))
        unit_k, _ = normalise(x_all[k].astype(F32))
        grad_gain = grad_gain + col_sum(grad_a * unit_k)
        grad_shift = grad_shift + col_sum(grad_a)
        normed[k] = grad_a.astype(BF)
    a_one = [w.push(normed.at[step4(p.u, d)], in_a.at[d - 1], p.udev(d)) for d in (1, 3, 2)]
    sums = jnp.broadcast_to(col_sum(grad_qkv.astype(F32)), (8, 640))
    spread = (((1,), (1,)), ((), ()))
    exact = lax.Precision.HIGHEST
    bias_q = lax.dot_general(sums, pick(0, F32), spread, precision=exact, preferred_element_type=F32)
    bias_v = lax.dot_general(sums, pick(1, F32), spread, precision=exact, preferred_element_type=F32)
    grad_vecs[0:1, :] = grad_gain
    grad_vecs[1:2, :] = grad_shift
    grad_vecs[2:3, :] = bias_q[0:1, :]
    grad_vecs[3:4, :] = bias_v[0:1, :]
    vec_in[0, p.z] = grad_vecs[...]
    vec_sends = [[w.push(grad_vecs, vec_in.at[0, p.z], p.zdev(d)) for d in (1, 3, 2)]]
    for part_ in firsts[:2]:
        part_.p3()
    for part_ in outs:
        part_.p2()
    for copy in one:
        copy.wait_recv()
    for k in range(4):
        total = rows_of(k, p.v)[...].astype(F32)
        for d in range(3):
            total = total + in1[d, k].astype(F32)
        part[k] = total.astype(BF)
    two = [w.push(part.at[step4(p.u, d)], in2.at[p.u], p.udev(d)) for d in (1, 3, 2)]
    in2[p.u] = part[p.u]
    for copy in vec_sends[0]:
        copy.wait_recv()
    vec_in[1, p.y] = ordered_sum(vec_in.at[0])
    vec_sends.append([w.push(vec_in.at[1, p.y], vec_in.at[1, p.y], p.ydev(d)) for d in (1, 3, 2)])
    for part_ in firsts[2:]:
        part_.p3()
    for part_ in downs:
        part_.p2()
    for copy in two:
        copy.wait_recv()
    three = [w.push(in2.at[pl.ds((1 - p.c) * 2, 2)], in0, p.sibling())]
    for copy in vec_sends[1]:
        copy.wait_recv()
    vec_in[2, p.x] = ordered_sum(vec_in.at[1])
    vec_sends.append([w.push(vec_in.at[2, p.x], vec_in.at[2, p.x], p.xdev(d)) for d in (1, 3, 2)])
    three[0].wait_recv()
    for k in range(2):
        held[k] = (in2[p.c * 2 + k].astype(F32) + in0[k].astype(F32)).astype(BF)
    in3[p.x] = held[...]
    four = [w.push(held, in3.at[p.x], p.xdev(d)) for d in (1, 3, 2)]
    for part_ in downs + outs:
        part_.p3()
    for part_ in firsts[:2]:
        part_.p4()
    for copy in a_one:
        copy.wait_recv()
    grad_a = normed[p.u].astype(F32)
    for d in range(3):
        grad_a = grad_a + in_a[d].astype(F32)
    unit, inverse = normalise(x[...].astype(F32))
    grad_input[...] = (total_out[...] + normalise_back(grad_a, unit, inverse, vecs[0:1, :])).astype(BF)
    for copy in vec_sends[2]:
        copy.wait_recv()
    vec_in[3, 0] = ordered_sum(vec_in.at[2])
    vec_sends.append([w.push(vec_in.at[3, 0], vec_in.at[3, 1], p.sibling())])
    for copy in four:
        copy.wait_recv()
    for k in range(2):
        total = in3[0, k].astype(F32)
        for d in range(1, 4):
            total = total + in3[d, k].astype(F32)
        packed_sum[p.c * 2 + k] = total
    here = packed_sum.at[pl.ds(p.c * 2, 2)]
    five = [w.push(here, here, p.sibling())]
    for part_ in downs + firsts[2:] + outs:
        part_.p4()
    vec_sends[3][0].wait_recv()
    o_vec[...] = vec_in[3, 0] + vec_in[3, 1]
    for part_ in downs:
        part_.p5()
    five[0].wait_recv()
    groups = [natural_group(packed_sum[g]) for g in range(4)]
    for k in range(3):
        o_rows[:, k * D : k * D + D] = jnp.concatenate(sum([groups[g][k] for g in range(4)], []), 1)
    for part_ in firsts + downs + outs:
        part_.end()
    rest_sends = one + a_one + two + three + four + five + sum(vec_sends, [])
    for copy in to_u + sum(to_v_back, []) + rest_sends:
        copy.wait_send()


def layer(x, cot, w_qkv, vec, lanes, rest, down, key_place, query_place):
    shapes = [
        pltpu.VMEM((4, 4, 48, 5 * D), BF),
        pltpu.VMEM((4, 4, 192, D), BF),
        pltpu.VMEM((4, 512, 640), BF),
        pltpu.VMEM((GROUP, 512), BF),
        pltpu.VMEM((GROUP, TILE), F32),
        pltpu.VMEM((GROUP, TILE), F32),
        pltpu.VMEM((3, 128, GROUP), BF),
        pltpu.VMEM((256, 512), F32),
        pltpu.VMEM((4, OWN, 256), BF),
        pltpu.VMEM((4, OWN, 256), BF),
        pltpu.VMEM((8, 512), F32),
        pltpu.VMEM((4, 4, 192, D), BF),
        pltpu.VMEM((4, 4, 48, FF), BF),
        pltpu.VMEM((4, 4, 48, D), BF),
        pltpu.VMEM((4, OWN, 256), BF),
        pltpu.VMEM((GROUP, 128), F32),
        pltpu.VMEM((3, 3, 4, OWN, 128), BF),
        pltpu.VMEM((OWN, D), F32),
        pltpu.VMEM((OWN, D), F32),
        pltpu.VMEM((2, OWN, D), BF),
        pltpu.VMEM((4, OWN, D), BF),
        pltpu.VMEM((16, 48, 640), BF),
        pltpu.VMEM((4, OWN, D), BF),
        pltpu.VMEM((4, 16, D), BF),
        pltpu.VMEM((4, 16, D), BF),
        pltpu.VMEM((16, D), F32),
        pltpu.VMEM((16, D), F32),
        pltpu.VMEM((4, 4, 16, D), F32),
        pltpu.VMEM((4, OWN, 640), BF),
        pltpu.VMEM((3, OWN, D), BF),
        pltpu.VMEM((3, 4, 48, 640), BF),
        pltpu.VMEM((4, 48, 640), BF),
        pltpu.VMEM((4, 48, 640), BF),
        pltpu.VMEM((2, 48, 640), BF),
        pltpu.VMEM((2, 48, 640), BF),
        pltpu.VMEM((4, 2, 48, 640), BF),
        pltpu.VMEM((4, 48, 640), F32),
    ]
    for _ in range(4):
        shapes += scatter_shapes(48, 384, BF)
    shapes += scatter_wide_shapes(48, 384, BF) + scatter_shapes(48, 384, BF)
    return pl.pallas_call(
        layer_kernel,
        out_shape=(
            jax.ShapeDtypeStruct((OWN, D), BF),
            jax.ShapeDtypeStruct((OWN, D), BF),
            jax.ShapeDtypeStruct((48, 8 * D), F32),
            jax.ShapeDtypeStruct((192, D), F32),
            jax.ShapeDtypeStruct((16, D), F32),
        ),
        in_specs=[VMEM] * 7 + [ANY, VMEM],
        out_specs=(VMEM,) * 5,
        scratch_shapes=shapes + sems(2 * GATHER_SENDS + GATHER_WIDE_SENDS + 5 * SCATTER_SENDS + SCATTER_WIDE_SENDS + 80, 5),
        compiler_params=pltpu.CompilerParams(
            collective_id=1, has_side_effects=True, vmem_limit_bytes=62 * MIB
        ),
        name="layer",
    )(x, cot, w_qkv, vec, lanes, rest, down, key_place, query_place)


def adamw(weight, moment, second, grad, rate, decay):
    moment_new = BETA_ONE * moment + (1.0 - BETA_ONE) * grad
    second_new = BETA_TWO * second + (1.0 - BETA_TWO) * grad * grad
    moment_hat = moment_new / (1.0 - BETA_ONE**STEP)
    second_hat = second_new / (1.0 - BETA_TWO**STEP)
    weight_new = weight - rate * (moment_hat / (jnp.sqrt(second_hat) + EPS_ADAM) + decay * weight)
    return (weight_new, moment_new, second_new)


def pack_groups(queries, keys, values):
    blank = jnp.zeros((queries.shape[0], HD), queries.dtype)
    groups = []
    for g in range(4):
        q, k, v = ([a[:, (3 * g + j) * HD : (3 * g + j + 1) * HD] for j in range(3)] for a in (queries, keys, values))
        groups.append(jnp.concatenate([v[0], k[0], k[1], v[1], v[2], k[2], q[1], q[0], blank, q[2]], 1))
    return jnp.stack(groups)


def per_device(
    tokens,
    cotangent,
    lengths,
    positions,
    w_rows,
    w_down,
    vectors,
    moment_rows,
    second_rows,
    moment_down,
    second_down,
    moment_vectors,
    second_vectors,
):
    shard_index = lax.axis_index("shard")
    core = lax.rem(lax.axis_index("replica"), 2)
    z, y = lax.div(shard_index, 4), lax.rem(shard_index, 4)
    own_v = jnp.where(core == 0, z, y)
    low_rows = w_rows.astype(BF)
    low_qkv = pack_groups(low_rows[:, :D], low_rows[:, D : 2 * D], low_rows[:, 2 * D : 3 * D])
    own_vecs = lax.dynamic_update_slice(
        jnp.zeros((16, D), BF), vectors.astype(BF), (0, shard_index * 48)
    )
    place_blocks = positions.reshape(4, 4, OWN)
    place_all = jnp.where(core == 0, place_blocks, place_blocks.transpose(1, 0, 2)).reshape(GROUP)
    seq_ends = jnp.cumsum(lengths[0])
    place_quarter = lax.dynamic_slice_in_dim(place_all, own_v * 512, 512)
    seq_start = jnp.max(
        jnp.where(place_quarter[None, :] >= seq_ends[:, None], seq_ends[:, None], 0), axis=0
    )
    key_place = jnp.broadcast_to(place_all.astype(F32)[:, None], (GROUP, 128))
    query_place = jnp.pad(jnp.stack([place_quarter, seq_start]).astype(F32), ((0, 6), (0, 0)))

    column = jnp.arange(640)
    block, within = column // HD, column % HD
    lanes = jnp.full((8, 640), -GROUP, jnp.int32)
    for row, places in ((0, ((7, 0), (6, 1), (9, 2))), (1, ((0, 0), (3, 1), (4, 2)))):
        for at, head in places:
            lanes = lanes.at[row].set(jnp.where(block == at, within + head * HD, lanes[row]))
    outputs, grad_input, grad_rows, grad_down, grad_vecs = layer(
        tokens, cotangent, low_qkv, own_vecs, lanes, low_rows[:, 3 * D :], w_down.astype(BF), key_place, query_place
    )
    own_grads = lax.dynamic_slice(grad_vecs, (0, shard_index * 48), (12, 48))
    rows_new = adamw(w_rows, moment_rows, second_rows, grad_rows, LR_MATRIX, DECAY)
    down_new = adamw(w_down, moment_down, second_down, grad_down, LR_MATRIX, DECAY)
    vec_new = adamw(vectors, moment_vectors, second_vectors, own_grads, LR_VECTOR, 0.0)
    return (
        outputs,
        grad_input,
        rows_new[0],
        rows_new[1],
        rows_new[2],
        down_new[0],
        down_new[1],
        down_new[2],
        vec_new[0],
        vec_new[1],
        vec_new[2],
    )


def solution(mesh):
    return jax.shard_map(
        per_device,
        mesh=mesh,
        in_specs=(
            P(("replica", "shard"), None),
            P(("replica", "shard"), None),
            P("replica", None),
            P("replica", None),
            P("shard", None),
            P("shard", None),
            P(None, "shard"),
            P("shard", None),
            P("shard", None),
            P("shard", None),
            P("shard", None),
            P(None, "shard"),
            P(None, "shard"),
        ),
        out_specs=(
            P(("replica", "shard"), None),
            P(("replica", "shard"), None),
            P("shard", None),
            P("shard", None),
            P("shard", None),
            P("shard", None),
            P("shard", None),
            P("shard", None),
            P(None, "shard"),
            P(None, "shard"),
            P(None, "shard"),
        ),
        check_vma=False,
    )
```

```python
import functools

import jax
import jax.numpy as jnp
from jax import lax
from jax.experimental import pallas as pl
from jax.experimental.pallas import tpu as pltpu
from jax.sharding import PartitionSpec as P

H = 12
HD = 64
STEP = 10
D = 768
FF = 3072
OWN = 128
GROUP = 2048
NEIGHBOURS = 4
TILE = 256
CHUNK = 256
STEPS = GROUP // CHUNK
MIB = 1 << 20

EPS_NORM = 1e-05
BETA_ONE = 0.9
BETA_TWO = 0.95
EPS_ADAM = 1e-08
LR_MATRIX = 0.02
LR_VECTOR = 0.3
DECAY = 0.1
HUGE_NEG = -1e30

BF = jnp.bfloat16
F32 = jnp.float32
MESH = pl.DeviceIdType.MESH
VMEM = pl.BlockSpec(memory_space=pltpu.VMEM)
ANY = pl.BlockSpec(memory_space=pl.ANY)


def step4(i, d):
    return lax.rem(i + d, 4)


class Place:
    def __init__(self):
        self.r = lax.axis_index("replica")
        self.s = lax.axis_index("shard")
        self.x = lax.div(self.r, 2)
        self.c = lax.rem(self.r, 2)
        self.z = lax.div(self.s, 4)
        self.y = lax.rem(self.s, 4)
        self.u = self.y + self.c * (self.z - self.y)
        self.v = self.z + self.c * (self.y - self.z)
        self.u_step = 1 + 3 * self.c
        self.v_step = 4 - 3 * self.c

    def ydev(self, d):
        return (self.r, self.z * 4 + step4(self.y, d))

    def zdev(self, d):
        return (self.r, step4(self.z, d) * 4 + self.y)

    def xdev(self, d):
        return (step4(self.x, d) * 2 + self.c, self.s)

    def udev(self, d):
        return (self.r, step4(self.u, d) * self.u_step + self.v * self.v_step)

    def vdev(self, d):
        return (self.r, self.u * self.u_step + step4(self.v, d) * self.v_step)

    def sibling(self):
        return (self.x * 2 + 1 - self.c, self.s)


def greet(devices):
    barrier = pltpu.get_barrier_semaphore()
    for device in devices:
        pl.semaphore_signal(barrier, inc=1, device_id=device, device_id_type=MESH)
    pl.semaphore_wait(barrier, len(devices))


class Wire:
    def __init__(self, send_sems, recv_sems, local_sems):
        self.send_sems, self.recv_sems, self.local_sems = send_sems, recv_sems, local_sems
        self.sent, self.moved = 0, 0

    def push(self, src, dst, device):
        k = self.sent
        self.sent += 1
        copy = pltpu.make_async_remote_copy(
            src_ref=src,
            dst_ref=dst,
            send_sem=self.send_sems.at[k],
            recv_sem=self.recv_sems.at[k],
            device_id=device,
            device_id_type=MESH,
        )
        copy.start()
        return copy

    def local(self, src, dst):
        k = self.moved
        self.moved += 1
        copy = pltpu.make_async_copy(src, dst, self.local_sems.at[k])
        copy.start()
        return copy


def sems(remote, local):
    return [
        pltpu.SemaphoreType.DMA((remote,)),
        pltpu.SemaphoreType.DMA((remote,)),
        pltpu.SemaphoreType.DMA((max(local, 1),)),
    ]


def region(row, rows, col, cols):
    row_cut = slice(None) if rows is None else pl.ds(row, rows)
    col_cut = slice(None) if cols is None else pl.ds(pl.multiple_of(col, 128), cols)
    return (row_cut, col_cut)


class Gather:
    def __init__(self, wire, place, shard, full, cut, y_first):
        self.wire, self.place, self.shard, self.full, self.cut = wire, place, shard, full, cut
        self.y_first = y_first
        self.near = place.ydev if y_first else place.zdev
        self.far = place.zdev if y_first else place.ydev
        self.sends = []

    def push(self, src, dst, device):
        copy = self.wire.push(src, dst, device)
        self.sends.append(copy)
        return copy

    def slab(self, d, blocks=slice(None)):
        p = self.place
        if self.y_first:
            return self.full.at[(step4(p.z, 4 - d), blocks) + self.cut]
        return self.full.at[(blocks, step4(p.y, 4 - d)) + self.cut]

    def first(self):
        p = self.place
        src = self.shard.at[self.cut]
        dst = self.full.at[(p.z, p.y) + self.cut]
        self.own = self.wire.local(src, dst)
        self.one = [self.push(src, dst, self.near(d)) for d in (1, 3, 2)]

    def second(self):
        self.own.wait()
        for copy in self.one:
            copy.wait_recv()
        slab = self.slab(0)
        self.two = [self.push(slab, slab, self.far(d)) for d in (1, 3)]
        self.across = [self.push(slab, slab, self.place.sibling())]

    def third(self):
        self.two[0].wait_recv()
        half = self.slab(1, pl.ds(0, 2))
        self.three = [self.push(half, half, self.far(1))]
        self.two[1].wait_recv()
        half = self.slab(3, pl.ds(2, 2))
        self.three.append(self.push(half, half, self.far(3)))
        for d in (1, 3):
            slab = self.slab(d)
            self.across.append(self.push(slab, slab, self.place.sibling()))

    def fourth(self):
        for copy in self.three:
            copy.wait_recv()
        slab = self.slab(2)
        self.across.append(self.push(slab, slab, self.place.sibling()))

    def arrive(self):
        for copy in self.across:
            copy.wait_recv()

    def end(self):
        for copy in self.sends:
            copy.wait_send()


GATHER_SENDS = 11


def scatter_shapes(rows, cols, dtype):
    return [
        pltpu.VMEM((4, 4, rows, cols), dtype),
        pltpu.VMEM((3, 4, rows, cols), dtype),
        pltpu.VMEM((4, rows, cols), dtype),
        pltpu.VMEM((3, rows, cols), dtype),
        pltpu.VMEM((4, rows, cols), dtype),
    ]


class Scatter:
    def __init__(self, wire, place, grad, out, mine, other, to, z_first, scratch):
        self.wire, self.place, self.grad, self.out = wire, place, grad, out
        self.z_first = z_first
        self.mine, self.other, self.to = mine, other, to
        self.in0, self.in1, self.part, self.in2, self.in3 = scratch
        self.sends, self.wait = [], []

    def push(self, src, dst, device):
        copy = self.wire.push(src, dst, device)
        self.sends.append(copy)
        return copy

    def p0(self):
        every = (slice(None), slice(None))
        self.wait.append(self.push(self.grad.at[every + self.other], self.in0, self.place.sibling()))

    def p1(self):
        p = self.place
        for copy in self.wait:
            copy.wait_recv()

        def add(i, carry):
            at = (lax.div(i, 4), lax.rem(i, 4))
            both = self.grad[at + self.mine].astype(F32) + self.in0[at].astype(F32)
            self.grad[at + self.mine] = both.astype(self.grad.dtype)
            return carry

        lax.fori_loop(0, 16, add, 0)
        self.wait = []
        for d in (1, 3, 2):
            if self.z_first:
                src, device = self.grad.at[(step4(p.z, d), slice(None)) + self.mine], p.zdev(d)
            else:
                src, device = self.grad.at[(slice(None), step4(p.y, d)) + self.mine], p.ydev(d)
            self.wait.append(self.push(src, self.in1.at[d - 1], device))

    def p2(self):
        p = self.place
        for copy in self.wait:
            copy.wait_recv()

        def add(i, carry):
            at = (p.z, i) if self.z_first else (i, p.y)
            total = self.grad[at + self.mine].astype(F32)
            for k in range(3):
                total = total + self.in1[k, i].astype(F32)
            self.part[i] = total.astype(self.part.dtype)
            return carry

        lax.fori_loop(0, 4, add, 0)
        self.wait = []
        for d in (1, 3, 2):
            if self.z_first:
                src, device = self.part.at[step4(p.y, d)], p.ydev(d)
            else:
                src, device = self.part.at[step4(p.z, d)], p.zdev(d)
            self.wait.append(self.push(src, self.in2.at[d - 1], device))

    def p3(self):
        p = self.place
        for copy in self.wait:
            copy.wait_recv()
        total = self.part[p.y if self.z_first else p.z].astype(F32)
        for k in range(3):
            total = total + self.in2[k].astype(F32)
        self.in3[p.x] = total.astype(self.in3.dtype)
        self.wait = [self.push(self.in3.at[p.x], self.in3.at[p.x], p.xdev(d)) for d in (1, 3, 2)]

    def p4(self):
        for copy in self.wait:
            copy.wait_recv()
        total = self.in3[0].astype(F32)
        for k in range(1, 4):
            total = total + self.in3[k].astype(F32)
        self.out[self.to] = total
        here = self.out.at[self.to]
        self.wait = [self.push(here, here, self.place.sibling())]

    def end(self):
        for copy in self.wait:
            copy.wait_recv()
        for copy in self.sends:
            copy.wait_send()


SCATTER_SENDS = 11


class GatherWide(Gather):
    def __init__(self, wire, place, shard, full, rows, cols):
        piece = (pl.ds(pl.multiple_of(place.x * rows, 16), rows), cols)
        super().__init__(wire, place, shard, full, piece, True)
        self.rows, self.cols = rows, cols
        self.along_x = {}

    def hand_on(self, d):
        slab = self.slab(d)
        self.along_x[d] = [self.push(slab, slab, self.place.xdev(e)) for e in (1, 3, 2)]

    def second(self):
        self.own.wait()
        for copy in self.one:
            copy.wait_recv()
        slab = self.slab(0)
        self.two = [self.push(slab, slab, self.far(d)) for d in (1, 3)]
        self.hand_on(0)

    def third(self):
        self.two[0].wait_recv()
        half = self.slab(1, pl.ds(0, 2))
        self.three = [self.push(half, half, self.far(1))]
        self.two[1].wait_recv()
        half = self.slab(3, pl.ds(2, 2))
        self.three.append(self.push(half, half, self.far(3)))
        self.hand_on(1)
        self.hand_on(3)

    def fourth(self):
        for copy in self.three:
            copy.wait_recv()
        self.hand_on(2)

    def fifth(self, order):
        self.across = []
        for d in order:
            for copy in self.along_x[d]:
                copy.wait_recv()
            slab = self.full.at[step4(self.place.z, 4 - d), :, :, self.cols]
            self.across.append(self.push(slab, slab, self.place.sibling()))


GATHER_WIDE_SENDS = 3 + 2 + 2 + 12 + 4


def scatter_wide_shapes(rows, cols, dtype):
    return [
        pltpu.VMEM((4, 4, 4 * rows, cols), dtype),
        pltpu.VMEM((3, 4, 4, rows, cols), dtype),
        pltpu.VMEM((3, 4, rows, cols), dtype),
        pltpu.VMEM((4, rows, cols), dtype),
        pltpu.VMEM((3, rows, cols), dtype),
    ]


class ScatterWide:
    def __init__(self, wire, place, grad, out, rows, mine, other, scratch):
        self.wire, self.place, self.grad, self.out, self.rows = wire, place, grad, out, rows
        self.mine, self.other = mine, other
        self.in0, self.in_x, self.in1, self.part, self.in2 = scratch
        self.sends, self.wait, self.slabs = [], [], []
        self.piece = self.quarter(place.x)

    def quarter(self, x):
        return (pl.ds(pl.multiple_of(x * self.rows, 16), self.rows), self.mine)

    def push(self, src, dst, device):
        copy = self.wire.push(src, dst, device)
        self.sends.append(copy)
        return copy

    def arrive(self):
        for copy in self.wait:
            copy.wait_recv()
        self.wait = []

    def p0_slab(self, i):
        here = self.grad.at[i, :, :, self.other]
        self.slabs.append(self.push(here, self.in0.at[i], self.place.sibling()))

    def p1_slab(self, i):
        p = self.place
        self.slabs[i].wait_recv()
        for k in range(4):
            both = self.grad[i, k, :, self.mine].astype(F32) + self.in0[i, k].astype(F32)
            self.grad[i, k, :, self.mine] = both.astype(self.grad.dtype)
        for d in (1, 3, 2):
            src = self.grad.at[(i, slice(None)) + self.quarter(step4(p.x, d))]
            self.wait.append(self.push(src, self.in_x.at[d - 1, i], p.xdev(d)))

    def p2(self):
        p = self.place
        self.arrive()

        def add(i, carry):
            at = (lax.div(i, 4), lax.rem(i, 4))
            total = self.grad[at + self.piece].astype(F32)
            for k in range(3):
                total = total + self.in_x[(k,) + at].astype(F32)
            self.grad[at + self.piece] = total.astype(self.grad.dtype)
            return carry

        lax.fori_loop(0, 16, add, 0)
        for d in (1, 3, 2):
            src = self.grad.at[(step4(p.z, d), slice(None)) + self.piece]
            self.wait.append(self.push(src, self.in1.at[d - 1], p.zdev(d)))

    def p3(self):
        p = self.place
        self.arrive()
        for i in range(4):
            total = self.grad[(p.z, i) + self.piece].astype(F32)
            for k in range(3):
                total = total + self.in1[k, i].astype(F32)
            self.part[i] = total.astype(self.part.dtype)
        for d in (1, 3, 2):
            self.wait.append(self.push(self.part.at[step4(p.y, d)], self.in2.at[d - 1], p.ydev(d)))

    def p4(self):
        p = self.place
        self.arrive()
        total = self.part[p.y].astype(F32)
        for k in range(3):
            total = total + self.in2[k].astype(F32)
        self.out[self.piece] = total
        here = self.out.at[self.piece]
        self.wait = [self.push(here, here, p.xdev(d)) for d in (1, 3, 2)]

    def p5(self):
        self.arrive()
        here = self.out.at[:, self.mine]
        self.wait = [self.push(here, here, self.place.sibling())]

    def end(self):
        self.arrive()
        for copy in self.sends:
            copy.wait_send()


SCATTER_WIDE_SENDS = 4 + 12 + 3 + 3 + 3 + 1


def all_peers(p):
    rings = [p.ydev(d) for d in (1, 2, 3)] + [p.zdev(d) for d in (1, 2, 3)]
    return rings + [p.sibling()]


def x_peers(p):
    return [p.xdev(d) for d in (1, 2, 3)]


def owner(p, u, v):
    return v * p.v_step + u * p.u_step


def half_lanes(value, right):
    lane = lax.broadcasted_iota(jnp.int32, value.shape, 1)
    keep = lane >= HD if right else lane < HD
    return jnp.where(keep, value, jnp.zeros_like(value))


def rows_max(value):
    return jnp.max(value.reshape(-1, 8, value.shape[1]), axis=0)


def rows_sum(value):
    return jnp.sum(value.reshape(-1, 8, value.shape[1]), axis=0)


def dot_lanes(left, right):
    return lax.dot_general(left, right, (((1,), (1,)), ((), ())), preferred_element_type=F32)


def dot_plain(left, right):
    return jnp.dot(left, right, preferred_element_type=F32)


def fill_bias(key_place, query_place, bias):
    def body(i, carry):
        rows = pl.ds(pl.multiple_of(i * CHUNK, CHUNK), CHUNK)
        keys = key_place[rows, 0:128]
        for k in range(4):
            cols = slice(k * 128, k * 128 + 128)
            ok = (keys <= query_place[0:1, cols]) & (keys >= query_place[1:2, cols])
            bias[rows, cols] = jnp.where(ok, 0.0, HUGE_NEG).astype(BF)
        return carry

    lax.fori_loop(0, STEPS, body, 0, unroll=True)


def key_chunk(kv, i, head):
    a, b = lax.div(i, 2), lax.rem(i, 2) * CHUNK
    return kv[a, pl.ds(pl.multiple_of(b, CHUNK), CHUNK), head * 128 : head * 128 + 128]


def chunk_rows(i):
    return pl.ds(pl.multiple_of(i * CHUNK, CHUNK), CHUNK)


def turn_keys(kv, head, turned):
    def body(i, carry):
        turned[head, :, chunk_rows(i)] = key_chunk(kv, i, head).T
        return carry

    lax.fori_loop(0, STEPS, body, 0, unroll=True)


def query_tile(kv, p, head, tile):
    block = 384 + head // 2 * 128
    return half_lanes(kv[p.v, tile * TILE : tile * TILE + TILE, block : block + 128], head != 1)


def attend(kv, p, head, tile, bias, scores, turned, head_out, lse):
    cols = slice(tile * TILE, tile * TILE + TILE)
    query = query_tile(kv, p, head, tile)

    def score(i, top):
        part = dot_lanes(key_chunk(kv, i, head), query) + bias[chunk_rows(i), cols].astype(F32)
        scores[chunk_rows(i), :] = part
        return jnp.maximum(top, rows_max(part))

    top = lax.fori_loop(0, STEPS, score, jnp.full((8, TILE), -jnp.inf, F32), unroll=True)
    top = jnp.max(top, axis=0, keepdims=True)

    def mix(i, carry):
        total, acc = carry
        raised = jnp.exp(scores[chunk_rows(i), :] - top)
        acc = acc + dot_plain(turned[head, :, chunk_rows(i)], raised.astype(BF))
        return total + rows_sum(raised), acc

    total, acc = lax.fori_loop(
        0, STEPS, mix, (jnp.zeros((8, TILE), F32), jnp.zeros((128, TILE), F32)), unroll=True
    )
    total = jnp.sum(total, axis=0, keepdims=True)
    acc = acc / total
    at = 64 if head == 1 else 0
    head_out[head * 64 : head * 64 + 64, cols] = acc[at : at + 64, :]
    lse[head : head + 1, cols] = top + jnp.log(total)


def attend_back(kv, p, head, tile, bias, probs, grad_probs, turned, dob, lse, acc, part_send, dq):
    cols = slice(tile * TILE, tile * TILE + TILE)
    query = query_tile(kv, p, head, tile)
    block = head // 2 * 128
    dout = dob[2 * tile : 2 * tile + 2, :, block : block + 128]
    dout = half_lanes(dout.reshape(TILE, 128), head == 1)
    total = lse[head : head + 1, cols]

    def weigh(i, inner):
        keys = key_chunk(kv, i, head)
        prob = jnp.exp(dot_lanes(keys, query) + bias[chunk_rows(i), cols].astype(F32) - total)
        gprob = dot_lanes(keys, dout)
        probs[chunk_rows(i), :] = prob
        grad_probs[chunk_rows(i), :] = gprob
        return inner + rows_sum(prob * gprob)

    inner = lax.fori_loop(0, STEPS, weigh, jnp.zeros((8, TILE), F32), unroll=True)
    inner = jnp.sum(inner, axis=0, keepdims=True)

    def back(i, total_dq):
        prob = probs[chunk_rows(i), :]
        gscore = (prob * (grad_probs[chunk_rows(i), :] - inner)).astype(BF)
        both = dot_plain(gscore, query) + dot_plain(prob.astype(BF), dout)
        if tile == 0:
            acc[chunk_rows(i), :] = both
        else:
            total_kv = (acc[chunk_rows(i), :] + both).astype(BF)
            lanes = slice(head * 128, head * 128 + 128)
            part_send[lax.div(i, 2), pl.ds(lax.rem(i, 2) * 2, 2), 0:OWN, lanes] = total_kv.reshape(2, OWN, 128)
        return total_dq + dot_plain(turned[head, :, chunk_rows(i)], gscore)

    total_dq = lax.fori_loop(0, STEPS, back, jnp.zeros((128, TILE), F32), unroll=True)
    total_dq = total_dq * (HD ** (-0.5))
    at = 0 if head == 1 else 64
    row = (64, 0, 192)[head]
    dq[row : row + 64, cols] = total_dq[at : at + 64, :]


def col_sum(value):
    return jnp.sum(value, axis=0, keepdims=True)


def normalise(value):
    average = jnp.mean(value, -1, keepdims=True)
    centred = value - average
    spread = jnp.mean(centred * centred, -1, keepdims=True)
    inverse = lax.rsqrt(spread + EPS_NORM)
    return centred * inverse, inverse


def normalise_back(grad, unit, inverse, gain):
    g = grad * gain
    return inverse * (
        g - jnp.mean(g, -1, keepdims=True) - unit * jnp.mean(g * unit, -1, keepdims=True)
    )


GELU_A = 0.7978845608028654
GELU_B = 0.044715


def out_rows(full_rest, g):
    own = full_rest[g, :, :, 0:D].reshape(192, D)
    return jnp.concatenate([own, jnp.zeros((64, D), BF)], 0)


def ordered_sum(blocks):
    total = blocks[0].astype(F32)
    for k in range(1, blocks.shape[0]):
        total = total + blocks[k].astype(F32)
    return total


def natural_group(packed):
    col = [packed[:, j * HD : (j + 1) * HD] for j in range(10)]
    return [[col[j] for j in order] for order in ((7, 6, 9), (1, 2, 5), (0, 3, 4))]


def layer_kernel(
    x, cot, w_qkv, vec, lanes, rest, down, key_place, query_place,
    outputs, grad_input, o_rows, o_down, o_vec, *scratch,
):
    (
        full_rest, full_down, kv, bias, probs, grad_probs, turned, head_out, out_send, attended, lse,
        g_down, g_first, g_out, dob, acc, part_in, total_out, total_dc, low,
        x_all, w_all, normed, vec_y, vec_z, vecs, grad_vecs, vec_in, back, in_a, in1, part, in2, in0, held, in3, packed_sum,
    ) = scratch[:37]
    part_send, grad_send, dq = full_down, out_send, head_out
    blocks = scratch[37:-3]
    p = Place()
    w = Wire(*scratch[-3:])
    greet(all_peers(p) + x_peers(p))

    places = w.local(key_place, grad_probs.at[:, pl.ds(0, 128)])
    w_one = [(d, w.push(w_qkv.at[step4(p.u, d)], w_all.at[p.s], p.udev(d))) for d in (1, 3, 2)]
    vec_one = [w.push(vec, vec_y.at[p.y], p.ydev(d)) for d in (1, 3, 2)]
    w_all[p.s] = w_qkv[p.u]
    vec_y[p.y] = vec[...]
    w_two = [w.push(w_all.at[p.s], w_all.at[p.s], p.vdev(e)) for e in (1, 3, 2)]
    x_one = [w.push(x, x_all.at[p.u], p.udev(d)) for d in (1, 3, 2)]
    x_all[p.u] = x[...]
    for d, copy in w_one:
        copy.wait_recv()
        block = w_all.at[owner(p, step4(p.u, 4 - d), p.v)]
        w_two += [w.push(block, block, p.vdev(e)) for e in (1, 3, 2)]
    for copy in vec_one:
        copy.wait_recv()
    vec_z[p.z] = ordered_sum(vec_y).astype(BF)
    vec_two = [w.push(vec_z.at[p.z], vec_z.at[p.z], p.zdev(d)) for d in (1, 3, 2)]
    half = p.c * 1920
    parts = [
        Gather(w, p, rest, full_rest, region(0, None, half, 1024), True),
        Gather(w, p, rest, full_rest, region(0, None, half + 1024, 896), False),
        GatherWide(w, p, down, full_down, 48, pl.ds(pl.multiple_of(p.c * 384, 128), 384)),
    ]
    for part_ in parts:
        part_.first()
    places.wait()
    fill_bias(grad_probs, query_place, bias)
    for copy in x_one + vec_two:
        copy.wait_recv()
    vecs[...] = ordered_sum(vec_z)
    low_vecs = vecs[...].astype(BF)

    def pick(row, dtype):
        column = lax.broadcasted_iota(jnp.int32, (D, 640), 0) - 192 * p.u
        return (column == lanes[row : row + 1, :]).astype(dtype)

    bias_own = dot_plain(low_vecs, pick(0, BF))[2:3, :] + dot_plain(low_vecs, pick(1, BF))[3:4, :]
    scale = jnp.where(lax.broadcasted_iota(jnp.int32, (1, 640), 1) < 384, 1.0, HD ** (-0.5)).astype(F32)
    for k in range(4):
        unit, _ = normalise(x_all[k].astype(F32))
        normed[k] = (unit * vecs[0:1, :] + vecs[1:2, :]).astype(BF)
    for part_ in parts:
        part_.second()
    for copy in w_two:
        copy.wait_recv()
    for k in range(4):
        projected = dot_plain(normed[k], w_all[...].reshape(D, 640)) + bias_own
        kv[p.v, k * OWN : k * OWN + OWN, :] = (projected.astype(BF).astype(F32) * scale).astype(BF)
    to_v = []
    for head in range(3):
        mine = kv.at[p.v, :, pl.ds(head * 128, 128)]
        to_v += [w.push(mine, mine, p.vdev(d)) for d in (1, 3, 2)]
    parts[2].third()
    head_out[192:256, :] = jnp.zeros((64, 512), F32)
    for head in range(3):
        for copy in to_v[3 * head : 3 * head + 3]:
            copy.wait_recv()
        turn_keys(kv, head, turned)
        for tile in range(2):
            attend(kv, p, head, tile, bias, probs, turned, head_out, lse)
        if head == 0:
            for part_ in parts[:2]:
                part_.third()
            parts[2].fourth()
    for k in range(4):
        out_send[k] = head_out[:, k * OWN : k * OWN + OWN].T.astype(BF)
    attended[p.u] = out_send[p.u]
    out_back = [w.push(out_send.at[step4(p.u, d)], attended.at[p.u], p.udev(d)) for d in (1, 3, 2)]
    for part_ in parts[:2]:
        part_.fourth()
    parts[2].fifth((0, 1, 3, 2))
    for copy in out_back:
        copy.wait_recv()
    for part_ in parts[:2]:
        part_.arrive()
    early = to_v + out_back + x_one + w_two + vec_one + vec_two + [c for _, c in w_one]

    grad_y = cot[...].astype(F32)
    middle = x[...].astype(F32) + vecs[4:5, :]
    for g in range(4):
        middle = middle + dot_plain(attended[g], out_rows(full_rest, g))
    unit, inverse = normalise(middle)
    low[0] = (unit * vecs[5:6, :] + vecs[6:7, :]).astype(BF)
    total_out[...] = middle + vecs[7:8, :]
    total_dc[...] = jnp.zeros((OWN, D), F32)
    low_turned = low[0].T

    parts[2].arrive()

    def first_part(i):
        at = i * D + p.c * 384
        to = i * D + (1 - p.c) * 384
        return Scatter(
            w, p, g_first, o_rows, region(0, None, at, 384), region(0, None, to, 384),
            region(0, None, at + 4 * D, 384), i % 2 == 0, blocks[5 * i : 5 * i + 5],
        )

    firsts = [first_part(i) for i in range(4)]
    at, to = p.c * 384, (1 - p.c) * 384
    downs = [
        ScatterWide(
            w, p, g_down, o_down, 48, pl.ds(pl.multiple_of(at, 128), 384),
            pl.ds(pl.multiple_of(to, 128), 384), blocks[20:25],
        )
    ]
    outs = [
        Scatter(
            w, p, g_out, o_rows, region(0, None, at, 384), region(0, None, to, 384),
            region(0, None, at + 3 * D, 384), False, blocks[25:30],
        )
    ]
    for i in range(4):
        w_first = full_rest[:, :, :, D + i * D : 2 * D + i * D].reshape(D, D)
        w_down = full_down[i].reshape(D, D)
        act = dot_plain(low[0], w_first) + vecs[8 + i : 9 + i, :]
        square = act * act
        bent = jnp.tanh(GELU_A * (act + GELU_B * act * square))
        hidden = (0.5 * act * (1.0 + bent)).astype(BF)
        slope = 0.5 * (1.0 + bent) + 0.5 * act * (1.0 - bent * bent) * (
            GELU_A * (1.0 + 3.0 * GELU_B * square)
        )
        hidden_turned = hidden.T
        for k in range(2):
            rows = slice(k * 384, k * 384 + 384)
            g_down[i, 2 * k : 2 * k + 2] = (
                dot_plain(hidden_turned[rows], cot[...]).astype(BF).reshape(2, 192, D)
            )
        for part_ in downs:
            part_.p0_slab(i)
        grad_act = (dot_lanes(cot[...], w_down) * slope).astype(BF)
        grad_vecs[8 + i : 9 + i, :] = col_sum(grad_act.astype(F32))
        for k in range(2):
            rows = slice(k * 384, k * 384 + 384)
            g_first[2 * k : 2 * k + 2, :, :, i * D : i * D + D] = (
                dot_plain(low_turned[rows], grad_act).astype(BF).reshape(2, 4, 48, D)
            )
        total_dc[...] += dot_lanes(grad_act, w_first)
        total_out[...] += dot_plain(hidden, w_down)
        if i > 0:
            downs[0].p1_slab(i - 1)
    for part_ in firsts:
        part_.p0()
    outputs[...] = total_out[...].astype(BF)

    for part_ in parts:
        part_.end()
    for copy in early:
        copy.wait_send()

    grad_c = total_dc[...]
    grad_m = grad_y + normalise_back(grad_c, unit, inverse, vecs[5:6, :])
    total_out[...] = grad_m
    low[1] = grad_m.astype(BF)
    for g in range(4):
        grad_send[g] = dot_lanes(low[1], out_rows(full_rest, g)).astype(BF)
    dob[p.u] = grad_send[p.u]
    to_u = [w.push(grad_send.at[step4(p.u, d)], dob.at[p.u], p.udev(d)) for d in (1, 3, 2)]
    for g in range(4):
        g_out[g] = dot_plain(attended[g].T, low[1])[0:192, :].astype(BF).reshape(4, 48, D)
    outs[0].p0()
    grad_vecs[0:4, :] = jnp.zeros((4, D), F32)
    grad_vecs[4:5, :] = col_sum(low[1].astype(F32))
    grad_vecs[5:6, :] = col_sum(grad_c * unit)
    grad_vecs[6:7, :] = col_sum(grad_c)
    grad_vecs[7:8, :] = col_sum(grad_y)
    grad_vecs[12:16, :] = jnp.zeros((4, D), F32)
    downs[0].p1_slab(3)
    for copy in to_u:
        copy.wait_recv()

    stages = [
        lambda: [part_.p1() for part_ in firsts[:2]],
        lambda: [part_.p1() for part_ in firsts[2:]],
        lambda: [part_.p1() for part_ in outs],
        lambda: None,
        lambda: [part_.p2() for part_ in firsts[:2]],
        lambda: None,
    ]
    to_v_back = []
    for head in range(3):
        for tile in range(2):
            attend_back(
                kv, p, head, tile, bias, probs, grad_probs, turned, dob, lse, acc, part_send, dq
            )
            if tile == 1:
                to_v_back.append(
                    [
                        w.push(
                            part_send.at[step4(p.v, d), :, pl.ds(0, OWN), pl.ds(head * 128, 128)],
                            part_in.at[head, d - 1],
                            p.vdev(d),
                        )
                        for d in (1, 3, 2)
                    ]
                )
            stages[head * 2 + tile]()
    dq[128:192, :] = jnp.zeros((64, 512), F32)
    for k in range(4):
        back[k, :, 384:640] = dq[:, k * OWN : k * OWN + OWN].T.astype(BF)

    def rows_of(u, v, col, cols):
        return full_rest.at[v + p.c * (u - v), u + p.c * (v - u), :, pl.ds(col, cols)]

    def send_columns(col, cols):
        grad_part = back[:, :, col : col + cols].reshape(512, cols)
        for k in range(2):
            turned_rows = normed[:, :, k * 384 : k * 384 + 384].reshape(512, 384).T
            g_part = dot_plain(turned_rows, grad_part).astype(BF)
            full_rest[2 * k : 2 * k + 2, :, :, col : col + cols] = g_part.reshape(2, 4, 48, cols)
        sent = []
        for d in (1, 3, 2):
            for k in range(4):
                src = rows_of(k, step4(p.v, d), col, cols)
                sent.append(w.push(src, in1.at[d - 1, k, :, pl.ds(col, cols)], p.vdev(d)))
        return sent

    one = send_columns(384, 256)
    for part_ in firsts[2:]:
        part_.p2()
    for head in range(3):
        for copy in to_v_back[head]:
            copy.wait_recv()
        columns = slice(head * 128, head * 128 + 128)
        for k in range(4):
            total = part_send[p.v, k, 0:OWN, columns].astype(F32)
            for d in range(3):
                total = total + part_in[head, d, k].astype(F32)
            back[k, :, columns] = total.astype(BF)
    one += send_columns(0, 384)
    for part_ in downs:
        part_.p2()
    grad_qkv = back[...].reshape(512, 640)
    grad_gain = jnp.zeros((1, D), F32)
    grad_shift = jnp.zeros((1, D), F32)
    for k in range(4):
        grad_a = dot_lanes(back[k], w_all[...].reshape(D, 640))
        unit_k, _ = normalise(x_all[k].astype(F32))
        grad_gain = grad_gain + col_sum(grad_a * unit_k)
        grad_shift = grad_shift + col_sum(grad_a)
        normed[k] = grad_a.astype(BF)
    a_one = [w.push(normed.at[step4(p.u, d)], in_a.at[d - 1], p.udev(d)) for d in (1, 3, 2)]
    sums = jnp.broadcast_to(col_sum(grad_qkv.astype(F32)), (8, 640))
    spread = (((1,), (1,)), ((), ()))
    exact = lax.Precision.HIGHEST
    bias_q = lax.dot_general(sums, pick(0, F32), spread, precision=exact, preferred_element_type=F32)
    bias_v = lax.dot_general(sums, pick(1, F32), spread, precision=exact, preferred_element_type=F32)
    grad_vecs[0:1, :] = grad_gain
    grad_vecs[1:2, :] = grad_shift
    grad_vecs[2:3, :] = bias_q[0:1, :]
    grad_vecs[3:4, :] = bias_v[0:1, :]
    vec_in[0, p.z] = grad_vecs[...]
    vec_sends = [[w.push(grad_vecs, vec_in.at[0, p.z], p.zdev(d)) for d in (1, 3, 2)]]
    for part_ in firsts[:2]:
        part_.p3()
    for part_ in outs:
        part_.p2()
    for copy in one:
        copy.wait_recv()
    for k in range(4):
        total = rows_of(k, p.v, 0, 640)[...].astype(F32)
        for d in range(3):
            total = total + in1[d, k].astype(F32)
        part[k] = total.astype(BF)
    two = [w.push(part.at[step4(p.u, d)], in2.at[p.u], p.udev(d)) for d in (1, 3, 2)]
    in2[p.u] = part[p.u]
    for copy in vec_sends[0]:
        copy.wait_recv()
    vec_in[1, p.y] = ordered_sum(vec_in.at[0])
    vec_sends.append([w.push(vec_in.at[1, p.y], vec_in.at[1, p.y], p.ydev(d)) for d in (1, 3, 2)])
    for part_ in firsts[2:]:
        part_.p3()
    for copy in two:
        copy.wait_recv()
    three = [w.push(in2.at[pl.ds((1 - p.c) * 2, 2)], in0, p.sibling())]
    for part_ in downs + outs:
        part_.p3()
    for copy in vec_sends[1]:
        copy.wait_recv()
    vec_in[2, p.x] = ordered_sum(vec_in.at[1])
    vec_sends.append([w.push(vec_in.at[2, p.x], vec_in.at[2, p.x], p.xdev(d)) for d in (1, 3, 2)])
    three[0].wait_recv()
    for k in range(2):
        held[k] = (in2[p.c * 2 + k].astype(F32) + in0[k].astype(F32)).astype(BF)
    in3[p.x] = held[...]
    four = [w.push(held, in3.at[p.x], p.xdev(d)) for d in (1, 3, 2)]
    for part_ in firsts[:2]:
        part_.p4()
    for copy in a_one:
        copy.wait_recv()
    grad_a = normed[p.u].astype(F32)
    for d in range(3):
        grad_a = grad_a + in_a[d].astype(F32)
    unit, inverse = normalise(x[...].astype(F32))
    grad_input[...] = (total_out[...] + normalise_back(grad_a, unit, inverse, vecs[0:1, :])).astype(BF)
    for part_ in downs:
        part_.p4()
    for copy in vec_sends[2]:
        copy.wait_recv()
    vec_in[3, 0] = ordered_sum(vec_in.at[2])
    vec_sends.append([w.push(vec_in.at[3, 0], vec_in.at[3, 1], p.sibling())])
    for copy in four:
        copy.wait_recv()
    for k in range(2):
        total = in3[0, k].astype(F32)
        for d in range(1, 4):
            total = total + in3[d, k].astype(F32)
        packed_sum[p.c * 2 + k] = total
    here = packed_sum.at[pl.ds(p.c * 2, 2)]
    five = [w.push(here, here, p.sibling())]
    for part_ in firsts[2:] + outs:
        part_.p4()
    vec_sends[3][0].wait_recv()
    o_vec[...] = vec_in[3, 0] + vec_in[3, 1]
    for part_ in downs:
        part_.p5()
    five[0].wait_recv()
    groups = [natural_group(packed_sum[g]) for g in range(4)]
    for k in range(3):
        o_rows[:, k * D : k * D + D] = jnp.concatenate(sum([groups[g][k] for g in range(4)], []), 1)
    for part_ in firsts + downs + outs:
        part_.end()
    rest_sends = one + a_one + two + three + four + five + sum(vec_sends, [])
    for copy in to_u + sum(to_v_back, []) + rest_sends:
        copy.wait_send()


def layer(x, cot, w_qkv, vec, lanes, rest, down, key_place, query_place):
    shapes = [
        pltpu.VMEM((4, 4, 48, 5 * D), BF),
        pltpu.VMEM((4, 4, 192, D), BF),
        pltpu.VMEM((4, 512, 640), BF),
        pltpu.VMEM((GROUP, 512), BF),
        pltpu.VMEM((GROUP, TILE), F32),
        pltpu.VMEM((GROUP, TILE), F32),
        pltpu.VMEM((3, 128, GROUP), BF),
        pltpu.VMEM((256, 512), F32),
        pltpu.VMEM((4, OWN, 256), BF),
        pltpu.VMEM((4, OWN, 256), BF),
        pltpu.VMEM((8, 512), F32),
        pltpu.VMEM((4, 4, 192, D), BF),
        pltpu.VMEM((4, 4, 48, FF), BF),
        pltpu.VMEM((4, 4, 48, D), BF),
        pltpu.VMEM((4, OWN, 256), BF),
        pltpu.VMEM((GROUP, 128), F32),
        pltpu.VMEM((3, 3, 4, OWN, 128), BF),
        pltpu.VMEM((OWN, D), F32),
        pltpu.VMEM((OWN, D), F32),
        pltpu.VMEM((2, OWN, D), BF),
        pltpu.VMEM((4, OWN, D), BF),
        pltpu.VMEM((16, 48, 640), BF),
        pltpu.VMEM((4, OWN, D), BF),
        pltpu.VMEM((4, 16, D), BF),
        pltpu.VMEM((4, 16, D), BF),
        pltpu.VMEM((16, D), F32),
        pltpu.VMEM((16, D), F32),
        pltpu.VMEM((4, 4, 16, D), F32),
        pltpu.VMEM((4, OWN, 640), BF),
        pltpu.VMEM((3, OWN, D), BF),
        pltpu.VMEM((3, 4, 48, 640), BF),
        pltpu.VMEM((4, 48, 640), BF),
        pltpu.VMEM((4, 48, 640), BF),
        pltpu.VMEM((2, 48, 640), BF),
        pltpu.VMEM((2, 48, 640), BF),
        pltpu.VMEM((4, 2, 48, 640), BF),
        pltpu.VMEM((4, 48, 640), F32),
    ]
    for _ in range(4):
        shapes += scatter_shapes(48, 384, BF)
    shapes += scatter_wide_shapes(48, 384, BF) + scatter_shapes(48, 384, BF)
    return pl.pallas_call(
        layer_kernel,
        out_shape=(
            jax.ShapeDtypeStruct((OWN, D), BF),
            jax.ShapeDtypeStruct((OWN, D), BF),
            jax.ShapeDtypeStruct((48, 8 * D), F32),
            jax.ShapeDtypeStruct((192, D), F32),
            jax.ShapeDtypeStruct((16, D), F32),
        ),
        in_specs=[VMEM] * 7 + [ANY, VMEM],
        out_specs=(VMEM,) * 5,
        scratch_shapes=shapes + sems(2 * GATHER_SENDS + GATHER_WIDE_SENDS + 5 * SCATTER_SENDS + SCATTER_WIDE_SENDS + 100, 5),
        compiler_params=pltpu.CompilerParams(
            collective_id=1, has_side_effects=True, vmem_limit_bytes=62 * MIB
        ),
        name="layer",
    )(x, cot, w_qkv, vec, lanes, rest, down, key_place, query_place)


def adamw(weight, moment, second, grad, rate, decay):
    moment_new = BETA_ONE * moment + (1.0 - BETA_ONE) * grad
    second_new = BETA_TWO * second + (1.0 - BETA_TWO) * grad * grad
    moment_hat = moment_new / (1.0 - BETA_ONE**STEP)
    second_hat = second_new / (1.0 - BETA_TWO**STEP)
    weight_new = weight - rate * (moment_hat / (jnp.sqrt(second_hat) + EPS_ADAM) + decay * weight)
    return (weight_new, moment_new, second_new)


def pack_groups(queries, keys, values):
    blank = jnp.zeros((queries.shape[0], HD), queries.dtype)
    groups = []
    for g in range(4):
        q, k, v = ([a[:, (3 * g + j) * HD : (3 * g + j + 1) * HD] for j in range(3)] for a in (queries, keys, values))
        groups.append(jnp.concatenate([v[0], k[0], k[1], v[1], v[2], k[2], q[1], q[0], blank, q[2]], 1))
    return jnp.stack(groups)


def per_device(
    tokens,
    cotangent,
    lengths,
    positions,
    w_rows,
    w_down,
    vectors,
    moment_rows,
    second_rows,
    moment_down,
    second_down,
    moment_vectors,
    second_vectors,
):
    shard_index = lax.axis_index("shard")
    core = lax.rem(lax.axis_index("replica"), 2)
    z, y = lax.div(shard_index, 4), lax.rem(shard_index, 4)
    own_v = jnp.where(core == 0, z, y)
    low_rows = w_rows.astype(BF)
    low_qkv = pack_groups(low_rows[:, :D], low_rows[:, D : 2 * D], low_rows[:, 2 * D : 3 * D])
    own_vecs = lax.dynamic_update_slice(
        jnp.zeros((16, D), BF), vectors.astype(BF), (0, shard_index * 48)
    )
    place_blocks = positions.reshape(4, 4, OWN)
    place_all = jnp.where(core == 0, place_blocks, place_blocks.transpose(1, 0, 2)).reshape(GROUP)
    seq_ends = jnp.cumsum(lengths[0])
    place_quarter = lax.dynamic_slice_in_dim(place_all, own_v * 512, 512)
    seq_start = jnp.max(
        jnp.where(place_quarter[None, :] >= seq_ends[:, None], seq_ends[:, None], 0), axis=0
    )
    key_place = jnp.broadcast_to(place_all.astype(F32)[:, None], (GROUP, 128))
    query_place = jnp.pad(jnp.stack([place_quarter, seq_start]).astype(F32), ((0, 6), (0, 0)))

    column = jnp.arange(640)
    block, within = column // HD, column % HD
    lanes = jnp.full((8, 640), -GROUP, jnp.int32)
    for row, places in ((0, ((7, 0), (6, 1), (9, 2))), (1, ((0, 0), (3, 1), (4, 2)))):
        for at, head in places:
            lanes = lanes.at[row].set(jnp.where(block == at, within + head * HD, lanes[row]))
    outputs, grad_input, grad_rows, grad_down, grad_vecs = layer(
        tokens, cotangent, low_qkv, own_vecs, lanes, low_rows[:, 3 * D :], w_down.astype(BF), key_place, query_place
    )
    own_grads = lax.dynamic_slice(grad_vecs, (0, shard_index * 48), (12, 48))
    rows_new = adamw(w_rows, moment_rows, second_rows, grad_rows, LR_MATRIX, DECAY)
    down_new = adamw(w_down, moment_down, second_down, grad_down, LR_MATRIX, DECAY)
    vec_new = adamw(vectors, moment_vectors, second_vectors, own_grads, LR_VECTOR, 0.0)
    return (
        outputs,
        grad_input,
        rows_new[0],
        rows_new[1],
        rows_new[2],
        down_new[0],
        down_new[1],
        down_new[2],
        vec_new[0],
        vec_new[1],
        vec_new[2],
    )


def solution(mesh):
    return jax.shard_map(
        per_device,
        mesh=mesh,
        in_specs=(
            P(("replica", "shard"), None),
            P(("replica", "shard"), None),
            P("replica", None),
            P("replica", None),
            P("shard", None),
            P("shard", None),
            P(None, "shard"),
            P("shard", None),
            P("shard", None),
            P("shard", None),
            P("shard", None),
            P(None, "shard"),
            P(None, "shard"),
        ),
        out_specs=(
            P(("replica", "shard"), None),
            P(("replica", "shard"), None),
            P("shard", None),
            P("shard", None),
            P("shard", None),
            P("shard", None),
            P("shard", None),
            P("shard", None),
            P(None, "shard"),
            P(None, "shard"),
            P(None, "shard"),
        ),
        check_vma=False,
    )
```

```python
import functools

import jax
import jax.numpy as jnp
from jax import lax
from jax.experimental import pallas as pl
from jax.experimental.pallas import tpu as pltpu
from jax.sharding import PartitionSpec as P

H = 12
HD = 64
STEP = 10
D = 768
FF = 3072
OWN = 128
GROUP = 2048
NEIGHBOURS = 4
TILE = 256
CHUNK = 256
STEPS = GROUP // CHUNK
MIB = 1 << 20

EPS_NORM = 1e-05
BETA_ONE = 0.9
BETA_TWO = 0.95
EPS_ADAM = 1e-08
LR_MATRIX = 0.02
LR_VECTOR = 0.3
DECAY = 0.1
HUGE_NEG = -1e30

BF = jnp.bfloat16
F32 = jnp.float32
MESH = pl.DeviceIdType.MESH
VMEM = pl.BlockSpec(memory_space=pltpu.VMEM)
ANY = pl.BlockSpec(memory_space=pl.ANY)


def step4(i, d):
    return lax.rem(i + d, 4)


class Place:
    def __init__(self):
        self.r = lax.axis_index("replica")
        self.s = lax.axis_index("shard")
        self.x = lax.div(self.r, 2)
        self.c = lax.rem(self.r, 2)
        self.z = lax.div(self.s, 4)
        self.y = lax.rem(self.s, 4)
        self.u = self.y + self.c * (self.z - self.y)
        self.v = self.z + self.c * (self.y - self.z)
        self.u_step = 1 + 3 * self.c
        self.v_step = 4 - 3 * self.c

    def ydev(self, d):
        return (self.r, self.z * 4 + step4(self.y, d))

    def zdev(self, d):
        return (self.r, step4(self.z, d) * 4 + self.y)

    def xdev(self, d):
        return (step4(self.x, d) * 2 + self.c, self.s)

    def udev(self, d):
        return (self.r, step4(self.u, d) * self.u_step + self.v * self.v_step)

    def vdev(self, d):
        return (self.r, self.u * self.u_step + step4(self.v, d) * self.v_step)

    def sibling(self):
        return (self.x * 2 + 1 - self.c, self.s)


def greet(devices):
    barrier = pltpu.get_barrier_semaphore()
    for device in devices:
        pl.semaphore_signal(barrier, inc=1, device_id=device, device_id_type=MESH)
    pl.semaphore_wait(barrier, len(devices))


class Wire:
    def __init__(self, send_sems, recv_sems, local_sems):
        self.send_sems, self.recv_sems, self.local_sems = send_sems, recv_sems, local_sems
        self.sent, self.moved = 0, 0

    def push(self, src, dst, device):
        k = self.sent
        self.sent += 1
        copy = pltpu.make_async_remote_copy(
            src_ref=src,
            dst_ref=dst,
            send_sem=self.send_sems.at[k],
            recv_sem=self.recv_sems.at[k],
            device_id=device,
            device_id_type=MESH,
        )
        copy.start()
        return copy

    def local(self, src, dst):
        k = self.moved
        self.moved += 1
        copy = pltpu.make_async_copy(src, dst, self.local_sems.at[k])
        copy.start()
        return copy


def sems(remote, local):
    return [
        pltpu.SemaphoreType.DMA((remote,)),
        pltpu.SemaphoreType.DMA((remote,)),
        pltpu.SemaphoreType.DMA((max(local, 1),)),
    ]


def region(row, rows, col, cols):
    row_cut = slice(None) if rows is None else pl.ds(row, rows)
    col_cut = slice(None) if cols is None else pl.ds(pl.multiple_of(col, 128), cols)
    return (row_cut, col_cut)


class Gather:
    def __init__(self, wire, place, shard, full, cut, y_first):
        self.wire, self.place, self.shard, self.full, self.cut = wire, place, shard, full, cut
        self.y_first = y_first
        self.near = place.ydev if y_first else place.zdev
        self.far = place.zdev if y_first else place.ydev
        self.sends = []

    def push(self, src, dst, device):
        copy = self.wire.push(src, dst, device)
        self.sends.append(copy)
        return copy

    def slab(self, d, blocks=slice(None)):
        p = self.place
        if self.y_first:
            return self.full.at[(step4(p.z, 4 - d), blocks) + self.cut]
        return self.full.at[(blocks, step4(p.y, 4 - d)) + self.cut]

    def first(self):
        p = self.place
        src = self.shard.at[self.cut]
        dst = self.full.at[(p.z, p.y) + self.cut]
        self.own = self.wire.local(src, dst)
        self.one = [self.push(src, dst, self.near(d)) for d in (1, 3, 2)]

    def second(self):
        self.own.wait()
        for copy in self.one:
            copy.wait_recv()
        slab = self.slab(0)
        self.two = [self.push(slab, slab, self.far(d)) for d in (1, 3)]
        self.across = [self.push(slab, slab, self.place.sibling())]

    def third(self):
        self.two[0].wait_recv()
        half = self.slab(1, pl.ds(0, 2))
        self.three = [self.push(half, half, self.far(1))]
        self.two[1].wait_recv()
        half = self.slab(3, pl.ds(2, 2))
        self.three.append(self.push(half, half, self.far(3)))
        for d in (1, 3):
            slab = self.slab(d)
            self.across.append(self.push(slab, slab, self.place.sibling()))

    def fourth(self):
        for copy in self.three:
            copy.wait_recv()
        slab = self.slab(2)
        self.across.append(self.push(slab, slab, self.place.sibling()))

    def arrive(self):
        for copy in self.across:
            copy.wait_recv()

    def end(self):
        for copy in self.sends:
            copy.wait_send()


GATHER_SENDS = 11


def scatter_shapes(rows, cols, dtype):
    return [
        pltpu.VMEM((4, 4, rows, cols), dtype),
        pltpu.VMEM((3, 4, rows, cols), dtype),
        pltpu.VMEM((4, rows, cols), dtype),
        pltpu.VMEM((3, rows, cols), dtype),
        pltpu.VMEM((4, rows, cols), dtype),
    ]


class Scatter:
    def __init__(self, wire, place, grad, out, mine, other, to, z_first, scratch):
        self.wire, self.place, self.grad, self.out = wire, place, grad, out
        self.z_first = z_first
        self.mine, self.other, self.to = mine, other, to
        self.in0, self.in1, self.part, self.in2, self.in3 = scratch
        self.sends, self.wait = [], []

    def push(self, src, dst, device):
        copy = self.wire.push(src, dst, device)
        self.sends.append(copy)
        return copy

    def p0(self):
        every = (slice(None), slice(None))
        self.wait.append(self.push(self.grad.at[every + self.other], self.in0, self.place.sibling()))

    def p1(self):
        p = self.place
        for copy in self.wait:
            copy.wait_recv()

        def add(i, carry):
            at = (lax.div(i, 4), lax.rem(i, 4))
            both = self.grad[at + self.mine].astype(F32) + self.in0[at].astype(F32)
            self.grad[at + self.mine] = both.astype(self.grad.dtype)
            return carry

        lax.fori_loop(0, 16, add, 0)
        self.wait = []
        for d in (1, 3, 2):
            if self.z_first:
                src, device = self.grad.at[(step4(p.z, d), slice(None)) + self.mine], p.zdev(d)
            else:
                src, device = self.grad.at[(slice(None), step4(p.y, d)) + self.mine], p.ydev(d)
            self.wait.append(self.push(src, self.in1.at[d - 1], device))

    def p2(self):
        p = self.place
        for copy in self.wait:
            copy.wait_recv()

        def add(i, carry):
            at = (p.z, i) if self.z_first else (i, p.y)
            total = self.grad[at + self.mine].astype(F32)
            for k in range(3):
                total = total + self.in1[k, i].astype(F32)
            self.part[i] = total.astype(self.part.dtype)
            return carry

        lax.fori_loop(0, 4, add, 0)
        self.wait = []
        for d in (1, 3, 2):
            if self.z_first:
                src, device = self.part.at[step4(p.y, d)], p.ydev(d)
            else:
                src, device = self.part.at[step4(p.z, d)], p.zdev(d)
            self.wait.append(self.push(src, self.in2.at[d - 1], device))

    def p3(self):
        p = self.place
        for copy in self.wait:
            copy.wait_recv()
        total = self.part[p.y if self.z_first else p.z].astype(F32)
        for k in range(3):
            total = total + self.in2[k].astype(F32)
        self.in3[p.x] = total.astype(self.in3.dtype)
        self.wait = [self.push(self.in3.at[p.x], self.in3.at[p.x], p.xdev(d)) for d in (1, 3, 2)]

    def p4(self):
        for copy in self.wait:
            copy.wait_recv()
        total = self.in3[0].astype(F32)
        for k in range(1, 4):
            total = total + self.in3[k].astype(F32)
        self.out[self.to] = total
        here = self.out.at[self.to]
        self.wait = [self.push(here, here, self.place.sibling())]

    def end(self):
        for copy in self.wait:
            copy.wait_recv()
        for copy in self.sends:
            copy.wait_send()


SCATTER_SENDS = 11


class GatherWide(Gather):
    def __init__(self, wire, place, shard, full, rows, cols):
        piece = (pl.ds(pl.multiple_of(place.x * rows, 16), rows), cols)
        super().__init__(wire, place, shard, full, piece, True)
        self.rows, self.cols = rows, cols
        self.along_x = {}

    def hand_on(self, d):
        slab = self.slab(d)
        self.along_x[d] = [self.push(slab, slab, self.place.xdev(e)) for e in (1, 3, 2)]

    def second(self):
        self.own.wait()
        for copy in self.one:
            copy.wait_recv()
        slab = self.slab(0)
        self.two = [self.push(slab, slab, self.far(d)) for d in (1, 3)]
        self.hand_on(0)

    def third(self):
        self.two[0].wait_recv()
        half = self.slab(1, pl.ds(0, 2))
        self.three = [self.push(half, half, self.far(1))]
        self.two[1].wait_recv()
        half = self.slab(3, pl.ds(2, 2))
        self.three.append(self.push(half, half, self.far(3)))
        self.hand_on(1)
        self.hand_on(3)

    def fourth(self):
        for copy in self.three:
            copy.wait_recv()
        self.hand_on(2)

    def fifth(self, order):
        self.across = []
        for d in order:
            for copy in self.along_x[d]:
                copy.wait_recv()
            slab = self.full.at[step4(self.place.z, 4 - d), :, :, self.cols]
            self.across.append(self.push(slab, slab, self.place.sibling()))


GATHER_WIDE_SENDS = 3 + 2 + 2 + 12 + 4


def scatter_wide_shapes(rows, cols, dtype):
    return [
        pltpu.VMEM((4, 4, 4 * rows, cols), dtype),
        pltpu.VMEM((3, 4, 4, rows, cols), dtype),
        pltpu.VMEM((3, 4, rows, cols), dtype),
        pltpu.VMEM((4, rows, cols), dtype),
        pltpu.VMEM((3, rows, cols), dtype),
    ]


class ScatterWide:
    def __init__(self, wire, place, grad, out, rows, mine, other, scratch):
        self.wire, self.place, self.grad, self.out, self.rows = wire, place, grad, out, rows
        self.mine, self.other = mine, other
        self.in0, self.in_x, self.in1, self.part, self.in2 = scratch
        self.sends, self.wait, self.slabs = [], [], []
        self.piece = self.quarter(place.x)

    def quarter(self, x):
        return (pl.ds(pl.multiple_of(x * self.rows, 16), self.rows), self.mine)

    def push(self, src, dst, device):
        copy = self.wire.push(src, dst, device)
        self.sends.append(copy)
        return copy

    def arrive(self):
        for copy in self.wait:
            copy.wait_recv()
        self.wait = []

    def p0_slab(self, i):
        here = self.grad.at[i, :, :, self.other]
        self.slabs.append(self.push(here, self.in0.at[i], self.place.sibling()))

    def p1_slab(self, i):
        p = self.place
        self.slabs[i].wait_recv()
        for k in range(4):
            both = self.grad[i, k, :, self.mine].astype(F32) + self.in0[i, k].astype(F32)
            self.grad[i, k, :, self.mine] = both.astype(self.grad.dtype)
        for d in (1, 3, 2):
            src = self.grad.at[(i, slice(None)) + self.quarter(step4(p.x, d))]
            self.wait.append(self.push(src, self.in_x.at[d - 1, i], p.xdev(d)))

    def p2(self):
        p = self.place
        self.arrive()

        def add(i, carry):
            at = (lax.div(i, 4), lax.rem(i, 4))
            total = self.grad[at + self.piece].astype(F32)
            for k in range(3):
                total = total + self.in_x[(k,) + at].astype(F32)
            self.grad[at + self.piece] = total.astype(self.grad.dtype)
            return carry

        lax.fori_loop(0, 16, add, 0)
        for d in (1, 3, 2):
            src = self.grad.at[(step4(p.z, d), slice(None)) + self.piece]
            self.wait.append(self.push(src, self.in1.at[d - 1], p.zdev(d)))

    def p3(self):
        p = self.place
        self.arrive()
        for i in range(4):
            total = self.grad[(p.z, i) + self.piece].astype(F32)
            for k in range(3):
                total = total + self.in1[k, i].astype(F32)
            self.part[i] = total.astype(self.part.dtype)
        for d in (1, 3, 2):
            self.wait.append(self.push(self.part.at[step4(p.y, d)], self.in2.at[d - 1], p.ydev(d)))

    def p4(self):
        p = self.place
        self.arrive()
        total = self.part[p.y].astype(F32)
        for k in range(3):
            total = total + self.in2[k].astype(F32)
        self.out[self.piece] = total
        here = self.out.at[self.piece]
        self.wait = [self.push(here, here, p.xdev(d)) for d in (1, 3, 2)]

    def p5(self):
        self.arrive()
        here = self.out.at[:, self.mine]
        self.wait = [self.push(here, here, self.place.sibling())]

    def end(self):
        self.arrive()
        for copy in self.sends:
            copy.wait_send()


SCATTER_WIDE_SENDS = 4 + 12 + 3 + 3 + 3 + 1


def all_peers(p):
    rings = [p.ydev(d) for d in (1, 2, 3)] + [p.zdev(d) for d in (1, 2, 3)]
    return rings + [p.sibling()]


def x_peers(p):
    return [p.xdev(d) for d in (1, 2, 3)]


def owner(p, u, v):
    return v * p.v_step + u * p.u_step


def half_lanes(value, right):
    lane = lax.broadcasted_iota(jnp.int32, value.shape, 1)
    keep = lane >= HD if right else lane < HD
    return jnp.where(keep, value, jnp.zeros_like(value))


def rows_max(value):
    return jnp.max(value.reshape(-1, 8, value.shape[1]), axis=0)


def rows_sum(value):
    return jnp.sum(value.reshape(-1, 8, value.shape[1]), axis=0)


def dot_lanes(left, right):
    return lax.dot_general(left, right, (((1,), (1,)), ((), ())), preferred_element_type=F32)


def dot_plain(left, right):
    return jnp.dot(left, right, preferred_element_type=F32)


def fill_bias(key_place, query_place, bias):
    for i in range(GROUP // OWN):
        keys = jnp.broadcast_to(key_place[i : i + 1, :], (OWN, OWN)).T
        for k in range(4):
            cols = slice(k * OWN, k * OWN + OWN)
            ok = (keys <= query_place[0:1, cols]) & (keys >= query_place[1:2, cols])
            bias[i * OWN : i * OWN + OWN, cols] = jnp.where(ok, 0.0, HUGE_NEG).astype(BF)


def key_chunk(kv, i, head):
    a, b = lax.div(i, 2), lax.rem(i, 2) * CHUNK
    return kv[a, pl.ds(pl.multiple_of(b, CHUNK), CHUNK), head * 128 : head * 128 + 128]


def chunk_rows(i):
    return pl.ds(pl.multiple_of(i * CHUNK, CHUNK), CHUNK)


def turn_keys(kv, head, turned):
    def body(i, carry):
        turned[head, :, chunk_rows(i)] = key_chunk(kv, i, head).T
        return carry

    lax.fori_loop(0, STEPS, body, 0, unroll=True)


def query_tile(kv, p, head, tile):
    block = 384 + head // 2 * 128
    return half_lanes(kv[p.v, tile * TILE : tile * TILE + TILE, block : block + 128], head != 1)


def attend(kv, p, head, tile, bias, scores, turned, head_out, lse):
    cols = slice(tile * TILE, tile * TILE + TILE)
    query = query_tile(kv, p, head, tile)

    def score(i, top):
        part = dot_lanes(key_chunk(kv, i, head), query) + bias[chunk_rows(i), cols].astype(F32)
        scores[chunk_rows(i), :] = part
        return jnp.maximum(top, rows_max(part))

    top = lax.fori_loop(0, STEPS, score, jnp.full((8, TILE), -jnp.inf, F32), unroll=True)
    top = jnp.max(top, axis=0, keepdims=True)

    def mix(i, carry):
        total, acc = carry
        raised = jnp.exp(scores[chunk_rows(i), :] - top)
        acc = acc + dot_plain(turned[head, :, chunk_rows(i)], raised.astype(BF))
        return total + rows_sum(raised), acc

    total, acc = lax.fori_loop(
        0, STEPS, mix, (jnp.zeros((8, TILE), F32), jnp.zeros((128, TILE), F32)), unroll=True
    )
    total = jnp.sum(total, axis=0, keepdims=True)
    acc = acc / total
    at = 64 if head == 1 else 0
    head_out[head * 64 : head * 64 + 64, cols] = acc[at : at + 64, :]
    lse[head : head + 1, cols] = top + jnp.log(total)


def attend_back(kv, p, head, tile, bias, probs, grad_probs, turned, dob, lse, acc, part_send, dq):
    cols = slice(tile * TILE, tile * TILE + TILE)
    query = query_tile(kv, p, head, tile)
    block = head // 2 * 128
    dout = dob[2 * tile : 2 * tile + 2, :, block : block + 128]
    dout = half_lanes(dout.reshape(TILE, 128), head == 1)
    total = lse[head : head + 1, cols]

    def weigh(i, inner):
        keys = key_chunk(kv, i, head)
        prob = jnp.exp(dot_lanes(keys, query) + bias[chunk_rows(i), cols].astype(F32) - total)
        gprob = dot_lanes(keys, dout)
        probs[chunk_rows(i), :] = prob
        grad_probs[chunk_rows(i), :] = gprob
        return inner + rows_sum(prob * gprob)

    inner = lax.fori_loop(0, STEPS, weigh, jnp.zeros((8, TILE), F32), unroll=True)
    inner = jnp.sum(inner, axis=0, keepdims=True)

    def back(i, total_dq):
        prob = probs[chunk_rows(i), :]
        gscore = (prob * (grad_probs[chunk_rows(i), :] - inner)).astype(BF)
        both = dot_plain(gscore, query) + dot_plain(prob.astype(BF), dout)
        if tile == 0:
            acc[chunk_rows(i), :] = both
        else:
            total_kv = (acc[chunk_rows(i), :] + both).astype(BF)
            lanes = slice(head * 128, head * 128 + 128)
            part_send[lax.div(i, 2), pl.ds(lax.rem(i, 2) * 2, 2), 0:OWN, lanes] = total_kv.reshape(2, OWN, 128)
        return total_dq + dot_plain(turned[head, :, chunk_rows(i)], gscore)

    total_dq = lax.fori_loop(0, STEPS, back, jnp.zeros((128, TILE), F32), unroll=True)
    total_dq = total_dq * (HD ** (-0.5))
    at = 0 if head == 1 else 64
    row = (64, 0, 192)[head]
    dq[row : row + 64, cols] = total_dq[at : at + 64, :]


def col_sum(value):
    return jnp.sum(value, axis=0, keepdims=True)


def normalise(value):
    average = jnp.mean(value, -1, keepdims=True)
    centred = value - average
    spread = jnp.mean(centred * centred, -1, keepdims=True)
    inverse = lax.rsqrt(spread + EPS_NORM)
    return centred * inverse, inverse


def normalise_back(grad, unit, inverse, gain):
    g = grad * gain
    return inverse * (
        g - jnp.mean(g, -1, keepdims=True) - unit * jnp.mean(g * unit, -1, keepdims=True)
    )


GELU_A = 0.7978845608028654
GELU_B = 0.044715


def out_rows(full_rest, g):
    own = full_rest[g, :, :, 0:D].reshape(192, D)
    return jnp.concatenate([own, jnp.zeros((64, D), BF)], 0)


def ordered_sum(blocks):
    total = blocks[0].astype(F32)
    for k in range(1, blocks.shape[0]):
        total = total + blocks[k].astype(F32)
    return total


def natural_group(packed):
    col = [packed[:, j * HD : (j + 1) * HD] for j in range(10)]
    return [[col[j] for j in order] for order in ((7, 6, 9), (1, 2, 5), (0, 3, 4))]


def layer_kernel(
    x, cot, w_qkv, vec, lanes, rest, down, key_place, query_place,
    outputs, grad_input, o_rows, o_down, o_vec, *scratch,
):
    (
        full_rest, full_down, kv, bias, probs, grad_probs, turned, head_out, out_send, attended, lse,
        g_down, g_first, g_out, dob, acc, part_in, total_out, total_dc, low,
        x_all, w_all, normed, vec_y, vec_z, vecs, grad_vecs, vec_in, back, in_a, in1, part, in2, in0, held, in3, packed_sum,
    ) = scratch[:37]
    part_send, grad_send, dq = full_down, out_send, head_out
    blocks = scratch[37:-3]
    p = Place()
    w = Wire(*scratch[-3:])
    greet(all_peers(p) + x_peers(p))

    w_one = [(d, w.push(w_qkv.at[step4(p.u, d)], w_all.at[p.s], p.udev(d))) for d in (1, 3, 2)]
    vec_one = [w.push(vec, vec_y.at[p.y], p.ydev(d)) for d in (1, 3, 2)]
    w_all[p.s] = w_qkv[p.u]
    vec_y[p.y] = vec[...]
    w_two = [w.push(w_all.at[p.s], w_all.at[p.s], p.vdev(e)) for e in (1, 3, 2)]
    x_one = [w.push(x, x_all.at[p.u], p.udev(d)) for d in (1, 3, 2)]
    x_all[p.u] = x[...]
    for d, copy in w_one:
        copy.wait_recv()
        block = w_all.at[owner(p, step4(p.u, 4 - d), p.v)]
        w_two += [w.push(block, block, p.vdev(e)) for e in (1, 3, 2)]
    for copy in vec_one:
        copy.wait_recv()
    vec_z[p.z] = ordered_sum(vec_y).astype(BF)
    vec_two = [w.push(vec_z.at[p.z], vec_z.at[p.z], p.zdev(d)) for d in (1, 3, 2)]
    half = p.c * 1920
    parts = [
        Gather(w, p, rest, full_rest, region(0, None, half, 1024), True),
        Gather(w, p, rest, full_rest, region(0, None, half + 1024, 896), False),
        GatherWide(w, p, down, full_down, 48, pl.ds(pl.multiple_of(p.c * 384, 128), 384)),
    ]
    for part_ in parts:
        part_.first()
    fill_bias(key_place, query_place, bias)
    for copy in x_one + vec_two:
        copy.wait_recv()
    vecs[...] = ordered_sum(vec_z)
    low_vecs = vecs[...].astype(BF)

    def pick(row, dtype):
        column = lax.broadcasted_iota(jnp.int32, (D, 640), 0) - 192 * p.u
        return (column == lanes[row : row + 1, :]).astype(dtype)

    bias_own = dot_plain(low_vecs, pick(0, BF))[2:3, :] + dot_plain(low_vecs, pick(1, BF))[3:4, :]
    scale = jnp.where(lax.broadcasted_iota(jnp.int32, (1, 640), 1) < 384, 1.0, HD ** (-0.5)).astype(F32)
    for k in range(4):
        unit, _ = normalise(x_all[k].astype(F32))
        normed[k] = (unit * vecs[0:1, :] + vecs[1:2, :]).astype(BF)
    parts[2].second()
    for copy in w_two:
        copy.wait_recv()
    for k in range(4):
        projected = dot_plain(normed[k], w_all[...].reshape(D, 640)) + bias_own
        kv[p.v, k * OWN : k * OWN + OWN, :] = (projected.astype(BF).astype(F32) * scale).astype(BF)
    to_v = []
    for head in range(3):
        mine = kv.at[p.v, :, pl.ds(head * 128, 128)]
        to_v += [w.push(mine, mine, p.vdev(d)) for d in (1, 3)]
    for part_ in parts[:2]:
        part_.second()
    parts[2].third()
    head_out[192:256, :] = jnp.zeros((64, 512), F32)
    passed = []
    for head in range(3):
        lane = pl.ds(head * 128, 128)
        to_v[2 * head].wait_recv()
        low_half = kv.at[step4(p.v, 3), pl.ds(0, 256), lane]
        passed.append(w.push(low_half, low_half, p.vdev(1)))
        to_v[2 * head + 1].wait_recv()
        high_half = kv.at[step4(p.v, 1), pl.ds(256, 256), lane]
        passed.append(w.push(high_half, high_half, p.vdev(3)))
    for head in range(3):
        for copy in passed[2 * head : 2 * head + 2]:
            copy.wait_recv()
        turn_keys(kv, head, turned)
        for tile in range(2):
            attend(kv, p, head, tile, bias, probs, turned, head_out, lse)
        if head == 0:
            for part_ in parts[:2]:
                part_.third()
            parts[2].fourth()
    for k in range(4):
        out_send[k] = head_out[:, k * OWN : k * OWN + OWN].T.astype(BF)
    attended[p.u] = out_send[p.u]
    out_back = [w.push(out_send.at[step4(p.u, d)], attended.at[p.u], p.udev(d)) for d in (1, 3, 2)]
    for part_ in parts[:2]:
        part_.fourth()
    parts[2].fifth((0, 1, 3, 2))
    for copy in out_back:
        copy.wait_recv()
    for part_ in parts[:2]:
        part_.arrive()
    early = to_v + passed + out_back + x_one + w_two + vec_one + vec_two + [c for _, c in w_one]

    grad_y = cot[...].astype(F32)
    middle = x[...].astype(F32) + vecs[4:5, :]
    for g in range(4):
        middle = middle + dot_plain(attended[g], out_rows(full_rest, g))
    unit, inverse = normalise(middle)
    low[0] = (unit * vecs[5:6, :] + vecs[6:7, :]).astype(BF)
    total_out[...] = middle + vecs[7:8, :]
    total_dc[...] = jnp.zeros((OWN, D), F32)
    low_turned = low[0].T

    parts[2].arrive()

    def first_part(i):
        at = i * D + p.c * 384
        to = i * D + (1 - p.c) * 384
        return Scatter(
            w, p, g_first, o_rows, region(0, None, at, 384), region(0, None, to, 384),
            region(0, None, at + 4 * D, 384), i % 2 == 0, blocks[5 * i : 5 * i + 5],
        )

    firsts = [first_part(i) for i in range(4)]
    at, to = p.c * 384, (1 - p.c) * 384
    downs = [
        ScatterWide(
            w, p, g_down, o_down, 48, pl.ds(pl.multiple_of(at, 128), 384),
            pl.ds(pl.multiple_of(to, 128), 384), blocks[20:25],
        )
    ]
    outs = [
        Scatter(
            w, p, g_out, o_rows, region(0, None, at, 384), region(0, None, to, 384),
            region(0, None, at + 3 * D, 384), False, blocks[25:30],
        )
    ]
    for i in range(4):
        w_first = full_rest[:, :, :, D + i * D : 2 * D + i * D].reshape(D, D)
        w_down = full_down[i].reshape(D, D)
        act = dot_plain(low[0], w_first) + vecs[8 + i : 9 + i, :]
        square = act * act
        bent = jnp.tanh(GELU_A * (act + GELU_B * act * square))
        hidden = (0.5 * act * (1.0 + bent)).astype(BF)
        slope = 0.5 * (1.0 + bent) + 0.5 * act * (1.0 - bent * bent) * (
            GELU_A * (1.0 + 3.0 * GELU_B * square)
        )
        hidden_turned = hidden.T
        for k in range(2):
            rows = slice(k * 384, k * 384 + 384)
            g_down[i, 2 * k : 2 * k + 2] = (
                dot_plain(hidden_turned[rows], cot[...]).astype(BF).reshape(2, 192, D)
            )
        for part_ in downs:
            part_.p0_slab(i)
        grad_act = (dot_lanes(cot[...], w_down) * slope).astype(BF)
        grad_vecs[8 + i : 9 + i, :] = col_sum(grad_act.astype(F32))
        for k in range(2):
            rows = slice(k * 384, k * 384 + 384)
            g_first[2 * k : 2 * k + 2, :, :, i * D : i * D + D] = (
                dot_plain(low_turned[rows], grad_act).astype(BF).reshape(2, 4, 48, D)
            )
        firsts[i].p0()
        total_dc[...] += dot_lanes(grad_act, w_first)
        total_out[...] += dot_plain(hidden, w_down)
        if i > 0:
            downs[0].p1_slab(i - 1)
    outputs[...] = total_out[...].astype(BF)

    for part_ in parts:
        part_.end()
    for copy in early:
        copy.wait_send()

    grad_c = total_dc[...]
    grad_m = grad_y + normalise_back(grad_c, unit, inverse, vecs[5:6, :])
    total_out[...] = grad_m
    low[1] = grad_m.astype(BF)
    for g in range(4):
        grad_send[g] = dot_lanes(low[1], out_rows(full_rest, g)).astype(BF)
    dob[p.u] = grad_send[p.u]
    to_u = [w.push(grad_send.at[step4(p.u, d)], dob.at[p.u], p.udev(d)) for d in (1, 3, 2)]
    for g in range(4):
        g_out[g] = dot_plain(attended[g].T, low[1])[0:192, :].astype(BF).reshape(4, 48, D)
    outs[0].p0()
    grad_vecs[0:4, :] = jnp.zeros((4, D), F32)
    grad_vecs[4:5, :] = col_sum(low[1].astype(F32))
    grad_vecs[5:6, :] = col_sum(grad_c * unit)
    grad_vecs[6:7, :] = col_sum(grad_c)
    grad_vecs[7:8, :] = col_sum(grad_y)
    grad_vecs[12:16, :] = jnp.zeros((4, D), F32)
    for part_ in firsts[:2]:
        part_.p1()
    downs[0].p1_slab(3)
    for copy in to_u:
        copy.wait_recv()

    stages = [
        lambda: [part_.p1() for part_ in firsts[2:3]],
        lambda: [part_.p1() for part_ in firsts[3:]],
        lambda: [part_.p1() for part_ in outs],
        lambda: None,
        lambda: [part_.p2() for part_ in firsts[:2]],
        lambda: None,
    ]
    to_v_back = []
    for head in range(3):
        for tile in range(2):
            attend_back(
                kv, p, head, tile, bias, probs, grad_probs, turned, dob, lse, acc, part_send, dq
            )
            if tile == 1:
                to_v_back.append(
                    [
                        w.push(
                            part_send.at[step4(p.v, d), :, pl.ds(0, OWN), pl.ds(head * 128, 128)],
                            part_in.at[head, d - 1],
                            p.vdev(d),
                        )
                        for d in (1, 3, 2)
                    ]
                )
            stages[head * 2 + tile]()
    dq[128:192, :] = jnp.zeros((64, 512), F32)
    for k in range(4):
        back[k, :, 384:640] = dq[:, k * OWN : k * OWN + OWN].T.astype(BF)

    def rows_of(u, v, col, cols):
        return full_rest.at[v + p.c * (u - v), u + p.c * (v - u), :, pl.ds(col, cols)]

    def send_columns(col, cols):
        grad_part = back[:, :, col : col + cols].reshape(512, cols)
        for k in range(2):
            turned_rows = normed[:, :, k * 384 : k * 384 + 384].reshape(512, 384).T
            g_part = dot_plain(turned_rows, grad_part).astype(BF)
            full_rest[2 * k : 2 * k + 2, :, :, col : col + cols] = g_part.reshape(2, 4, 48, cols)
        sent = []
        for d in (1, 3, 2):
            for k in range(4):
                src = rows_of(k, step4(p.v, d), col, cols)
                sent.append(w.push(src, in1.at[d - 1, k, :, pl.ds(col, cols)], p.vdev(d)))
        return sent

    one = send_columns(384, 256)
    for part_ in firsts[2:]:
        part_.p2()
    for head in range(3):
        for copy in to_v_back[head]:
            copy.wait_recv()
        columns = slice(head * 128, head * 128 + 128)
        for k in range(4):
            total = part_send[p.v, k, 0:OWN, columns].astype(F32)
            for d in range(3):
                total = total + part_in[head, d, k].astype(F32)
            back[k, :, columns] = total.astype(BF)
    one += send_columns(0, 384)
    for part_ in downs:
        part_.p2()
    grad_qkv = back[...].reshape(512, 640)
    grad_gain = jnp.zeros((1, D), F32)
    grad_shift = jnp.zeros((1, D), F32)
    for k in range(4):
        grad_a = dot_lanes(back[k], w_all[...].reshape(D, 640))
        unit_k, _ = normalise(x_all[k].astype(F32))
        grad_gain = grad_gain + col_sum(grad_a * unit_k)
        grad_shift = grad_shift + col_sum(grad_a)
        normed[k] = grad_a.astype(BF)
    a_one = [w.push(normed.at[step4(p.u, d)], in_a.at[d - 1], p.udev(d)) for d in (1, 3, 2)]
    sums = jnp.broadcast_to(col_sum(grad_qkv.astype(F32)), (8, 640))
    spread = (((1,), (1,)), ((), ()))
    exact = lax.Precision.HIGHEST
    bias_q = lax.dot_general(sums, pick(0, F32), spread, precision=exact, preferred_element_type=F32)
    bias_v = lax.dot_general(sums, pick(1, F32), spread, precision=exact, preferred_element_type=F32)
    grad_vecs[0:1, :] = grad_gain
    grad_vecs[1:2, :] = grad_shift
    grad_vecs[2:3, :] = bias_q[0:1, :]
    grad_vecs[3:4, :] = bias_v[0:1, :]
    vec_in[0, p.z] = grad_vecs[...]
    vec_sends = [[w.push(grad_vecs, vec_in.at[0, p.z], p.zdev(d)) for d in (1, 3, 2)]]
    for part_ in firsts[:2]:
        part_.p3()
    for part_ in outs:
        part_.p2()
    for copy in one:
        copy.wait_recv()
    for k in range(4):
        total = rows_of(k, p.v, 0, 640)[...].astype(F32)
        for d in range(3):
            total = total + in1[d, k].astype(F32)
        part[k] = total.astype(BF)
    two = [w.push(part.at[step4(p.u, d)], in2.at[p.u], p.udev(d)) for d in (1, 3, 2)]
    in2[p.u] = part[p.u]
    for copy in vec_sends[0]:
        copy.wait_recv()
    vec_in[1, p.y] = ordered_sum(vec_in.at[0])
    vec_sends.append([w.push(vec_in.at[1, p.y], vec_in.at[1, p.y], p.ydev(d)) for d in (1, 3, 2)])
    for part_ in firsts[2:]:
        part_.p3()
    for copy in two:
        copy.wait_recv()
    three = [w.push(in2.at[pl.ds((1 - p.c) * 2, 2)], in0, p.sibling())]
    for part_ in downs + outs:
        part_.p3()
    for copy in vec_sends[1]:
        copy.wait_recv()
    vec_in[2, p.x] = ordered_sum(vec_in.at[1])
    vec_sends.append([w.push(vec_in.at[2, p.x], vec_in.at[2, p.x], p.xdev(d)) for d in (1, 3, 2)])
    three[0].wait_recv()
    for k in range(2):
        held[k] = (in2[p.c * 2 + k].astype(F32) + in0[k].astype(F32)).astype(BF)
    in3[p.x] = held[...]
    four = [w.push(held, in3.at[p.x], p.xdev(d)) for d in (1, 3, 2)]
    for part_ in firsts[:2]:
        part_.p4()
    for copy in a_one:
        copy.wait_recv()
    grad_a = normed[p.u].astype(F32)
    for d in range(3):
        grad_a = grad_a + in_a[d].astype(F32)
    unit, inverse = normalise(x[...].astype(F32))
    grad_input[...] = (total_out[...] + normalise_back(grad_a, unit, inverse, vecs[0:1, :])).astype(BF)
    for part_ in downs:
        part_.p4()
    for copy in vec_sends[2]:
        copy.wait_recv()
    vec_in[3, 0] = ordered_sum(vec_in.at[2])
    vec_sends.append([w.push(vec_in.at[3, 0], vec_in.at[3, 1], p.sibling())])
    for copy in four:
        copy.wait_recv()
    for k in range(2):
        total = in3[0, k].astype(F32)
        for d in range(1, 4):
            total = total + in3[d, k].astype(F32)
        packed_sum[p.c * 2 + k] = total
    here = packed_sum.at[pl.ds(p.c * 2, 2)]
    five = [w.push(here, here, p.sibling())]
    for part_ in firsts[2:] + outs:
        part_.p4()
    vec_sends[3][0].wait_recv()
    o_vec[...] = vec_in[3, 0] + vec_in[3, 1]
    for part_ in downs:
        part_.p5()
    five[0].wait_recv()
    groups = [natural_group(packed_sum[g]) for g in range(4)]
    for k in range(3):
        o_rows[:, k * D : k * D + D] = jnp.concatenate(sum([groups[g][k] for g in range(4)], []), 1)
    for part_ in firsts + downs + outs:
        part_.end()
    rest_sends = one + a_one + two + three + four + five + sum(vec_sends, [])
    for copy in to_u + sum(to_v_back, []) + rest_sends:
        copy.wait_send()


def layer(x, cot, w_qkv, vec, lanes, rest, down, key_place, query_place):
    shapes = [
        pltpu.VMEM((4, 4, 48, 5 * D), BF),
        pltpu.VMEM((4, 4, 192, D), BF),
        pltpu.VMEM((4, 512, 640), BF),
        pltpu.VMEM((GROUP, 512), BF),
        pltpu.VMEM((GROUP, TILE), F32),
        pltpu.VMEM((GROUP, TILE), F32),
        pltpu.VMEM((3, 128, GROUP), BF),
        pltpu.VMEM((256, 512), F32),
        pltpu.VMEM((4, OWN, 256), BF),
        pltpu.VMEM((4, OWN, 256), BF),
        pltpu.VMEM((8, 512), F32),
        pltpu.VMEM((4, 4, 192, D), BF),
        pltpu.VMEM((4, 4, 48, FF), BF),
        pltpu.VMEM((4, 4, 48, D), BF),
        pltpu.VMEM((4, OWN, 256), BF),
        pltpu.VMEM((GROUP, 128), F32),
        pltpu.VMEM((3, 3, 4, OWN, 128), BF),
        pltpu.VMEM((OWN, D), F32),
        pltpu.VMEM((OWN, D), F32),
        pltpu.VMEM((2, OWN, D), BF),
        pltpu.VMEM((4, OWN, D), BF),
        pltpu.VMEM((16, 48, 640), BF),
        pltpu.VMEM((4, OWN, D), BF),
        pltpu.VMEM((4, 16, D), BF),
        pltpu.VMEM((4, 16, D), BF),
        pltpu.VMEM((16, D), F32),
        pltpu.VMEM((16, D), F32),
        pltpu.VMEM((4, 4, 16, D), F32),
        pltpu.VMEM((4, OWN, 640), BF),
        pltpu.VMEM((3, OWN, D), BF),
        pltpu.VMEM((3, 4, 48, 640), BF),
        pltpu.VMEM((4, 48, 640), BF),
        pltpu.VMEM((4, 48, 640), BF),
        pltpu.VMEM((2, 48, 640), BF),
        pltpu.VMEM((2, 48, 640), BF),
        pltpu.VMEM((4, 2, 48, 640), BF),
        pltpu.VMEM((4, 48, 640), F32),
    ]
    for _ in range(4):
        shapes += scatter_shapes(48, 384, BF)
    shapes += scatter_wide_shapes(48, 384, BF) + scatter_shapes(48, 384, BF)
    return pl.pallas_call(
        layer_kernel,
        out_shape=(
            jax.ShapeDtypeStruct((OWN, D), BF),
            jax.ShapeDtypeStruct((OWN, D), BF),
            jax.ShapeDtypeStruct((48, 8 * D), F32),
            jax.ShapeDtypeStruct((192, D), F32),
            jax.ShapeDtypeStruct((16, D), F32),
        ),
        in_specs=[VMEM] * 9,
        out_specs=(VMEM,) * 5,
        scratch_shapes=shapes + sems(2 * GATHER_SENDS + GATHER_WIDE_SENDS + 5 * SCATTER_SENDS + SCATTER_WIDE_SENDS + 100, 5),
        compiler_params=pltpu.CompilerParams(
            collective_id=1, has_side_effects=True, vmem_limit_bytes=62 * MIB
        ),
        name="layer",
    )(x, cot, w_qkv, vec, lanes, rest, down, key_place, query_place)


def adamw(weight, moment, second, grad, rate, decay):
    moment_new = BETA_ONE * moment + (1.0 - BETA_ONE) * grad
    second_new = BETA_TWO * second + (1.0 - BETA_TWO) * grad * grad
    moment_hat = moment_new / (1.0 - BETA_ONE**STEP)
    second_hat = second_new / (1.0 - BETA_TWO**STEP)
    weight_new = weight - rate * (moment_hat / (jnp.sqrt(second_hat) + EPS_ADAM) + decay * weight)
    return (weight_new, moment_new, second_new)


def pack_groups(queries, keys, values):
    blank = jnp.zeros((queries.shape[0], HD), queries.dtype)
    groups = []
    for g in range(4):
        q, k, v = ([a[:, (3 * g + j) * HD : (3 * g + j + 1) * HD] for j in range(3)] for a in (queries, keys, values))
        groups.append(jnp.concatenate([v[0], k[0], k[1], v[1], v[2], k[2], q[1], q[0], blank, q[2]], 1))
    return jnp.stack(groups)


def per_device(
    tokens,
    cotangent,
    lengths,
    positions,
    w_rows,
    w_down,
    vectors,
    moment_rows,
    second_rows,
    moment_down,
    second_down,
    moment_vectors,
    second_vectors,
):
    shard_index = lax.axis_index("shard")
    core = lax.rem(lax.axis_index("replica"), 2)
    z, y = lax.div(shard_index, 4), lax.rem(shard_index, 4)
    own_v = jnp.where(core == 0, z, y)
    low_qkv = pack_groups(*(w_rows[:, k * D : k * D + D].astype(BF) for k in range(3)))
    own_vecs = lax.dynamic_update_slice(
        jnp.zeros((16, D), BF), vectors.astype(BF), (0, shard_index * 48)
    )
    place_blocks = positions.reshape(4, 4, OWN)
    place_all = jnp.where(core == 0, place_blocks, place_blocks.transpose(1, 0, 2)).reshape(GROUP)
    seq_ends = jnp.cumsum(lengths[0])
    place_quarter = lax.dynamic_slice_in_dim(place_all, own_v * 512, 512)
    seq_start = jnp.max(
        jnp.where(place_quarter[None, :] >= seq_ends[:, None], seq_ends[:, None], 0), axis=0
    )
    key_place = place_all.astype(F32).reshape(GROUP // OWN, OWN)
    query_place = jnp.pad(jnp.stack([place_quarter, seq_start]).astype(F32), ((0, 6), (0, 0)))

    column = jnp.arange(640)
    block, within = column // HD, column % HD
    lanes = jnp.full((8, 640), -GROUP, jnp.int32)
    for row, places in ((0, ((7, 0), (6, 1), (9, 2))), (1, ((0, 0), (3, 1), (4, 2)))):
        for at, head in places:
            lanes = lanes.at[row].set(jnp.where(block == at, within + head * HD, lanes[row]))
    outputs, grad_input, grad_rows, grad_down, grad_vecs = layer(
        tokens, cotangent, low_qkv, own_vecs, lanes, w_rows[:, 3 * D :].astype(BF), w_down.astype(BF), key_place, query_place
    )
    own_grads = lax.dynamic_slice(grad_vecs, (0, shard_index * 48), (12, 48))
    rows_new = adamw(w_rows, moment_rows, second_rows, grad_rows, LR_MATRIX, DECAY)
    down_new = adamw(w_down, moment_down, second_down, grad_down, LR_MATRIX, DECAY)
    vec_new = adamw(vectors, moment_vectors, second_vectors, own_grads, LR_VECTOR, 0.0)
    return (
        outputs,
        grad_input,
        rows_new[0],
        rows_new[1],
        rows_new[2],
        down_new[0],
        down_new[1],
        down_new[2],
        vec_new[0],
        vec_new[1],
        vec_new[2],
    )


def solution(mesh):
    return jax.shard_map(
        per_device,
        mesh=mesh,
        in_specs=(
            P(("replica", "shard"), None),
            P(("replica", "shard"), None),
            P("replica", None),
            P("replica", None),
            P("shard", None),
            P("shard", None),
            P(None, "shard"),
            P("shard", None),
            P("shard", None),
            P("shard", None),
            P("shard", None),
            P(None, "shard"),
            P(None, "shard"),
        ),
        out_specs=(
            P(("replica", "shard"), None),
            P(("replica", "shard"), None),
            P("shard", None),
            P("shard", None),
            P("shard", None),
            P("shard", None),
            P("shard", None),
            P("shard", None),
            P(None, "shard"),
            P(None, "shard"),
            P(None, "shard"),
        ),
        check_vma=False,
    )
```
